32 devices in a mesh: seq: 8 (over z, x), rows: 4 (over y, core).
Axes of the slice: x: 2, y: 2, z: 4, core: 2. Of those that a mesh axis runs over, the one named last changes fastest.
Arguments:
- tokens: bfloat16 [4, 1024, 768], P('rows', 'seq'), may hold values from -6 to 6
- lengths: int32 [4, 8], P('rows'), may hold values from 1 to 968, as said below
- cotangent: bfloat16 [4, 1024, 768], P('rows', 'seq'), may hold values from -6 to 6
- w_query: bfloat16 [2, 768, 768], replicated, may hold values from -0.21875 to 0.21875
- b_query: bfloat16 [2, 768], replicated, may hold values from -3 to 3
- w_key: bfloat16 [2, 768, 768], replicated, may hold values from -0.21875 to 0.21875
- b_key: bfloat16 [2, 768], replicated, may hold values from -3 to 3
- w_value: bfloat16 [2, 768, 768], replicated, may hold values from -0.21875 to 0.21875
- b_value: bfloat16 [2, 768], replicated, may hold values from -0.059814453 to 0.059814453
- w_out: bfloat16 [2, 768, 768], replicated, may hold values from -1 to 1
- b_out: bfloat16 [2, 768], replicated, may hold values from -2 to 2
- norm1_gain: bfloat16 [2, 768], replicated, may hold values from 0.5 to 1.5
- norm1_bias: bfloat16 [2, 768], replicated, may hold values from -2 to 2
- w_inner: bfloat16 [2, 768, 3072], replicated, may hold values from -0.21875 to 0.21875
- b_inner: bfloat16 [2, 3072], replicated, may hold values from -3 to 3
- w_outer: bfloat16 [2, 3072, 768], replicated, may hold values from -0.109375 to 0.109375
- b_outer: bfloat16 [2, 768], replicated, may hold values from -2 to 2
- norm2_gain: bfloat16 [2, 768], replicated, may hold values from 0.5 to 1.5
- norm2_bias: bfloat16 [2, 768], replicated, may hold values from -2 to 2
Outputs:
- output: bfloat16 [4, 1024, 768], P('rows', 'seq')
- tokens_grad: bfloat16 [4, 1024, 768], P('rows', 'seq')
- w_query_grad: float32 [2, 768, 768], P(None, 'seq', 'rows')
- b_query_grad: float32 [2, 768], P(None, 'seq')
- w_key_grad: float32 [2, 768, 768], P(None, 'seq', 'rows')
- b_key_grad: float32 [2, 768], P(None, 'seq')
- w_value_grad: float32 [2, 768, 768], P(None, 'seq', 'rows')
- b_value_grad: float32 [2, 768], P(None, 'seq')
- w_out_grad: float32 [2, 768, 768], P(None, 'seq', 'rows')
- b_out_grad: float32 [2, 768], P(None, 'seq')
- norm1_gain_grad: float32 [2, 768], P(None, 'seq')
- norm1_bias_grad: float32 [2, 768], P(None, 'seq')
- w_inner_grad: float32 [2, 768, 3072], P(None, 'seq', 'rows')
- b_inner_grad: float32 [2, 3072], P(None, 'seq')
- w_outer_grad: float32 [2, 3072, 768], P(None, 'seq', 'rows')
- b_outer_grad: float32 [2, 768], P(None, 'seq')
- norm2_gain_grad: float32 [2, 768], P(None, 'seq')
- norm2_bias_grad: float32 [2, 768], P(None, 'seq')
The draws below stay inside these ranges and needn't reach their ends.
Inputs may be any that keep to these rules, and one draw needn't show every extreme that they name: In every row the 8 lengths are positive and add up to 1024; one document of each row, never the first or the last, has exactly the largest length, and some document has length 1.
All inputs are finite; a program needn't handle non-finite values.
Results may differ from the reference program's by a relative error of at most 0.035.
Values may be sent and summed in bfloat16 or wider, within the bound.
No kernel may reach another device: no remote copies, remote signals or barrier semaphores. Data moves between devices by JAX's collectives and lax.ppermute only.
A program may use at most 448 MiB of HBM per device.

```python
import jax
import jax.numpy as jnp
from jax import lax

D = 768
HEADS = 12
HEAD_DIM = 64
FF = 3072
TOK_DEV = 128
LAYERS = 2
DOCS = 8
SEQ_LEN = 1024
ROWS = 4


def draw_lengths(key, part):
    key = jax.random.fold_in(key, 11)
    unit_size = TOK_DEV // 16
    others_total = (DOCS - 1) * unit_size

    def one_row(row_key):
        pick_key, size_key, unit_key = jax.random.split(row_key, 3)
        spanning = jax.random.randint(pick_key, (), 1, DOCS - 1)
        places = jnp.arange(DOCS)
        single_place = (spanning + 1) % DOCS
        balance_place = (spanning + 2 + jax.random.randint(unit_key, (), 0, DOCS - 2)) % DOCS
        pieces = jax.random.randint(size_key, (DOCS,), 1, unit_size + 1)
        pieces = jnp.where(places == single_place, 1, pieces)
        pieces = jnp.where((places == spanning) | (places == balance_place), 0, pieces)
        balance = others_total - jnp.sum(pieces)
        pieces = jnp.where(places == balance_place, balance, pieces)
        return jnp.where(places == spanning, SEQ_LEN - others_total, pieces).astype(jnp.int32)
    return jax.vmap(one_row)(jax.random.split(key, ROWS))


def levels(key, extent, cuts, low, top_value):
    loudness, own = 1.0, jax.random.fold_in(key, 6)
    for axis_at, parts in cuts:
        steps = jnp.exp(jax.random.uniform(jax.random.fold_in(own, axis_at), (parts,), jnp.float32, low / len(cuts), top_value / len(cuts)))
        loudness = loudness * jnp.repeat(steps, extent[axis_at] // parts).reshape([-1 if axis == axis_at else 1 for axis in range(len(extent))])
    return loudness


def noise(stream_key, extent, scale, limit, cuts=(), held_as=jnp.bfloat16):
    loudness = levels(stream_key, extent, cuts, -0.22, 0.18) if cuts else 1.0
    drawn = jax.random.normal(stream_key, extent, jnp.float32) * scale * loudness
    return jnp.minimum(jnp.maximum(drawn, -limit), limit).astype(held_as)


def setup_inputs(seed: int = 0) -> dict:
    streams_of = jax.random.split(jax.random.key(seed), 20)
    tokens = noise(streams_of[0], (ROWS, SEQ_LEN, D), 1.0, 6.0, ((0, 4), (1, 8)))
    lengths = draw_lengths(jax.random.fold_in(streams_of[19], 71), 0)
    cotangent = noise(streams_of[2], (ROWS, SEQ_LEN, D), 1.0, 6.0, ((0, 4), (1, 8)))
    w_query = noise(streams_of[3], (LAYERS, D, D), D ** -0.5, 0.21875)
    b_query = noise(streams_of[4], (LAYERS, D), 0.5, 3.0)
    w_key = noise(streams_of[5], (LAYERS, D, D), D ** -0.5, 0.21875)
    b_key = noise(streams_of[6], (LAYERS, D), 0.5, 3.0)
    w_value = noise(streams_of[7], (LAYERS, D, D), D ** -0.5, 0.21875)
    b_value = noise(streams_of[8], (LAYERS, D), 0.01, 0.059814453)
    w_out = jnp.clip(jax.random.uniform(streams_of[9], (LAYERS, D, D), jnp.float32, -1.0, 1.0), -1.0, 1.0).astype(jnp.bfloat16)
    b_out = noise(streams_of[10], (LAYERS, D), 0.3, 2.0)
    norm1_gain = jnp.clip(1.0 + 0.1 * jax.random.normal(streams_of[11], (LAYERS, D), jnp.float32), 0.5, 1.5).astype(jnp.bfloat16)
    norm1_bias = noise(streams_of[12], (LAYERS, D), 0.3, 2.0)
    w_inner = noise(streams_of[13], (LAYERS, D, FF), D ** -0.5, 0.21875)
    b_inner = noise(streams_of[14], (LAYERS, FF), 0.5, 3.0)
    w_outer = noise(streams_of[15], (LAYERS, FF, D), FF ** -0.5, 0.109375)
    b_outer = noise(streams_of[16], (LAYERS, D), 0.3, 2.0)
    norm2_gain = jnp.clip(1.0 + 0.1 * jax.random.normal(streams_of[17], (LAYERS, D), jnp.float32), 0.5, 1.5).astype(jnp.bfloat16)
    norm2_bias = noise(streams_of[18], (LAYERS, D), 0.3, 2.0)
    return {"tokens": tokens, "lengths": lengths, "cotangent": cotangent, "w_query": w_query, "b_query": b_query, "w_key": w_key, "b_key": b_key, "w_value": w_value, "b_value": b_value, "w_out": w_out, "b_out": b_out, "norm1_gain": norm1_gain, "norm1_bias": norm1_bias, "w_inner": w_inner, "b_inner": b_inner, "w_outer": w_outer, "b_outer": b_outer, "norm2_gain": norm2_gain, "norm2_bias": norm2_bias}


NEG_FILL = -1e+30
NORM_EPS = 1e-12
PRECISE = lax.Precision.HIGHEST

@jax.custom_vjp
def low(v):
    return lax.optimization_barrier(v.astype(jnp.bfloat16)).astype(jnp.float32)

@jax.custom_vjp
def low_back(v):
    return v

def low_keep(v):
    return (low(v), None)

def low_pass(kept, grad):
    return (grad,)

def back_keep(v):
    return (v, None)

def back_low(kept, grad):
    return (low(grad),)
low.defvjp(low_keep, low_pass)
low_back.defvjp(back_keep, back_low)

def doc_layout(lengths_row, index):
    ends = jnp.cumsum(lengths_row, dtype=jnp.int32)
    passed = (index[:, None] >= ends[None, :]).astype(jnp.int32)
    segment = lax.optimization_barrier(jnp.sum(passed, axis=1, dtype=jnp.int32))
    begin = lax.optimization_barrier(jnp.sum(passed * lengths_row[None, :], axis=1, dtype=jnp.int32))
    return (segment, (index - begin).astype(jnp.int32))

def rotary_tables(position):
    pairs = jnp.arange(HEAD_DIM // 2, dtype=jnp.int32).astype(jnp.float32)
    inverse = jnp.power(jnp.float32(10000.0), -2.0 * pairs / HEAD_DIM)
    angle = position.astype(jnp.float32)[:, None] * inverse[None, :]
    cosine = jnp.tile(jnp.repeat(jnp.cos(angle), 2, axis=1), (1, HEADS))
    sine = jnp.tile(jnp.repeat(jnp.sin(angle), 2, axis=1), (1, HEADS))
    return (cosine, sine)

def rotate_pairs(values):
    shaped = values.reshape(values.shape[:-1] + (values.shape[-1] // 2, 2))
    return jnp.stack([-shaped[..., 1], shaped[..., 0]], axis=-1).reshape(values.shape)

def apply_rotary(values, cosine, sine):
    return values * cosine + rotate_pairs(values) * sine

def norm_forward(values, gain, bias):
    centered = values - lax.optimization_barrier(jnp.mean(values, axis=-1, keepdims=True))
    rstd = lax.rsqrt(lax.optimization_barrier(jnp.mean(centered * centered, axis=-1, keepdims=True)) + NORM_EPS)
    normed = centered * rstd
    return (normed * gain + bias, normed, rstd)

def linear(inputs, weight, bias):
    return jnp.dot(inputs, weight, precision=PRECISE, preferred_element_type=jnp.float32) + bias

def attention_rows(query, key, value, segment):
    blocks = SEQ_LEN // TOK_DEV
    query_blocks = query.reshape(blocks, TOK_DEV, HEADS, HEAD_DIM)
    segment_blocks = segment.reshape(blocks, TOK_DEV)
    key_heads = key.reshape(SEQ_LEN, HEADS, HEAD_DIM)
    value_heads = value.reshape(SEQ_LEN, HEADS, HEAD_DIM)

    def one_block(item):
        query_block, segment_block = item
        raw = jnp.einsum('qhd,khd->hqk', query_block, key_heads, precision=PRECISE)
        scores = low_back(raw) * HEAD_DIM ** (-0.5)
        same = (segment_block[:, None] == segment[None, :])[None]
        masked = jnp.where(same, scores, NEG_FILL)
        top = lax.optimization_barrier(jnp.max(masked, axis=2, keepdims=True))
        log_total = top + jnp.log(lax.optimization_barrier(jnp.sum(jnp.exp(masked - top), axis=2, keepdims=True)))
        prob = low(jnp.exp(masked - log_total))
        return jnp.einsum('hqk,khd->qhd', prob, value_heads, precision=PRECISE)
    return lax.map(jax.checkpoint(one_block), (query_blocks, segment_blocks)).reshape(SEQ_LEN, D)

def layer_forward(current, weights, segment, cosine, sine):
    w_query, b_query, w_key, b_key, w_value, b_value, w_out, b_out, gain_one, bias_one, w_inner, b_inner, w_outer, b_outer, gain_two, bias_two = weights
    inputs = low(current)
    query = low(apply_rotary(low_back(linear(inputs, w_query, b_query)), cosine, sine))
    key = low(apply_rotary(low_back(linear(inputs, w_key, b_key)), cosine, sine))
    value = low(low_back(linear(inputs, w_value, b_value)))
    attn = low(low_back(attention_rows(query, key, value, segment)))
    branch = low_back(linear(attn, w_out, b_out))
    hidden = norm_forward(current + branch, gain_one, bias_one)[0]
    inner = low_back(linear(low(hidden), w_inner, b_inner))
    active = low(jax.nn.gelu(inner, approximate=False))
    outer = low_back(linear(active, w_outer, b_outer))
    return norm_forward(hidden + outer, gain_two, bias_two)[0]

def reference(tokens, lengths, cotangent, w_query, b_query, w_key, b_key, w_value, b_value, w_out, b_out, norm1_gain, norm1_bias, w_inner, b_inner, w_outer, b_outer, norm2_gain, norm2_bias):
    params = tuple((param.astype(jnp.float32) for param in (w_query, b_query, w_key, b_key, w_value, b_value, w_out, b_out, norm1_gain, norm1_bias, w_inner, b_inner, w_outer, b_outer, norm2_gain, norm2_bias)))

    def row_step(totals, row):
        tokens_row, lengths_row, cotangent_row = row
        index = jnp.arange(SEQ_LEN, dtype=jnp.int32)
        segment, position = doc_layout(lengths_row, index)
        cosine, sine = rotary_tables(position)

        def forward(inputs, weights):
            current = inputs
            for layer in range(LAYERS):
                current = layer_forward(current, tuple((param[layer] for param in weights)), segment, cosine, sine)
            return current
        result, pullback = jax.vjp(forward, tokens_row.astype(jnp.float32), params)
        input_grad, weight_grads = pullback(cotangent_row.astype(jnp.float32))
        totals = jax.tree.map(lambda first, second: first + second, totals, weight_grads)
        return (totals, (result.astype(jnp.bfloat16), input_grad.astype(jnp.bfloat16)))
    zeros = tuple((jnp.zeros_like(param) for param in params))
    totals, (outputs, grads) = lax.scan(row_step, zeros, (tokens, lengths, cotangent))
    return (outputs, grads, totals[0], totals[1], totals[2], totals[3], totals[4], totals[5], totals[6], totals[7], totals[8], totals[9], totals[10], totals[11], totals[12], totals[13], totals[14], totals[15])
```

```python
import functools

import jax
import jax.numpy as jnp
from jax import lax
from jax.experimental import pallas as pl
from jax.experimental.pallas import tpu as pltpu
from jax.sharding import PartitionSpec as P

D = 768
HEADS = 12
HEAD_DIM = 64
FF = 3072
LAYERS = 2
LANES = 128
PAIRS = D // LANES
CHUNK = D // 4
NEG_FILL = -1e30
NORM_EPS = 1e-12
SCALE = HEAD_DIM**-0.5
BF = jnp.bfloat16
F32 = jnp.float32
BOTH = ("seq", "rows")
MIB = 1 << 20

BQ, BK, BV, BO, G1, C1, BU, G2, C2 = range(9)
LSE_HI, LSE_LO, DELTA_HI, DELTA_LO = 0, 16, 32, 48


def dot(a, b):
    return jnp.dot(a, b, preferred_element_type=F32)


def dot_nt(a, b):
    return lax.dot_general(a, b, (((1,), (1,)), ((), ())), preferred_element_type=F32)


def call(kernel, name, grid, in_specs, out_specs, out_shape, args, flops, scratch=(), scalars=(), vmem=40):
    size = sum(a.size * a.dtype.itemsize for a in args) + sum(
        s.size * s.dtype.itemsize for s in jax.tree.leaves(out_shape)
    )
    return pl.pallas_call(
        kernel,
        name=name,
        grid_spec=pltpu.PrefetchScalarGridSpec(
            num_scalar_prefetch=len(scalars),
            grid=grid,
            in_specs=in_specs,
            out_specs=out_specs,
            scratch_shapes=list(scratch),
        ),
        out_shape=out_shape,
        compiler_params=pltpu.CompilerParams(
            dimension_semantics=("arbitrary",) * len(grid), vmem_limit_bytes=vmem * MIB
        ),
        cost_estimate=pl.CostEstimate(flops=int(flops), bytes_accessed=int(size), transcendentals=0),
    )(*scalars, *args)


def whole(array):
    return pl.BlockSpec(array.shape, lambda *_: (0,) * array.ndim)


def layer_block(array, layer):
    return pl.BlockSpec((None,) + array.shape[1:], lambda *_: (layer,) + (0,) * (array.ndim - 1))


def sds(shape, dtype):
    return jax.ShapeDtypeStruct(shape, dtype)


def lane_is_even(shape):
    return lax.broadcasted_iota(jnp.int32, shape, 1) % 2 == 0


def swap_pairs(v):
    return jnp.where(lane_is_even(v.shape), pltpu.roll(v, LANES - 1, 1), pltpu.roll(v, 1, 1))


def lanes(j):
    return slice(j * LANES, (j + 1) * LANES)


def qkv_kernel(x_ref, wq_ref, wk_ref, wv_ref, vec_ref, cos_ref, sin_ref, q_ref, k_ref, v_ref):
    x, cos, sin = x_ref[...], cos_ref[...], sin_ref[...]
    for w_ref, row, o_ref in ((wq_ref, BQ, q_ref), (wk_ref, BK, k_ref)):
        y = dot(x, w_ref[...]) + vec_ref[row : row + 1, :]
        for j in range(PAIRS):
            t = y[:, lanes(j)]
            o_ref[:, lanes(j)] = (t * cos + swap_pairs(t) * sin).astype(BF)
    v_ref[...] = (dot(x, wv_ref[...]) + vec_ref[BV : BV + 1, :]).astype(BF)


def project(rows, layer, wq, wk, wv, vec, cos, sin):
    total = rows.shape[0]
    block = min(256, total)
    tok = lambda w: pl.BlockSpec((block, w), lambda i: (i, 0))
    return call(
        qkv_kernel, "qkv", (total // block,),
        [tok(D)] + [layer_block(w, layer) for w in (wq, wk, wv, vec)] + [tok(LANES), tok(LANES)],
        [tok(D)] * 3, [sds((total, D), BF)] * 3,
        (rows, wq, wk, wv, vec, cos, sin), 6 * total * D * D,
    )


def over_chunks(total, body, carry):
    size = min(total, 1024)
    if size == total:
        return body(slice(None), carry)
    return lax.fori_loop(
        0, total // size, lambda i, c: body(pl.ds(pl.multiple_of(i * size, size), size), c), carry
    )


def two_heads(v):
    low = lax.broadcasted_iota(jnp.int32, v.shape, 1) < HEAD_DIM
    zero = jnp.zeros_like(v)
    return jnp.concatenate([jnp.where(low, v, zero), jnp.where(low, zero, v)], axis=0)


def join_heads(v):
    n = v.shape[0] // 2
    low = lax.broadcasted_iota(jnp.int32, (n, LANES), 1) < HEAD_DIM
    return jnp.where(low, v[:n], v[n:])


def attend_kernel(q_ref, k_ref, v_ref, own_ref, all_ref, attn_ref, lse_ref):
    pair = pl.program_id(0)
    n, total = q_ref.shape[0], k_ref.shape[0]
    q = two_heads(q_ref[...] * jnp.asarray(SCALE, BF))
    own = own_ref[...]

    def body(at, carry):
        top, tot, acc = carry
        same = own == all_ref[:, at]
        s = jnp.where(jnp.concatenate([same, same], axis=0), dot_nt(q, k_ref[at, :]), NEG_FILL)
        fresh = jnp.maximum(top, jnp.max(s, axis=1, keepdims=True))
        e = jnp.exp(s - fresh)
        keep = jnp.exp(top - fresh)
        tot = tot * keep + jnp.sum(e, axis=1, keepdims=True)
        acc = acc * keep + dot(e.astype(BF), v_ref[at, :])
        return fresh, tot, acc

    zero = jnp.zeros((2 * n, 1), F32)
    top, tot, acc = over_chunks(total, body, (zero + NEG_FILL, zero, jnp.zeros((2 * n, LANES), F32)))
    attn_ref[...] = join_heads(acc / tot)
    lse = top + jnp.log(tot)
    lane = lax.broadcasted_iota(jnp.int32, (n, LANES), 1)

    @pl.when(pair == 0)
    def _():
        lse_ref[...] = jnp.zeros_like(lse_ref)

    old = lse_ref[...]
    lse_ref[...] = jnp.where(lane == 2 * pair, lse[:n], jnp.where(lane == 2 * pair + 1, lse[n:], old))


def attend(q, k, v, own_seg, all_seg, n):
    total = k.shape[0]
    own = pl.BlockSpec((n, LANES), lambda p: (0, p))
    row = pl.BlockSpec((total, LANES), lambda p: (0, p))
    return call(
        attend_kernel, "attend", (PAIRS,),
        [own, row, row, whole(own_seg), whole(all_seg)],
        [own, pl.BlockSpec((n, LANES), lambda p: (0, 0))],
        [sds((n, D), F32), sds((n, LANES), F32)],
        (q, k, v, own_seg, all_seg), 4 * n * total * D * 2, vmem=56,
    )


def normalize(values):
    centered = values - jnp.mean(values, axis=-1, keepdims=True)
    rstd = lax.rsqrt(jnp.mean(centered * centered, axis=-1, keepdims=True) + NORM_EPS)
    return centered * rstd, rstd


FB = 768


def ffn_kernel(
    x_ref, attn_ref, wo_ref, wi_ref, bi_ref, wu_ref, vec_ref,
    out_ref, outb_ref, n1_ref, n2_ref, stat_ref, slope_ref, pack_ref,
    hid_ref, acc_ref,
):
    j = pl.program_id(0)
    lane = lax.broadcasted_iota(jnp.int32, stat_ref.shape, 1)

    @pl.when(j == 0)
    def _():
        attn_b = attn_ref[...].astype(BF)
        pack_ref[:, D : 2 * D] = attn_b
        branch = dot(attn_b, wo_ref[...]) + vec_ref[BO : BO + 1, :]
        n1, r1 = normalize(x_ref[...].astype(F32) + branch)
        hidden = n1 * vec_ref[G1 : G1 + 1, :] + vec_ref[C1 : C1 + 1, :]
        n1_ref[...] = n1
        stat_ref[...] = jnp.where(lane == 0, r1, 0.0)
        pack_ref[:, :D] = hidden.astype(BF)
        hid_ref[...] = hidden
        acc_ref[...] = jnp.zeros_like(acc_ref)

    inner = dot(pack_ref[:, :D], wi_ref[...]) + bi_ref[...]
    half = 0.5 + 0.5 * lax.erf(inner * (0.5**0.5))
    active = (inner * half).astype(BF)
    slope_ref[...] = half + inner * jnp.exp(-0.5 * inner * inner) * 0.3989422804014327
    pack_ref[:, pl.ds(pl.multiple_of(2 * D + j * FB, LANES), FB)] = active
    acc_ref[...] += dot(active, wu_ref[...])

    @pl.when(j == pl.num_programs(0) - 1)
    def _():
        n2, r2 = normalize(hid_ref[...] + acc_ref[...] + vec_ref[BU : BU + 1, :])
        out = n2 * vec_ref[G2 : G2 + 1, :] + vec_ref[C2 : C2 + 1, :]
        n2_ref[...] = n2
        stat_ref[...] = jnp.where(lane == 1, r2, stat_ref[...])
        out_ref[...] = out
        outb_ref[...] = out.astype(BF)


def feed_forward(x, attn, layer, wo, wi, bi, wu, vec):
    n = x.shape[0]
    fixed = lambda w: pl.BlockSpec((n, w), lambda j: (0, 0))
    return call(
        ffn_kernel, "ffn", (FF // FB,),
        [
            fixed(D), fixed(D), layer_block(wo, layer),
            pl.BlockSpec((None, D, FB), lambda j: (layer, 0, j)),
            pl.BlockSpec((None, 1, FB), lambda j: (layer, 0, j)),
            pl.BlockSpec((None, FB, D), lambda j: (layer, j, 0)),
            layer_block(vec, layer),
        ],
        [fixed(D)] * 4 + [fixed(LANES), pl.BlockSpec((n, FB), lambda j: (0, j)), fixed(2 * D + FF)],
        [sds((n, D), F32), sds((n, D), BF), sds((n, D), F32), sds((n, D), F32), sds((n, LANES), F32),
         sds((n, FF), F32), sds((n, 2 * D + FF), BF)],
        (x, attn, wo, wi, bi, wu, vec), 2 * n * (D * D + 2 * D * FF),
        scratch=[pltpu.VMEM((n, D), F32), pltpu.VMEM((n, D), F32)],
    )


def column_sum(v):
    return jnp.sum(v.astype(F32), axis=0, keepdims=True)


def norm_back(grad, normed, rstd, gain):
    scaled = grad * gain
    centered = scaled - jnp.mean(scaled, axis=-1, keepdims=True)
    return rstd * (centered - normed * jnp.mean(scaled * normed, axis=-1, keepdims=True))


def halves(v, c):
    part = [v[:, k * CHUNK : (k + 1) * CHUNK] for k in range(4)]
    even, odd = jnp.concatenate([part[0], part[2]], axis=1), jnp.concatenate([part[1], part[3]], axis=1)
    return jnp.where(c == 0, even, odd), jnp.where(c == 0, odd, even)


def hi_lo(v):
    hi = v.astype(BF)
    return hi, (v - hi.astype(F32)).astype(BF)


def ffn_back_kernel(
    place_ref, grad_ref, n1_ref, n2_ref, stat_ref, slope_ref, wu_ref, wi_ref, wo_ref, vec_ref, attn_ref, lse_ref,
    keep_ref, send_ref, keep_in_ref, send_in_ref, pre_ref, pack_ref, delta_ref, sums_ref, inner_sum_ref,
    two_ref, outer_ref, acc_ref,
):
    j = pl.program_id(0)
    c = place_ref[2]

    @pl.when(j == 0)
    def _():
        grad, n2 = grad_ref[...].astype(F32), n2_ref[...]
        sums_ref[0:1, :] = column_sum(grad * n2)
        sums_ref[1:2, :] = column_sum(grad)
        pre_two = norm_back(grad, n2, stat_ref[:, 1:2], vec_ref[G2 : G2 + 1, :])
        outer = pre_two.astype(BF)
        sums_ref[2:3, :] = column_sum(outer)
        two_ref[...] = pre_two
        outer_ref[...] = outer
        keep, send = halves(outer, c)
        keep_ref[:, : 2 * CHUNK] = keep
        send_ref[:, : 2 * CHUNK] = send
        acc_ref[...] = jnp.zeros_like(acc_ref)

    inner = (dot_nt(outer_ref[...], wu_ref[...]) * slope_ref[...]).astype(BF)
    inner_sum_ref[...] = column_sum(inner)

    @pl.when(j % 2 == c)
    def _():
        keep_in_ref[...] = inner

    @pl.when(j % 2 != c)
    def _():
        send_in_ref[...] = inner

    acc_ref[...] += dot_nt(inner, wi_ref[...])

    @pl.when(j == pl.num_programs(0) - 1)
    def _():
        grad, n1 = two_ref[...] + acc_ref[...], n1_ref[...]
        sums_ref[3:4, :] = column_sum(grad * n1)
        sums_ref[4:5, :] = column_sum(grad)
        pre_one = norm_back(grad, n1, stat_ref[:, 0:1], vec_ref[G1 : G1 + 1, :])
        pre_ref[...] = pre_one
        branch = pre_one.astype(BF)
        sums_ref[5:6, :] = column_sum(branch)
        sums_ref[6:8, :] = jnp.zeros((2, D), F32)
        keep, send = halves(branch, c)
        keep_ref[:, 2 * CHUNK :] = keep
        send_ref[:, 2 * CHUNK :] = send
        attn_grad = dot_nt(branch, wo_ref[...]).astype(BF)
        pack_ref[:, :D] = attn_grad
        feature = lax.broadcasted_iota(jnp.int32, (D, LANES), 0) // HEAD_DIM
        member = (feature == lax.broadcasted_iota(jnp.int32, (D, LANES), 1)).astype(BF)
        hi, lo = hi_lo(attn_grad.astype(F32) * attn_ref[...])
        delta = dot(hi, member) + dot(lo, member)
        delta_ref[...] = delta
        lse_hi, lse_lo = hi_lo(lse_ref[...])
        delta_hi, delta_lo = hi_lo(delta)
        extra = lse_hi.astype(F32)
        for v, at in ((lse_lo, LSE_LO), (delta_hi, DELTA_HI), (delta_lo, DELTA_LO)):
            extra = extra + pltpu.roll(v.astype(F32), at, 1)
        pack_ref[:, D:] = extra.astype(BF)


def feed_forward_back(spot, grad, kept, layer, wu, wi, wo, vec):
    n = grad.shape[0]
    assert FF // FB == 4
    fixed = lambda w: pl.BlockSpec((n, w), lambda j, s: (0, 0))
    args = (grad, kept["n1"], kept["n2"], kept["stat"], kept["slope"], wu, wi, wo, vec, kept["attn"], kept["lse"])
    return call(
        ffn_back_kernel, "ffn_back", (FF // FB,),
        [
            fixed(D), fixed(D), fixed(D), fixed(LANES),
            pl.BlockSpec((n, FB), lambda j, s: (0, j)),
            pl.BlockSpec((None, FB, D), lambda j, s: (layer, j, 0)),
            pl.BlockSpec((None, D, FB), lambda j, s: (layer, 0, j)),
            layer_block(wo, layer), layer_block(vec, layer), fixed(D), fixed(LANES),
        ],
        [
            fixed(4 * CHUNK), fixed(4 * CHUNK), pl.BlockSpec((n, FB), lambda j, s: (0, j // 2)), pl.BlockSpec((n, FB), lambda j, s: (0, j // 2)),
            fixed(D), fixed(D + LANES), fixed(LANES),
            pl.BlockSpec((8, D), lambda j, s: (0, 0)), pl.BlockSpec((1, FB), lambda j, s: (0, j)),
        ],
        [sds((n, 4 * CHUNK), BF)] * 2 + [sds((n, 2 * FB), BF)] * 2
        + [sds((n, D), F32), sds((n, D + LANES), BF), sds((n, LANES), F32), sds((8, D), F32), sds((1, FF), F32)],
        args, 2 * n * (D * D + 2 * D * FF),
        scratch=[pltpu.VMEM((n, D), F32), pltpu.VMEM((n, D), BF), pltpu.VMEM((n, D), F32)],
        scalars=(spot,),
    )


def unrotate(v, cos, sin):
    t = v * sin
    return v * cos + swap_pairs(t)


def lane_of(v, lane):
    at = lax.broadcasted_iota(jnp.int32, v.shape, 1)
    return jnp.sum(jnp.where(at == lane, v, 0.0), axis=1, keepdims=True)


def query_back_kernel(
    place_ref, q_ref, k_ref, v_ref, g_ref, lse_ref, delta_ref, own_ref, all_ref, cos_ref, sin_ref,
    dq_ref, keep_ref, send_ref, sum_ref,
    full_ref,
):
    pair = pl.program_id(0)
    n, total = q_ref.shape[0], k_ref.shape[0]
    q = two_heads(q_ref[...] * jnp.asarray(SCALE, BF))
    g = two_heads(g_ref[...])
    own = own_ref[...]
    lse = jnp.concatenate([lane_of(lse_ref[...], 2 * pair), lane_of(lse_ref[...], 2 * pair + 1)], axis=0)
    delta = jnp.concatenate([lane_of(delta_ref[...], 2 * pair), lane_of(delta_ref[...], 2 * pair + 1)], axis=0)

    def body(at, acc):
        same = own == all_ref[:, at]
        k = k_ref[at, :]
        s = jnp.where(jnp.concatenate([same, same], axis=0), dot_nt(q, k) - lse, NEG_FILL)
        ds = (jnp.exp(s) * (dot_nt(g, v_ref[at, :]) - delta)).astype(BF)
        return acc + dot(ds, k)

    acc = join_heads(over_chunks(total, body, jnp.zeros((2 * n, LANES), F32))) * SCALE
    dq = unrotate(acc, cos_ref[...], sin_ref[...]).astype(BF)
    dq_ref[...] = dq
    sum_ref[...] = column_sum(dq)
    full_ref[:, pl.ds(pl.multiple_of(pair * LANES, LANES), LANES)] = dq

    @pl.when(pair == pl.num_programs(0) - 1)
    def _():
        keep_ref[...], send_ref[...] = halves(full_ref[...], place_ref[2])


def query_back(spot, q, k, v, pack, lse, delta, own_seg, all_seg, cos, sin):
    n, total = pack.shape[0], k.shape[0]
    own = pl.BlockSpec((n, LANES), lambda p, s: (0, p))
    row = pl.BlockSpec((total, LANES), lambda p, s: (0, p))
    fixed = lambda w: pl.BlockSpec((n, w), lambda p, s: (0, 0))
    return call(
        query_back_kernel, "query_back", (PAIRS,),
        [own, row, row, own, fixed(LANES), fixed(LANES), whole(own_seg), whole(all_seg), fixed(LANES), fixed(LANES)],
        [own, fixed(2 * CHUNK), fixed(2 * CHUNK), pl.BlockSpec((1, LANES), lambda p, s: (0, p))],
        [sds((n, D), BF), sds((n, 2 * CHUNK), BF), sds((n, 2 * CHUNK), BF), sds((1, D), F32)],
        (q, k, v, pack, lse, delta, own_seg, all_seg, cos, sin), 6 * n * total * D * 2,
        scratch=[pltpu.VMEM((n, D), BF)], scalars=(spot,), vmem=56,
    )


def key_back_kernel(
    place_ref, k_ref, v_ref, q_ref, g_ref, extra_ref, own_ref, all_ref, cos_ref, sin_ref,
    dk_ref, dv_ref, keep_ref, send_ref, dk_sum_ref, dv_sum_ref,
    rows_ref, full_k_ref, full_v_ref,
):
    pair = pl.program_id(0)
    n, total = k_ref.shape[0], q_ref.shape[0]

    @pl.when(pair == 0)
    def _():
        row = lax.broadcasted_iota(jnp.int32, (32, LANES), 0)
        lane = lax.broadcasted_iota(jnp.int32, (32, LANES), 1)
        first = jnp.where(row < 16, LSE_HI, DELTA_HI - 16) + row
        pick = ((lane == first) | (lane == first + 16)).astype(BF)

        def fill(at, carry):
            rows_ref[:, at] = dot_nt(pick, extra_ref[at, :])
            return carry

        over_chunks(total, fill, 0)

    k = two_heads(k_ref[...] * jnp.asarray(SCALE, BF))
    v = two_heads(v_ref[...])
    own = own_ref[...]

    def body(at, carry):
        dk, dv = carry
        same = own == all_ref[:, at]
        q, g = q_ref[at, :], g_ref[at, :]
        s, dp = dot_nt(k, q), dot_nt(v, g)
        probs, ds = [], []
        for h in range(2):
            part = slice(h * n, (h + 1) * n)
            lse = rows_ref[pl.ds(2 * pair + h, 1), at]
            delta = rows_ref[pl.ds(16 + 2 * pair + h, 1), at]
            p = jnp.exp(jnp.where(same, s[part] - lse, NEG_FILL))
            probs.append(p.astype(BF))
            ds.append((p * (dp[part] - delta)).astype(BF))
        dk = dk + dot(jnp.concatenate(ds, axis=0), q)
        dv = dv + dot(jnp.concatenate(probs, axis=0), g)
        return dk, dv

    zero = jnp.zeros((2 * n, LANES), F32)
    dk, dv = over_chunks(total, body, (zero, zero))
    dk = unrotate(join_heads(dk) * SCALE, cos_ref[...], sin_ref[...]).astype(BF)
    dv = join_heads(dv).astype(BF)
    dk_ref[...] = dk
    dv_ref[...] = dv
    dk_sum_ref[...] = column_sum(dk)
    dv_sum_ref[...] = column_sum(dv)
    at = pl.ds(pl.multiple_of(pair * LANES, LANES), LANES)
    full_k_ref[:, at] = dk
    full_v_ref[:, at] = dv

    @pl.when(pair == pl.num_programs(0) - 1)
    def _():
        c = place_ref[2]
        k_keep, k_send = halves(full_k_ref[...], c)
        v_keep, v_send = halves(full_v_ref[...], c)
        for o_ref, kk, vv in ((keep_ref, k_keep, v_keep), (send_ref, k_send, v_send)):
            parts = [u[:, y * CHUNK : (y + 1) * CHUNK] for y in range(2) for u in (kk, vv)]
            o_ref[...] = jnp.concatenate(parts, axis=1)


def key_back(spot, k, v, q, pack_all, own_seg, all_seg, cos, sin, n):
    total = q.shape[0]
    own = pl.BlockSpec((n, LANES), lambda p, s: (0, p))
    row = pl.BlockSpec((total, LANES), lambda p, s: (0, p))
    fixed = lambda w: pl.BlockSpec((n, w), lambda p, s: (0, 0))
    one = pl.BlockSpec((1, LANES), lambda p, s: (0, p))
    return call(
        key_back_kernel, "key_back", (PAIRS,),
        [own, own, row, row, pl.BlockSpec((total, LANES), lambda p, s: (0, PAIRS)),
         whole(own_seg), whole(all_seg), fixed(LANES), fixed(LANES)],
        [own, own, fixed(4 * CHUNK), fixed(4 * CHUNK), one, one],
        [sds((n, D), BF), sds((n, D), BF), sds((n, 4 * CHUNK), BF), sds((n, 4 * CHUNK), BF), sds((1, D), F32), sds((1, D), F32)],
        (k, v, q, pack_all, pack_all, own_seg, all_seg, cos, sin), 8 * n * total * D * 2,
        scratch=[pltpu.VMEM((32, total), F32), pltpu.VMEM((n, D), BF), pltpu.VMEM((n, D), BF)],
        scalars=(spot,), vmem=56,
    )


def input_back_kernel(pre_ref, dq_ref, dk_ref, dv_ref, wq_ref, wk_ref, wv_ref, out_ref):
    total = pre_ref[...]
    for d_ref, w_ref in ((dq_ref, wq_ref), (dk_ref, wk_ref), (dv_ref, wv_ref)):
        total = total + dot_nt(d_ref[...], w_ref[...])
    out_ref[...] = total.astype(out_ref.dtype)


def input_back(pre_one, dq, dk, dv, layer, wq, wk, wv, dtype):
    n = pre_one.shape[0]
    block = 256
    col = pl.BlockSpec((n, block), lambda j: (0, j))
    fixed = pl.BlockSpec((n, D), lambda j: (0, 0))
    weight = pl.BlockSpec((None, block, D), lambda j: (layer, j, 0))
    return call(
        input_back_kernel, "input_back", (D // block,), [col, fixed, fixed, fixed, weight, weight, weight],
        col, sds((n, D), dtype), (pre_one, dq, dk, dv, wq, wk, wv), 6 * n * D * D,
    )


def turned(ref, *parts):
    n = parts[0].shape[0]
    for i, part in enumerate(parts):
        ref[:, i * n : (i + 1) * n] = part.T


def shard_rows(ref, x):
    width = D // 8
    return jnp.concatenate(
        [ref[pl.ds(pl.multiple_of((2 * z + x) * width, 32), width), :] for z in range(4)], axis=0
    )


def inner_kernel(place_ref, a_ref, b_ref, gk_ref, gg_ref, keep_ref, send_ref, at_ref):
    @pl.when(pl.program_id(0) == 0)
    def _():
        turned(at_ref, a_ref[...], b_ref[...])

    g = jnp.concatenate([gk_ref[...], gg_ref[...]], axis=0)
    x = place_ref[0]
    for o_ref, side in ((keep_ref, x), (send_ref, 1 - x)):
        o_ref[...] = dot(shard_rows(at_ref, side), g).astype(BF).reshape(o_ref.shape)


def inner_pieces(spot, own, other, keep, got):
    n = own.shape[0]
    a = pl.BlockSpec((n, D), lambda y, s: (0, 0))
    g = pl.BlockSpec((n, FB), lambda y, s: (0, y))
    o = pl.BlockSpec((1, 4, D // 8, FB), lambda y, s: (y, 0, 0, 0))
    return call(
        inner_kernel, "inner_pieces", (2,), [a, a, g, g], [o, o], [sds((2, 4, D // 8, FB), BF)] * 2,
        (own, other, keep, got), 2 * 2 * n * D * 2 * FB,
        scratch=[pltpu.VMEM((D, 2 * n), BF)], scalars=(spot,),
    )


def outer_kernel(place_ref, a_ref, b_ref, gk_ref, gg_ref, keep_ref, send_ref, gt_ref):
    @pl.when(pl.program_id(0) == 0)
    def _():
        for h in range(2):
            part = slice(h * CHUNK, (h + 1) * CHUNK)
            turned(gt_ref.at[h], gk_ref[:, part], gg_ref[:, part])

    a = jnp.concatenate([a_ref[...], b_ref[...]], axis=0)
    y = place_ref[1]
    width = FF // 8
    for o_ref, side in ((keep_ref, y), (send_ref, 1 - y)):
        out = dot(gt_ref[side], a).astype(BF)
        for x in range(2):
            o_ref[0, x] = out[:, x * width : (x + 1) * width]


def outer_pieces(spot, own, other, keep, got):
    n = own.shape[0]
    a = pl.BlockSpec((n, 2 * FF // 8), lambda z, s: (0, 2 + z))
    g = pl.BlockSpec((n, 2 * CHUNK), lambda z, s: (0, 0))
    o = pl.BlockSpec((1, 2, CHUNK, FF // 8), lambda z, s: (z, 0, 0, 0))
    return call(
        outer_kernel, "outer_pieces", (4,), [a, a, g, g], [o, o], [sds((4, 2, CHUNK, FF // 8), BF)] * 2,
        (own, other, keep, got), 2 * 2 * n * FF * 2 * CHUNK,
        scratch=[pltpu.VMEM((2, CHUNK, 2 * n), BF)], scalars=(spot,),
    )


def query_out_kernel(place_ref, rows_ref, a_ref, b_ref, qk_ref, qg_ref, ok_ref, og_ref, keep_ref, send_ref, in_ref, at_ref):
    turned(in_ref, rows_ref[...])
    turned(at_ref, a_ref[...], b_ref[...])
    gq = jnp.concatenate([qk_ref[...], qg_ref[...]], axis=0)
    go = jnp.concatenate([ok_ref[...], og_ref[...]], axis=0)
    x = place_ref[0]
    for o_ref, side in ((keep_ref, x), (send_ref, 1 - x)):
        q = dot(shard_rows(in_ref, side), gq)
        o = dot(shard_rows(at_ref, side), go)
        for y in range(2):
            part = slice(y * CHUNK, (y + 1) * CHUNK)
            both = jnp.concatenate([q[:, part], o[:, part]], axis=1).astype(BF)
            o_ref[y] = both.reshape(o_ref.shape[1:])


def query_out_pieces(spot, rows, own, other, q_keep, q_got, keep, got):
    n = own.shape[0]
    a = pl.BlockSpec((n, D), lambda i, s: (0, 1))
    q = pl.BlockSpec((n, 2 * CHUNK), lambda i, s: (0, 0))
    g = pl.BlockSpec((n, 2 * CHUNK), lambda i, s: (0, 1))
    o = pl.BlockSpec((2, 4, D // 8, 2 * CHUNK), lambda i, s: (0, 0, 0, 0))
    return call(
        query_out_kernel, "query_out_pieces", (1,),
        [pl.BlockSpec((2 * n, D), lambda i, s: (0, 0)), a, a, q, q, g, g], [o, o],
        [sds((2, 4, D // 8, 2 * CHUNK), BF)] * 2, (rows, own, other, q_keep, q_got, keep, got),
        4 * 2 * n * D * 2 * CHUNK, scratch=[pltpu.VMEM((D, 2 * n), BF)] * 2, scalars=(spot,),
    )


def key_value_kernel(place_ref, rows_ref, gk_ref, gg_ref, keep_ref, send_ref, in_ref):
    turned(in_ref, rows_ref[...])
    x = place_ref[0]
    for y in range(2):
        part = slice(y * 2 * CHUNK, (y + 1) * 2 * CHUNK)
        g = jnp.concatenate([gk_ref[:, part], gg_ref[:, part]], axis=0)
        for o_ref, side in ((keep_ref, x), (send_ref, 1 - x)):
            o_ref[y] = dot(shard_rows(in_ref, side), g).astype(BF).reshape(o_ref.shape[1:])


def key_value_pieces(spot, rows, keep, got):
    n = keep.shape[0]
    g = pl.BlockSpec((n, 4 * CHUNK), lambda i, s: (0, 0))
    o = pl.BlockSpec((2, 4, D // 8, 2 * CHUNK), lambda i, s: (0, 0, 0, 0))
    return call(
        key_value_kernel, "key_value_pieces", (1,),
        [pl.BlockSpec((2 * n, D), lambda i, s: (0, 0)), g, g], [o, o], [sds((2, 4, D // 8, 2 * CHUNK), BF)] * 2,
        (rows, keep, got), 4 * 2 * n * D * 2 * CHUNK, scratch=[pltpu.VMEM((D, 2 * n), BF)], scalars=(spot,),
    )


def linear(z, x, y, c):
    return (z * 2 + x) * 4 + y * 2 + c


PLACES = [(z, x, y, c) for z in range(4) for x in range(2) for y in range(2) for c in range(2)]


def move(array, where):
    pairs = [(linear(*place), linear(*where(*place))) for place in PLACES]
    return lax.ppermute(array, BOTH, pairs)


def to_plane(z, x, y, c):
    return (2 * y + c, x, z >> 1, z & 1)


def other_core(z, x, y, c):
    return (z, x, y, 1 - c)


def other_x(z, x, y, c):
    return (z, 1 - x, y, c)


def other_y(z, x, y, c):
    return (z, x, 1 - y, c)


def other_xy(z, x, y, c):
    return (z, 1 - x, 1 - y, c)


def along_z(step):
    return lambda z, x, y, c: ((z + step) % 4, x, y, c)


def pick(array, index, axis):
    return lax.dynamic_index_in_dim(array, index, axis, keepdims=False)


def add(a, b):
    return (a.astype(F32) + b.astype(F32)).astype(BF)


class Small:
    def __init__(self):
        seq, rows = lax.axis_index("seq"), lax.axis_index("rows")
        self.z, self.x, self.y, self.c = seq // 2, seq % 2, rows // 2, rows % 2
        self.spot = jnp.stack([self.x, self.y, self.c, self.z]).astype(jnp.int32)

    def enter(self, array):
        return move(array, to_plane)

    leave = enter

    def starts(self, count):
        out = []
        for dc in (0, 1):
            for dx, dy in ((0, 0), (1, 0), (0, 1), (1, 1)):
                x, y, c = self.x ^ dx, self.y ^ dy, self.c ^ dc
                out.append(((2 * y + c) * 2 + x) * count)
        out[1:5] = [out[4], out[1], out[2], out[3]]
        return jnp.stack(out)

    def gather(self, array):
        near = [array, move(array, other_core)]
        far = jnp.concatenate([move(array, other_x), move(array, other_y), move(array, other_xy)], axis=0)
        return jnp.concatenate(near + [far, move(far, other_core)], axis=0)

    def finish(self, t):
        total = pick(t, self.z, 0).astype(F32)
        for k in (1, 2, 3):
            total = total + move(pick(t, (self.z + k) % 4, 0), along_z(k)).astype(F32)
        return total

    def x_first(self, keep, send):
        s = add(keep, move(send, other_x))
        return self.finish(add(pick(s, self.y, 0), move(pick(s, 1 - self.y, 0), other_y)))

    def y_first(self, keep, send):
        s = add(keep, move(send, other_y))
        return self.finish(add(pick(s, self.x, 1), move(pick(s, 1 - self.x, 1), other_x)))

    def carry(self, kept):
        kept["pack_other"] = move(kept["pack"], other_core)

    def feed_grads(self, kept, keep, send, keep_in, send_in):
        got, got_in = move(send, other_core), move(send_in, other_core)
        own, other = kept["pack"], kept["pack_other"]
        inner = self.x_first(*inner_pieces(self.spot, own, other, keep_in, got_in))
        outer = self.y_first(*outer_pieces(self.spot, own, other, keep, got))
        return {"inner": inner, "outer": outer.T, "keep": keep, "got": got}

    def query_grads(self, kept, grads, dq, keep, send):
        got = move(send, other_core)
        pieces = query_out_pieces(
            self.spot, kept["rows"], kept["pack"], kept["pack_other"], keep, got, grads["keep"], grads["got"]
        )
        both = self.x_first(*pieces)
        grads["query"], grads["out"] = both[:, :CHUNK], both[:, CHUNK:]

    def key_grads(self, kept, grads, dk, dv, keep, send):
        got = move(send, other_core)
        both = self.x_first(*key_value_pieces(self.spot, kept["rows"], keep, got))
        grads["key"], grads["value"] = both[:, :CHUNK], both[:, CHUNK:]

    def vectors(self, flat):
        for where in (other_core, other_x, other_y):
            flat = flat + move(flat, where)
        flat = flat + move(flat, lambda z, x, y, c: (z ^ 1, x, y, c))
        return flat + move(flat, lambda z, x, y, c: (z ^ 2, x, y, c))


class Large:
    def __init__(self):
        self.shards = lax.axis_size("seq")
        self.spot = jnp.zeros((4,), jnp.int32)

    def enter(self, array):
        return array

    leave = enter

    def starts(self, count):
        me = lax.axis_index("seq")
        return (me + jnp.arange(self.shards, dtype=jnp.int32)) % self.shards * count

    def gather(self, array):
        whole_row = lax.all_gather(array, "seq", axis=0, tiled=True)
        return jnp.roll(whole_row, -lax.axis_index("seq") * array.shape[0], axis=0)

    def carry(self, kept):
        pass

    def spread(self, left, right):
        grad = lax.dot_general(left, right, (((0,), (0,)), ((), ())), preferred_element_type=F32).astype(BF)
        grad = lax.psum_scatter(grad, "seq", scatter_dimension=0, tiled=True)
        return lax.psum_scatter(grad, "rows", scatter_dimension=1, tiled=True).astype(F32)

    def feed_grads(self, kept, keep, send, keep_in, send_in):
        def mixed(a, b, at, w):
            return jnp.concatenate([a[:, at : at + w], b[:, at : at + w], a[:, at + w : at + 2 * w], b[:, at + w : at + 2 * w]], axis=1)

        pack = kept["pack"]
        return {
            "inner": self.spread(pack[:, :D], mixed(keep_in, send_in, 0, FB)),
            "outer": self.spread(pack[:, 2 * D :], mixed(keep, send, 0, CHUNK)),
            "out": self.spread(pack[:, D : 2 * D], mixed(keep, send, 2 * CHUNK, CHUNK)),
        }

    def query_grads(self, kept, grads, dq, keep, send):
        grads["query"] = self.spread(kept["rows"][: dq.shape[0]], dq)

    def key_grads(self, kept, grads, dk, dv, keep, send):
        grads["key"] = self.spread(kept["rows"][: dk.shape[0]], dk)
        grads["value"] = self.spread(kept["rows"][: dk.shape[0]], dv)

    def vectors(self, flat):
        return lax.psum(flat, BOTH)


def doc_layout(lengths_row, index):
    ends = jnp.cumsum(lengths_row, dtype=jnp.int32)
    passed = (index[:, None] >= ends[None, :]).astype(jnp.int32)
    segment = jnp.sum(passed, axis=1, dtype=jnp.int32)
    begin = jnp.sum(passed * lengths_row[None, :], axis=1, dtype=jnp.int32)
    return (segment, (index - begin).astype(jnp.int32))


def rotary_tables(position):
    lane = jnp.arange(LANES, dtype=jnp.int32)
    pairs = (lane % HEAD_DIM // 2).astype(F32)
    inverse = jnp.power(jnp.float32(10000.0), -2.0 * pairs / HEAD_DIM)
    angle = position.astype(F32)[:, None] * inverse[None, :]
    return jnp.cos(angle), jnp.sin(angle) * jnp.where(lane % 2 == 0, -1.0, 1.0)[None, :]


def body(large, tokens, lengths, cotangent, *params):
    wq, bq, wk, bk, wv, bv, wo, bo, g1, c1, wi, bi, wu, bu, g2, c2 = params
    place = Large() if large else Small()
    spot = place.spot
    n = tokens.shape[1]
    current = place.enter(tokens[0])
    lengths_row = place.enter(lengths)[0]
    vec = jnp.stack([bq, bk, bv, bo, g1, c1, bu, g2, c2], axis=1).astype(F32)
    bi = bi.astype(F32)[:, None, :]
    index = (place.starts(n)[:, None] + jnp.arange(n, dtype=jnp.int32)).reshape(-1)
    segment, position = doc_layout(lengths_row, index)
    own_seg, all_seg = segment[:n, None], segment[None, :]
    cos, sin = rotary_tables(position)
    saved = []
    current_b = current
    for layer in range(LAYERS):
        rows = place.gather(current_b)
        q, k, v = project(rows, layer, wq, wk, wv, vec, cos, sin)
        attn, lse = attend(q, k, v, own_seg, all_seg, n)
        current, current_b, n1, n2, stat, slope, pack = feed_forward(current, attn, layer, wo, wi, bi, wu, vec)
        kept = dict(rows=rows, q=q, k=k, v=v, attn=attn, lse=lse, n1=n1, n2=n2, stat=stat, slope=slope, pack=pack)
        place.carry(kept)
        saved.append(kept)
    output = place.leave(current_b)
    grad = place.enter(cotangent[0])
    grads, sums = [None] * LAYERS, [None] * LAYERS
    for layer in range(LAYERS - 1, -1, -1):
        kept = saved[layer]
        keep, send, keep_in, send_in, pre_one, pack, delta, feed_sums, inner_sum = feed_forward_back(
            spot, grad, kept, layer, wu, wi, wo, vec
        )
        pack_all = place.gather(pack)
        found = place.feed_grads(kept, keep, send, keep_in, send_in)
        dq, q_keep, q_send, dq_sum = query_back(
            spot, kept["q"], kept["k"], kept["v"], pack, kept["lse"], delta, own_seg, all_seg, cos, sin
        )
        place.query_grads(kept, found, dq, q_keep, q_send)
        dk, dv, kv_keep, kv_send, dk_sum, dv_sum = key_back(
            spot, kept["k"], kept["v"], kept["q"], pack_all, own_seg, all_seg, cos, sin, n
        )
        place.key_grads(kept, found, dk, dv, kv_keep, kv_send)
        grad = input_back(pre_one, dq, dk, dv, layer, wq, wk, wv, F32 if layer else BF)
        grads[layer] = found
        shards = lax.axis_size("seq")
        sums[layer] = jnp.concatenate(
            [
                jnp.concatenate([feed_sums[:6], dq_sum, dk_sum, dv_sum], axis=0).reshape(9, shards, -1).swapaxes(0, 1),
                inner_sum.reshape(shards, FF // D, -1),
            ],
            axis=1,
        )
    tokens_grad = place.leave(grad)
    flat = place.vectors(jnp.stack(sums, axis=1).reshape(shards, -1))
    flat = pick(flat, lax.axis_index("seq"), 0).reshape(LAYERS, 13, -1)
    g2_, c2_, bu_, g1_, c1_, bo_, bq_, bk_, bv_ = [flat[:, i] for i in range(9)]
    bi_ = flat[:, 9:].reshape(LAYERS, -1)
    m = {name: jnp.stack([grads[layer][name] for layer in range(LAYERS)]) for name in grads[0] if name not in ("keep", "got")}
    return (
        output[None], tokens_grad[None],
        m["query"], bq_, m["key"], bk_, m["value"], bv_, m["out"], bo_, g1_, c1_,
        m["inner"], bi_, m["outer"], bu_, g2_, c2_,
    )


def solution(mesh):
    token = P("rows", "seq", None)
    mat, vec = P(None, "seq", "rows"), P(None, "seq")
    small = (mesh.shape["seq"], mesh.shape["rows"]) == (8, 4)
    return jax.shard_map(
        functools.partial(body, not small),
        mesh=mesh,
        in_specs=(token, P("rows", None), token) + (P(),) * 16,
        out_specs=(token, token, mat, vec, mat, vec, mat, vec, mat, vec, vec, vec, mat, vec, mat, vec, vec, vec),
        check_vma=False,
    )
```

```python
import jax
import jax.numpy as jnp
from jax import lax
from jax.experimental import pallas as pl
from jax.experimental.pallas import tpu as pltpu
from jax.sharding import PartitionSpec as P

D = 768
HEADS = 12
HEAD_DIM = 64
FF = 3072
LAYERS = 2
LANES = 128
PAIRS = D // LANES
CHUNK = D // 4
NEG_FILL = -1e30
NORM_EPS = 1e-12
SCALE = HEAD_DIM**-0.5
BF = jnp.bfloat16
F32 = jnp.float32
BOTH = ("seq", "rows")
MIB = 1 << 20

BQ, BK, BV, BO, G1, C1, BU, G2, C2 = range(9)
FB = 768
WIDTH = D // 8
ACTIVE = FF // 8
QKV = 3 * CHUNK
IO = FB + CHUNK
IO_PAD = FB + 2 * LANES

NEAR_OUTER, NEAR_OUT, NEAR = FB, FB + 2 * CHUNK, FB + 3 * CHUNK
NEAR_PACK = NEAR + 64
SIDE_OUT, SIDE = 2 * FB, 2 * FB + 2 * CHUNK
PACK = 2 * D + FF // 2

LSE_HI, LSE_LO, DELTA_HI, DELTA_LO = 0, 16, 32, 48


class Names(dict):
    __getattr__ = dict.__getitem__
    __setattr__ = dict.__setitem__


def dot(a, b):
    return jnp.dot(a, b, preferred_element_type=F32)


def dot_nt(a, b):
    return lax.dot_general(a, b, (((1,), (1,)), ((), ())), preferred_element_type=F32)


def call(kernel, name, grid, in_specs, out_specs, out_shape, args, flops, scratch=(), scalars=(), vmem=60, after=(), aliases=None):
    size = sum(a.size * a.dtype.itemsize for a in args) + sum(
        s.size * s.dtype.itemsize for s in jax.tree.leaves(out_shape)
    )
    lead, many = len(scalars) + len(args), len(after)

    def run(*refs):
        kernel(*refs[:lead], *refs[lead + many :])

    return pl.pallas_call(
        run,
        name=name,
        grid_spec=pltpu.PrefetchScalarGridSpec(
            num_scalar_prefetch=len(scalars),
            grid=grid,
            in_specs=list(in_specs) + [pl.BlockSpec(memory_space=pl.ANY)] * many,
            out_specs=out_specs,
            scratch_shapes=list(scratch),
        ),
        out_shape=out_shape,
        input_output_aliases=aliases or {},
        compiler_params=pltpu.CompilerParams(
            dimension_semantics=("arbitrary",) * len(grid), vmem_limit_bytes=vmem * MIB
        ),
        cost_estimate=pl.CostEstimate(flops=int(flops), bytes_accessed=int(size), transcendentals=0),
    )(*scalars, *args, *after)


def whole(array):
    return pl.BlockSpec(array.shape, lambda *_: (0,) * array.ndim)


def layer_block(array, layer):
    return pl.BlockSpec((None,) + array.shape[1:], lambda *_: (layer,) + (0,) * (array.ndim - 1))


def sds(shape, dtype):
    return jax.ShapeDtypeStruct(shape, dtype)


def lane_is_even(shape):
    return lax.broadcasted_iota(jnp.int32, shape, 1) % 2 == 0


def swap_pairs(v):
    return jnp.where(lane_is_even(v.shape), pltpu.roll(v, LANES - 1, 1), pltpu.roll(v, 1, 1))


def lanes(j):
    return slice(j * LANES, (j + 1) * LANES)


def qkv_kernel(x_ref, wq_ref, wk_ref, wv_ref, vec_ref, cos_ref, sin_ref, q_ref, k_ref, v_ref):
    x, cos, sin = x_ref[...], cos_ref[...], sin_ref[...]
    for w_ref, row, o_ref in ((wq_ref, BQ, q_ref), (wk_ref, BK, k_ref)):
        y = dot(x, w_ref[...]) + vec_ref[row : row + 1, :]
        for j in range(PAIRS):
            t = y[:, lanes(j)]
            o_ref[:, lanes(j)] = (t * cos + swap_pairs(t) * sin).astype(BF)
    v_ref[...] = (dot(x, wv_ref[...]) + vec_ref[BV : BV + 1, :]).astype(BF)


def project(rows, layer, wq, wk, wv, vec, cos, sin):
    total = rows.shape[0]
    block = min(256, total)
    tok = lambda w: pl.BlockSpec((block, w), lambda i: (i, 0))
    return call(
        qkv_kernel, "qkv", (total // block,),
        [tok(D)] + [layer_block(w, layer) for w in (wq, wk, wv, vec)] + [tok(LANES), tok(LANES)],
        [tok(D)] * 3, [sds((total, D), BF)] * 3,
        (rows, wq, wk, wv, vec, cos, sin), 6 * total * D * D,
    )


def over_chunks(total, body, carry):
    size = min(total, 1024)
    if size == total:
        return body(slice(None), carry)
    return lax.fori_loop(
        0, total // size, lambda i, c: body(pl.ds(pl.multiple_of(i * size, size), size), c), carry
    )


def two_heads(v):
    low = lax.broadcasted_iota(jnp.int32, v.shape, 1) < HEAD_DIM
    zero = jnp.zeros_like(v)
    return jnp.concatenate([jnp.where(low, v, zero), jnp.where(low, zero, v)], axis=0)


def join_heads(v):
    n = v.shape[0] // 2
    low = lax.broadcasted_iota(jnp.int32, (n, LANES), 1) < HEAD_DIM
    return jnp.where(low, v[:n], v[n:])


def normalize(values):
    centered = values - jnp.mean(values, axis=-1, keepdims=True)
    rstd = lax.rsqrt(jnp.mean(centered * centered, axis=-1, keepdims=True) + NORM_EPS)
    return centered * rstd, rstd


def column_sum(v):
    return jnp.sum(v.astype(F32), axis=0, keepdims=True)


def norm_back(grad, normed, rstd, gain):
    scaled = grad * gain
    centered = scaled - jnp.mean(scaled, axis=-1, keepdims=True)
    return rstd * (centered - normed * jnp.mean(scaled * normed, axis=-1, keepdims=True))


def either(first, a, b):
    return jnp.where(first, a, b), jnp.where(first, b, a)


def cat(*parts):
    return jnp.concatenate(parts, axis=1)


def quarters(v, y, c):
    part = [v[:, k * CHUNK : (k + 1) * CHUNK] for k in range(4)]
    mine0, theirs0 = either(c == 0, part[0], part[1])
    mine1, theirs1 = either(c == 0, part[2], part[3])
    mine, mine_y = either(y == 0, mine0, mine1)
    theirs, theirs_y = either(y == 0, theirs0, theirs1)
    return mine, theirs, mine_y, theirs_y


def hi_lo(v):
    hi = v.astype(BF)
    return hi, (v - hi.astype(F32)).astype(BF)


def unrotate(v, cos, sin):
    t = v * sin
    return v * cos + swap_pairs(t)


def lane_of(v, lane):
    at = lax.broadcasted_iota(jnp.int32, v.shape, 1)
    return jnp.sum(jnp.where(at == lane, v, 0.0), axis=1, keepdims=True)


def query_back_kernel(
    q_ref, k_ref, v_ref, g_ref, lse_ref, delta_ref, own_ref, all_ref, cos_ref, sin_ref,
    dq_ref, sum_ref,
):
    pair = pl.program_id(0)
    n, total = q_ref.shape[0], k_ref.shape[0]
    q = two_heads(q_ref[...] * jnp.asarray(SCALE, BF))
    g = two_heads(g_ref[...])
    own = own_ref[...]
    lse = jnp.concatenate([lane_of(lse_ref[...], 2 * pair), lane_of(lse_ref[...], 2 * pair + 1)], axis=0)
    delta = jnp.concatenate([lane_of(delta_ref[...], 2 * pair), lane_of(delta_ref[...], 2 * pair + 1)], axis=0)

    def body(at, acc):
        same = own == all_ref[:, at]
        k = k_ref[at, :]
        s = jnp.where(jnp.concatenate([same, same], axis=0), dot_nt(q, k) - lse, NEG_FILL)
        ds = (jnp.exp(s) * (dot_nt(g, v_ref[at, :]) - delta)).astype(BF)
        return acc + dot(ds, k)

    acc = join_heads(over_chunks(total, body, jnp.zeros((2 * n, LANES), F32))) * SCALE
    dq = unrotate(acc, cos_ref[...], sin_ref[...]).astype(BF)
    dq_ref[...] = dq
    sum_ref[...] = column_sum(dq)


def query_back(q, k, v, pack, lse, delta, own_seg, all_seg, cos, sin, after=()):
    n, total = pack.shape[0], k.shape[0]
    own = pl.BlockSpec((n, LANES), lambda p: (0, p))
    row = pl.BlockSpec((total, LANES), lambda p: (0, p))
    fixed = lambda w: pl.BlockSpec((n, w), lambda p: (0, 0))
    return call(
        query_back_kernel, "query_back", (PAIRS,),
        [own, row, row, own, fixed(LANES), fixed(LANES), whole(own_seg), whole(all_seg), fixed(LANES), fixed(LANES)],
        [own, pl.BlockSpec((1, LANES), lambda p: (0, p))],
        [sds((n, D), BF), sds((1, D), F32)],
        (q, k, v, pack, lse, delta, own_seg, all_seg, cos, sin), 6 * n * total * D * 2, after=after,
    )


def turned(ref, *parts):
    n = parts[0].shape[0]
    for i, part in enumerate(parts):
        ref[:, i * n : (i + 1) * n] = part.T


def shard_rows(ref, x):
    width = WIDTH
    return jnp.concatenate(
        [ref[pl.ds(pl.multiple_of((2 * z + x) * width, 32), width), :] for z in range(4)], axis=0
    )


def mega(kernel, name, ins, outs, scratch, flops, hbm=(), after=(), vmem=60):
    flat_in, tree_in = jax.tree.flatten(dict(ins))
    flat_out, tree_out = jax.tree.flatten(dict(outs))

    def spec_of(key):
        space = pl.ANY if key in hbm else pltpu.SMEM if key == "place" else pltpu.VMEM
        return pl.BlockSpec(memory_space=space)

    specs_in = jax.tree.leaves({k: jax.tree.map(lambda _: spec_of(k), v) for k, v in ins.items()})
    specs_out = jax.tree.leaves({k: jax.tree.map(lambda _: spec_of(k), v) for k, v in outs.items()})
    many_in, many_out = len(flat_in), len(flat_out)

    def run(*refs):
        lead = many_in + len(after)
        named = Names(tree_in.unflatten(refs[:many_in]))
        named.update(tree_out.unflatten(refs[lead : lead + many_out]))
        named.update(zip(scratch, refs[lead + many_out :]))
        kernel(named)

    size = sum(a.size * a.dtype.itemsize for a in flat_out) + sum(
        a.size * a.dtype.itemsize for k, v in ins.items() if k not in hbm for a in jax.tree.leaves(v)
    )
    out = pl.pallas_call(
        run,
        name=name,
        in_specs=specs_in + [pl.BlockSpec(memory_space=pl.ANY)] * len(after),
        out_specs=specs_out,
        out_shape=flat_out,
        scratch_shapes=list(scratch.values()),
        compiler_params=pltpu.CompilerParams(vmem_limit_bytes=vmem * MIB),
        cost_estimate=pl.CostEstimate(flops=int(flops), bytes_accessed=int(size), transcendentals=0),
    )(*flat_in, *after)
    return Names(tree_out.unflatten(out))


SHAPES = Names(wq=(D, D), wk=(D, D), wv=(D, D), wo=(D, D), wi=(D, FF), wu=(FF, D))


def rooms(names):
    found = Names(("m_" + name, pltpu.VMEM(SHAPES[name], BF)) for name in names)
    found.sems = pltpu.SemaphoreType.DMA((16,))
    return found


def units(j):
    return pl.ds(j * FB, FB)


class Copies:
    def __init__(self, sems):
        self.sems, self.copies = sems, {}

    def start(self, name, src, dst):
        self.copies[name] = pltpu.make_async_copy(src, dst, self.sems.at[len(self.copies)])
        self.copies[name].start()

    def weights(self, r, layer, names):
        for name in names:
            src, dst = r["w_" + name].at[layer], r["m_" + name]
            if name not in ("wi", "wu"):
                self.start(name, src, dst)
                continue
            for j in range(FF // FB):
                at = (slice(None), units(j)) if name == "wi" else (units(j), slice(None))
                self.start(f"{name}{j}", src.at[at], dst.at[at])

    def wait(self, *names):
        for name in names:
            if name in self.copies:
                self.copies.pop(name).wait()


def join(dst, refs, columns):
    at = 0
    for ref in refs:
        dst[at : at + ref.shape[0], :] = ref[:, columns]
        at += ref.shape[0]


def row_of(r, index):
    return r.vec[index : index + 1, :]


def qkv_phase(r, copies):
    rows, cos, sin = r.s_rows, r.cos, r.sin
    total = rows.shape[0]
    block = min(256, total)
    for name, bias in (("k", BK), ("v", BV), ("q", BQ)):
        copies.wait("w" + name)
        for i in range(total // block):
            at = pl.ds(i * block, block)
            y = dot(rows[at, :], r["m_w" + name][...]) + row_of(r, bias)
            if name == "v":
                r.s_v[at, :] = y.astype(BF)
                continue
            for j in range(PAIRS):
                t = y[:, lanes(j)]
                r["s_" + name][at, lanes(j)] = (t * cos[at, :] + swap_pairs(t) * sin[at, :]).astype(BF)


def attend_phase(r):
    n, total = r.attn.shape[0], r.s_k.shape[0]
    own = r.own[...]
    lane = lax.broadcasted_iota(jnp.int32, (n, LANES), 1)
    lse = jnp.zeros((n, LANES), F32)
    for p in range(PAIRS):
        q = two_heads(r.s_q[:n, lanes(p)] * jnp.asarray(SCALE, BF))

        def body(at, carry):
            top, tot, acc = carry
            same = own == r.all[:, at]
            s = dot_nt(q, r.s_k[at, lanes(p)])
            s = jnp.where(jnp.concatenate([same, same], axis=0), s, NEG_FILL)
            fresh = jnp.maximum(top, jnp.max(s, axis=1, keepdims=True))
            e = jnp.exp(s - fresh)
            keep = jnp.exp(top - fresh)
            tot = tot * keep + jnp.sum(e, axis=1, keepdims=True)
            acc = acc * keep + dot(e.astype(BF), r.s_v[at, lanes(p)])
            return fresh, tot, acc

        zero = jnp.zeros((2 * n, 1), F32)
        top, tot, acc = over_chunks(total, body, (zero + NEG_FILL, zero, jnp.zeros((2 * n, LANES), F32)))
        r.attn[:, lanes(p)] = join_heads(acc / tot)
        part = top + jnp.log(tot)
        lse = jnp.where(lane == 2 * p, part[:n], jnp.where(lane == 2 * p + 1, part[n:], lse))
    r.lse[...] = lse


def ffn_phase(r, copies):
    stat_ref = r.stat
    lane = lax.broadcasted_iota(jnp.int32, stat_ref.shape, 1)
    copies.wait("wo")
    branch = dot(r.attn[...].astype(BF), r.m_wo[...]) + row_of(r, BO)
    n1, r1 = normalize(r.x[...].astype(F32) + branch)
    hidden = n1 * row_of(r, G1) + row_of(r, C1)
    r.n1[...] = n1
    hidden_b = hidden.astype(BF)
    r.s_hidden[...] = hidden_b
    total = hidden + row_of(r, BU)
    for j in range(FF // FB):
        copies.wait(f"wi{j}")
        inner = dot(hidden_b, r.m_wi[:, units(j)]) + r.bi[:, units(j)]
        half = 0.5 + 0.5 * lax.erf(inner * (0.5**0.5))
        active = (inner * half).astype(BF)
        r.slope[:, units(j)] = (half + inner * jnp.exp(-0.5 * inner * inner) * 0.3989422804014327).astype(BF)
        r.s_active[:, units(j)] = active
        copies.wait(f"wu{j}")
        total = total + dot(active, r.m_wu[units(j), :])
    n2, r2 = normalize(total)
    r.n2[...] = n2
    stat_ref[...] = jnp.where(lane == 0, r1, jnp.where(lane == 1, r2, 0.0))
    return n2 * row_of(r, G2) + row_of(r, C2)


def store_active(r, ref, at, x):
    for z in range(4):
        src = pl.ds(pl.multiple_of((2 * z + x) * ACTIVE, LANES), ACTIVE)
        ref[:, at + z * ACTIVE : at + (z + 1) * ACTIVE] = r.s_active[:, src]


def store_pack(r, ref, at, x):
    ref[:, at : at + D] = r.s_hidden[...]
    ref[:, at + D : at + 2 * D] = r.attn[...].astype(BF)
    store_active(r, ref, at + 2 * D, x)


def feed_back_phase(r, copies, grad):
    place = r.place
    y, c = place[1], place[2]
    n2 = r.n2[...]
    sums = r.sums
    sums[0:1, :] = column_sum(grad * n2)
    sums[1:2, :] = column_sum(grad)
    grad = norm_back(grad, n2, r.stat[:, 1:2], row_of(r, G2))
    outer = grad.astype(BF)
    sums[2:3, :] = column_sum(outer)
    mine, theirs, mine_y, theirs_y = quarters(outer, 0, c)
    mine, theirs = cat(mine, mine_y), cat(theirs, theirs_y)
    r.near[:, NEAR_OUTER:NEAR_OUT] = mine
    r.send[:, NEAR_OUTER:NEAR_OUT] = theirs
    r.to_x[:, : 2 * CHUNK] = mine
    r.to_x[:, 2 * CHUNK : D] = theirs
    for j in range(FF // FB):
        copies.wait(f"wu{j}")
        inner = (dot_nt(outer, r.m_wu[units(j), :]) * r.slope[:, units(j)].astype(F32)).astype(BF)
        sums[6 + j : 7 + j, :] = column_sum(inner)
        r.s_inner[:, units(j)] = inner
        copies.wait(f"wi{j}")
        grad = grad + dot_nt(inner, r.m_wi[:, units(j)])
    n1 = r.n1[...]
    sums[3:4, :] = column_sum(grad * n1)
    sums[4:5, :] = column_sum(grad)
    pre_one = norm_back(grad, n1, r.stat[:, 0:1], row_of(r, G1))
    r.pre[...] = pre_one
    branch = pre_one.astype(BF)
    sums[5:6, :] = column_sum(branch)
    sums[10:16, :] = jnp.zeros((6, D), F32)
    mine, theirs, mine_y, theirs_y = quarters(branch, y, c)
    r.near[:, NEAR_OUT:NEAR] = mine
    r.send[:, NEAR_OUT:NEAR] = theirs
    r.to_y[:, SIDE_OUT:SIDE] = cat(mine_y, theirs_y)
    copies.wait("wo")
    attn_grad = dot_nt(branch, r.m_wo[...]).astype(BF)
    r.pack[:, :D] = attn_grad
    feature = lax.broadcasted_iota(jnp.int32, (D, LANES), 0) // HEAD_DIM
    member = (feature == lax.broadcasted_iota(jnp.int32, (D, LANES), 1)).astype(BF)
    hi, lo = hi_lo(attn_grad.astype(F32) * r.attn[...])
    delta = dot(hi, member) + dot(lo, member)
    r.delta[...] = delta
    lse_hi, lse_lo = hi_lo(r.lse[...])
    delta_hi, delta_lo = hi_lo(delta)
    extra = lse_hi.astype(F32)
    for v, at in ((lse_lo, LSE_LO), (delta_hi, DELTA_HI), (delta_lo, DELTA_LO)):
        extra = extra + pltpu.roll(v.astype(F32), at, 1)
    r.pack[:, D:] = extra.astype(BF)
    shard = 2 * y + c
    for ref, at, k in (
        (r.near, 0, shard), (r.send, 0, 2 * y + 1 - c), (r.to_y, 0, 2 - 2 * y + c), (r.to_y, FB, 3 - 2 * y - c),
    ):
        ref[:, at : at + FB] = r.s_inner[:, pl.ds(pl.multiple_of(k * FB, LANES), FB)]


def key_back_phase(r, copies):
    place = r.place
    n, total = r.k.shape[0], r.s_g.shape[0]
    row = lax.broadcasted_iota(jnp.int32, (32, LANES), 0)
    lane = lax.broadcasted_iota(jnp.int32, (32, LANES), 1)
    first = jnp.where(row < 16, LSE_HI, DELTA_HI - 16) + row
    pick = ((lane == first) | (lane == first + 16)).astype(BF)
    rows_ref, own = r.s_stats, r.own[...]

    def fill(at, carry):
        rows_ref[:, at] = dot_nt(pick, r.s_extra[at, :])
        return carry

    over_chunks(total, fill, 0)
    for p in range(PAIRS):
        copies.wait(f"q{p}")
        k = two_heads(r.k[:, lanes(p)] * jnp.asarray(SCALE, BF))
        v = two_heads(r.v[:, lanes(p)])

        def body(at, carry):
            dk, dv = carry
            same = own == r.all[:, at]
            q, g = r.s_q[at, lanes(p)], r.s_g[at, lanes(p)]
            s, dp = dot_nt(k, q), dot_nt(v, g)
            probs, ds = [], []
            for h in range(2):
                half = slice(h * n, (h + 1) * n)
                lse, delta = rows_ref[2 * p + h : 2 * p + h + 1, at], rows_ref[16 + 2 * p + h : 17 + 2 * p + h, at]
                prob = jnp.exp(jnp.where(same, s[half] - lse, NEG_FILL))
                probs.append(prob.astype(BF))
                ds.append((prob * (dp[half] - delta)).astype(BF))
            return dk + dot(jnp.concatenate(ds, axis=0), q), dv + dot(jnp.concatenate(probs, axis=0), g)

        zero = jnp.zeros((2 * n, LANES), F32)
        dk, dv = over_chunks(total, body, (zero, zero))
        r.s_dk[:, lanes(p)] = unrotate(join_heads(dk) * SCALE, r.cos[...], r.sin[...]).astype(BF)
        r.s_dv[:, lanes(p)] = join_heads(dv).astype(BF)
    dq, dk, dv = r.dq[...], r.s_dk[...], r.s_dv[...]
    for i, v in enumerate((dq, dk, dv)):
        r.qkv_sums[i : i + 1, :] = column_sum(v)
    r.qkv_sums[3:8, :] = jnp.zeros((5, D), F32)
    mine, theirs, mine_y, theirs_y = zip(*[quarters(v, place[1], place[2]) for v in (dq, dk, dv)])
    r.qkv_near[...] = cat(*mine)
    r.qkv_send[...] = cat(*theirs)
    r.qkv_y[...] = cat(*mine_y, *theirs_y)


def input_back_phase(r, copies):
    total = r.pre_above[...]
    for name, ref in (("wq", r.dq), ("wk", r.s_dk), ("wv", r.s_dv)):
        copies.wait(name)
        total = total + dot_nt(ref[...], r["m_" + name][...])
    return total


def layer_forward(layer, place, x, blocks, weights, bi, vec, cos, sin, own_seg, all_seg, qkv=None, cotangent=None, after=()):
    n = x.shape[0]
    total = all_seg.shape[1]
    last = cotangent is not None
    names = ("wo", "wi", "wu") if qkv else ("wk", "wv", "wq", "wo", "wi", "wu")
    ins = Names(place=place, x=x, own=own_seg, all=all_seg, bi=bi[layer], vec=vec[layer])
    ins.update({"w_" + name: weights[name] for name in names})
    hbm = {"w_" + name for name in names}
    outs = Names(attn=sds((n, D), F32), lse=sds((n, LANES), F32), result_b=sds((n, D), BF))
    scratch = Names(
        s_hidden=pltpu.VMEM((n, D), BF), s_active=pltpu.VMEM((n, FF), BF), **rooms(names),
    )
    inner = Names(
        n1=sds((n, D), F32), n2=sds((n, D), F32), stat=sds((n, LANES), F32), slope=sds((n, FF), BF),
    )
    flops = 2 * n * (D * D + 2 * D * FF) + 4 * n * total * D * 2
    if qkv:
        ins.update(zip(("s_q", "s_k", "s_v"), qkv))
    else:
        ins.update(blocks=blocks, cos=cos, sin=sin)
        for name in "qkv":
            outs[name] = sds((total, D), BF)
            hbm.add(name)
            if name != "q":
                outs["own_" + name] = sds((n, D), BF)
            scratch["s_" + name] = pltpu.VMEM((total, D), BF)
        scratch.s_rows = pltpu.VMEM((total, D), BF)
        scratch.out_sems = pltpu.SemaphoreType.DMA((3,))
        flops += 6 * total * D * D
    if last:
        scratch.update({k: pltpu.VMEM(v.shape, v.dtype) for k, v in inner.items()})
        scratch.s_inner = pltpu.VMEM((n, FF), BF)
        ins.cotangent = cotangent
        outs.update(feed_back_outs(n, True))
        flops += 2 * n * (D * D + 2 * D * FF)
    else:
        outs.update(inner)
        outs.result = sds((n, D), F32)
        outs.update(keep_pack=sds((n, PACK), BF), side=sds((n, 2 * D), BF), active=sds((n, FF // 2), BF))

    def kernel(r):
        copies = Copies(r.sems)
        copies.weights(r, layer, names)
        if not qkv:
            join(r.s_rows, r.blocks, slice(0, D))
            qkv_phase(r, copies)
            back = Copies(r.out_sems)
            for name in "qkv":
                back.start(name, r["s_" + name], r[name])
            for name in "kv":
                r["own_" + name][...] = r["s_" + name][:n, :]
        attend_phase(r)
        result = ffn_phase(r, copies)
        r.result_b[...] = result.astype(BF)
        x = r.place[0]
        if last:
            feed_back_phase(r, copies, r.cotangent[...].astype(F32))
            for ref, at in ((r.near, NEAR_PACK), (r.send, NEAR_PACK)):
                ref[:, NEAR:NEAR_PACK] = jnp.zeros((n, NEAR_PACK - NEAR), BF)
                store_pack(r, ref, at, x)
            r.to_y[:, SIDE : SIDE + D] = r.s_hidden[...]
            r.to_y[:, SIDE + D :] = r.attn[...].astype(BF)
            store_active(r, r.to_x, D, 1 - x)
        else:
            r.result[...] = result
            store_pack(r, r.keep_pack, 0, x)
            r.side[:, :D] = r.s_hidden[...]
            r.side[:, D:] = r.attn[...].astype(BF)
            store_active(r, r.active, 0, 1 - x)
        if not qkv:
            back.wait(*"qkv")

    return mega(kernel, "forward_last" if last else "forward", ins, outs, scratch, flops, hbm=hbm, after=after)


def feed_back_outs(n, last):
    return Names(
        near=sds((n, NEAR_PACK + PACK if last else NEAR), BF), send=sds((n, NEAR_PACK + PACK if last else NEAR), BF),
        to_x=sds((n, D + FF // 2 if last else D), BF), to_y=sds((n, SIDE + 2 * D if last else SIDE), BF),
        pre=sds((n, D), F32), pack=sds((n, D + LANES), BF), delta=sds((n, LANES), F32),
        sums=sds((16, D), F32),
    )


def layer_back(layer, place, kept, back, dq, blocks, weights, vec, cos, sin, own_seg, all_seg, below=None, after=()):
    n, total = dq.shape[0], all_seg.shape[1]
    names = ("wq", "wk", "wv") + (("wo", "wi", "wu") if below else ())
    ins = Names(
        place=place, k=kept.own_k, v=kept.own_v, q=kept.q, dq=dq, pre_above=back.pre, blocks=blocks,
        own=own_seg, all=all_seg, cos=cos, sin=sin,
    )
    ins.update({"w_" + name: weights[name] for name in names})
    hbm = {"w_" + name for name in names} | {"q"}
    single = len(blocks) == 1
    if single:
        hbm.add("blocks")
    outs = Names(
        qkv_near=sds((n, QKV), BF), qkv_send=sds((n, QKV), BF), qkv_y=sds((n, 2 * QKV), BF), qkv_sums=sds((8, D), F32),
        dk=sds((n, D), BF), dv=sds((n, D), BF),
    )
    scratch = Names(
        s_q=pltpu.VMEM((total, D), BF), s_g=pltpu.VMEM((total, D), BF), s_extra=pltpu.VMEM((total, LANES), BF),
        s_stats=pltpu.VMEM((32, total), F32), s_dk=pltpu.VMEM((n, D), BF), s_dv=pltpu.VMEM((n, D), BF),
        q_sems=pltpu.SemaphoreType.DMA((PAIRS + 2,)), **rooms(names),
    )
    if below:
        ins.update({k: below[k] for k in ("n1", "n2", "stat", "slope", "attn", "lse")}, vec=vec[layer - 1])
        outs.update(feed_back_outs(n, False))
        scratch.s_inner = pltpu.VMEM((n, FF), BF)
    else:
        outs.grad = sds((n, D), BF)

    def kernel(r):
        queries = Copies(r.q_sems)
        if single:
            queries.start("g", r.blocks[0].at[:, :D], r.s_g)
            queries.start("extra", r.blocks[0].at[:, D:], r.s_extra)
        for p in range(PAIRS):
            queries.start(f"q{p}", r.q.at[:, lanes(p)], r.s_q.at[:, lanes(p)])
        copies = Copies(r.sems)
        copies.weights(r, layer, names[:3])
        if below:
            copies.weights(r, layer - 1, names[3:])
        if single:
            queries.wait("g", "extra")
        else:
            join(r.s_g, r.blocks, slice(0, D))
            join(r.s_extra, r.blocks, slice(D, D + LANES))
        key_back_phase(r, queries)
        r.dk[...] = r.s_dk[...]
        r.dv[...] = r.s_dv[...]
        grad = input_back_phase(r, copies)
        if below:
            feed_back_phase(r, copies, grad)
        else:
            r.grad[...] = grad.astype(BF)

    flops = 8 * n * total * D * 2 + 6 * n * D * D + (2 * n * (D * D + 2 * D * FF) if below else 0)
    return mega(kernel, "layer_back" if below else "layer_back_first", ins, outs, scratch, flops, hbm=hbm, after=after)


def feed_pieces(place, packs, near, side, cross, after=()):
    n = near[0].shape[0]
    here, there = packs
    ins = Names(
        place=place, here=[a for a, _ in here], att=[a for a, _, _, _ in there], act=[a for _, _, a, _ in there],
        near=list(near), side=list(side), cross=list(cross),
    )
    io, u = sds((4, WIDTH, IO), BF), sds((4, WIDTH, 2 * ACTIVE), BF)
    scratch = Names(
        t_hidden=pltpu.VMEM((D, 4 * n), BF), t_attn=pltpu.VMEM((D, 4 * n), BF), t_outer=pltpu.VMEM((2, CHUNK, 4 * n), BF),
    )

    def kernel(r):
        hidden = [(ref, at) for ref, (_, at) in zip(r.here, here)] + [(ref, at) for ref, (_, at, _, _) in zip(r.att, there)]
        turned(r.t_hidden, *[ref[:, at : at + D] for ref, at in hidden])
        turned(r.t_attn, *[ref[:, at + D : at + 2 * D] for ref, at in hidden])
        n0, n1 = r.near
        y0, y1 = r.side
        x0, x1 = r.cross
        inner = jnp.concatenate([n0[:, :FB], n1[:, :FB], y0[:, :FB], y1[:, FB : 2 * FB]], axis=0)
        out = jnp.concatenate(
            [n0[:, NEAR_OUT:NEAR], n1[:, NEAR_OUT:NEAR], y0[:, SIDE_OUT : SIDE_OUT + CHUNK], y1[:, SIDE_OUT + CHUNK : SIDE]], axis=0
        )
        x, y = r.place[0], r.place[1]
        for name, side_x in (("io_send", 1 - x), ("io_keep", x)):
            r[name][:, :, :FB] = dot(shard_rows(r.t_hidden, side_x), inner).astype(BF).reshape(4, WIDTH, FB)
            r[name][:, :, FB:] = dot(shard_rows(r.t_attn, side_x), out).astype(BF).reshape(4, WIDTH, CHUNK)
        sources = [(n0, NEAR_OUTER), (n1, NEAR_OUTER), (x0, 0), (x1, 2 * CHUNK)]
        for h in range(2):
            turned(r.t_outer.at[h], *[ref[:, at + h * CHUNK : at + (h + 1) * CHUNK] for ref, at in sources])
        active = [ref[:, at + 2 * D : at + PACK] for ref, (_, at) in zip(r.here, here)]
        active += [ref[:, at : at + FF // 2] for ref, (_, _, _, at) in zip(r.act, there)]
        active = jnp.concatenate(active, axis=0)
        for name, side_y in (("u_send", 1 - y), ("u_keep", y)):
            t = dot(r.t_outer[side_y], active).astype(BF)
            for z in range(4):
                part = t[:, z * ACTIVE : (z + 1) * ACTIVE]
                r[name][z, :, :ACTIVE] = part[:WIDTH]
                r[name][z, :, ACTIVE:] = part[WIDTH:]

    outs = Names(io_keep=io, io_send=io, u_keep=u, u_send=u)
    return mega(kernel, "feed_pieces", ins, outs, scratch, 8 * n * (D * IO + FF * CHUNK), after=after)


def qkv_pieces(place, blocks, near, side, after=()):
    n = near[0].shape[0]
    ins = Names(place=place, blocks=[blocks[b] for b in (0, 4, 2, 6)], near=list(near), side=list(side))
    o = sds((4, WIDTH, QKV), BF)

    def kernel(r):
        turned(r.t_rows, *[ref[...] for ref in r.blocks])
        (g0, g1), (y0, y1) = r.near, r.side
        g = jnp.concatenate([g0[...], g1[...], y0[:, :QKV], y1[:, QKV:]], axis=0)
        x = r.place[0]
        for name, side_x in (("send", 1 - x), ("keep", x)):
            r[name][...] = dot(shard_rows(r.t_rows, side_x), g).astype(BF).reshape(4, WIDTH, QKV)

    return mega(
        kernel, "qkv_pieces", ins, Names(keep=o, send=o), Names(t_rows=pltpu.VMEM((D, 4 * n), BF)), 8 * n * D * QKV, after=after
    )


def padded(w):
    return -(-w // LANES) * LANES


def first_sum(place, pairs, after=()):
    width = sum(padded(a.shape[2]) for a, _ in pairs)
    o = sds((2, WIDTH, width), BF)

    def kernel(r):
        bit = r.place[3] % 2
        for name, side in (("keep", bit), ("send", 1 - bit)):
            for i in range(2):
                at = 0
                for a, b in zip(r.own, r.got):
                    w = a.shape[2]
                    r[name][i, :, at : at + w] = (a[2 * i + side].astype(F32) + b[2 * i + side].astype(F32)).astype(BF)
                    at += padded(w)

    ins = Names(place=place, own=[a for a, _ in pairs], got=[b for _, b in pairs])
    return mega(kernel, "first_sum", ins, Names(keep=o, send=o), {}, 1000, after=after)


def second_sum(place, keep, got, after=()):
    o = sds(keep.shape[1:], BF)

    def kernel(r):
        bit = r.place[3] // 2
        for name, side in (("keep", bit), ("send", 1 - bit)):
            r[name][...] = (r.own[side].astype(F32) + r.got[side].astype(F32)).astype(BF)

    return mega(kernel, "second_sum", Names(place=place, own=keep, got=got), Names(keep=o, send=o), {}, 1000, after=after)


FEED_SHAPES = Names(inner=(WIDTH, FB), out=(WIDTH, CHUNK), outer=(CHUNK, ACTIVE))
QKV_SHAPES = Names(query=(WIDTH, CHUNK), key=(WIDTH, CHUNK), value=(WIDTH, CHUNK))


def last_sum(feed, layers):
    shapes = FEED_SHAPES if feed else QKV_SHAPES
    outs = Names((k, sds((LAYERS,) + v, F32)) for k, v in shapes.items())

    def kernel(r):
        for layer, (a, b) in enumerate(zip(r.own, r.got)):
            total = a[...].astype(F32) + b[...].astype(F32)
            if not feed:
                for i, name in enumerate(shapes):
                    r[name][layer] = total[:, i * CHUNK : (i + 1) * CHUNK]
                continue
            r.inner[layer] = total[:, :FB]
            r.out[layer] = total[:, FB:IO]
            r.outer[layer, :WIDTH] = total[:, IO_PAD : IO_PAD + ACTIVE]
            r.outer[layer, WIDTH:] = total[:, IO_PAD + ACTIVE :]

    return mega(kernel, "last_sum", Names(own=[a for a, _ in layers], got=[b for _, b in layers]), outs, {}, 1000)


def linear(z, x, y, c):
    return (z * 2 + x) * 4 + y * 2 + c


PLACES = [(z, x, y, c) for z in range(4) for x in range(2) for y in range(2) for c in range(2)]


def move(array, where):
    pairs = [(linear(*place), linear(*where(*place))) for place in PLACES]
    return lax.ppermute(array, BOTH, pairs)


def to_plane(z, x, y, c):
    return (2 * y + c, x, z >> 1, z & 1)


def other_core(z, x, y, c):
    return (z, x, y, 1 - c)


def other_x(z, x, y, c):
    return (z, 1 - x, y, c)


def other_y(z, x, y, c):
    return (z, x, 1 - y, c)


def other_xy(z, x, y, c):
    return (z, 1 - x, 1 - y, c)


def near_z(z, x, y, c):
    return (z ^ 1, x, y, c)


def far_z(z, x, y, c):
    return (z ^ 2, x, y, c)


def gate(arrays, *others):
    return lax.optimization_barrier((arrays, others))[0]


def pick(array, index, axis):
    return lax.dynamic_index_in_dim(array, index, axis, keepdims=False)


class Small:
    def __init__(self):
        seq, rows = lax.axis_index("seq"), lax.axis_index("rows")
        self.z, self.x, self.y, self.c = seq // 2, seq % 2, rows // 2, rows % 2
        self.spot = jnp.stack([self.x, self.y, self.c, self.z]).astype(jnp.int32)

    def starts(self, count):
        out = []
        for dc in (0, 1):
            for dx, dy in ((0, 0), (1, 0), (0, 1), (1, 1)):
                x, y, c = self.x ^ dx, self.y ^ dy, self.c ^ dc
                out.append(((2 * y + c) * 2 + x) * count)
        return jnp.stack(out)

    def reach(self, array):
        return [array, move(array, other_x), move(array, other_y), move(array, other_xy)]

    def share(self, mine):
        return mine + [move(a, other_core) for a in mine]


class Large:
    def __init__(self):
        self.shards = lax.axis_size("seq")
        self.spot = jnp.zeros((4,), jnp.int32)

    def starts(self, count):
        me = lax.axis_index("seq")
        return (me + jnp.arange(self.shards, dtype=jnp.int32)) % self.shards * count

    def gather(self, array):
        whole_row = lax.all_gather(array, "seq", axis=0, tiled=True)
        return [jnp.roll(whole_row, -lax.axis_index("seq") * array.shape[0], axis=0)]

    def spread(self, left, right):
        grad = lax.dot_general(left, right, (((0,), (0,)), ((), ())), preferred_element_type=F32).astype(BF)
        grad = lax.psum_scatter(grad, "seq", scatter_dimension=0, tiled=True)
        return lax.psum_scatter(grad, "rows", scatter_dimension=1, tiled=True).astype(F32)

    def grads(self, kept, back, tail, dq):
        near, send, to_x, to_y = back.near, back.send, back.to_x, back.to_y
        inner = cat(near[:, :FB], send[:, :FB], to_y[:, : 2 * FB])
        out = cat(near[:, NEAR_OUT:NEAR], send[:, NEAR_OUT:NEAR], to_y[:, SIDE_OUT:SIDE])
        outer = cat(*[to_x[:, i * CHUNK : (i + 1) * CHUNK] for i in (0, 2, 1, 3)])
        if "active" in kept:
            hidden, attn = kept.side[:, :D], kept.side[:, D:]
            mine, other = kept.keep_pack[:, 2 * D :], kept.active
        else:
            hidden, attn = to_y[:, SIDE : SIDE + D], to_y[:, SIDE + D :]
            mine, other = near[:, NEAR_PACK + 2 * D :], to_x[:, D:]
        active = jnp.stack([v.reshape(-1, 4, ACTIVE) for v in (mine, other)], axis=2).reshape(-1, FF)
        own = kept.blocks[0][: dq.shape[0]]
        return Names(
            inner=self.spread(hidden, inner), out=self.spread(attn, out), outer=self.spread(active, outer),
            query=self.spread(own, dq), key=self.spread(own, tail.dk), value=self.spread(own, tail.dv),
        )


def doc_layout(lengths_row, index):
    ends = jnp.cumsum(lengths_row, dtype=jnp.int32)
    passed = (index[:, None] >= ends[None, :]).astype(jnp.int32)
    segment = jnp.sum(passed, axis=1, dtype=jnp.int32)
    begin = jnp.sum(passed * lengths_row[None, :], axis=1, dtype=jnp.int32)
    return (segment, (index - begin).astype(jnp.int32))


def rotary_tables(position):
    lane = jnp.arange(LANES, dtype=jnp.int32)
    pairs = (lane % HEAD_DIM // 2).astype(F32)
    inverse = jnp.power(jnp.float32(10000.0), -2.0 * pairs / HEAD_DIM)
    angle = position.astype(F32)[:, None] * inverse[None, :]
    return jnp.cos(angle), jnp.sin(angle) * jnp.where(lane % 2 == 0, -1.0, 1.0)[None, :]


def both_cores(array):
    return array, move(array, other_core)


def all_sums(two, tail_two, one, tail_one):
    return jnp.concatenate([one.sums[:10], tail_one.qkv_sums[:3], two.sums[:10], tail_two.qkv_sums[:3]], axis=0)


VECTOR_ROWS = Names(g2=0, c2=1, bu=2, g1=3, c1=4, bo=5, bq=10, bk=11, bv=12)
LAYER_ROWS = 13


def last_vectors(place, own, got):
    outs = Names((name, sds((LAYERS, WIDTH), F32)) for name in VECTOR_ROWS)
    outs.bi = sds((LAYERS, ACTIVE), F32)

    def kernel(r):
        x, z = r.place[0], r.place[3]
        total = r.own[...] + r.got[...]
        r.s_total[...] = total
        shard = 2 * z + x
        turn = pltpu.roll(total, (D - shard * WIDTH) % D, 1)[:, :WIDTH]
        for layer in range(LAYERS):
            for name, row in VECTOR_ROWS.items():
                at = LAYER_ROWS * layer + row
                r[name][layer : layer + 1, :] = turn[at : at + 1]
            row = r.s_total[pl.ds(LAYER_ROWS * layer + 6 + z, 1), :]
            r.bi[layer : layer + 1, :] = jnp.where(x == 0, row[:, :ACTIVE], row[:, ACTIVE:])

    scratch = Names(s_total=pltpu.VMEM(own.shape, F32))
    return mega(kernel, "last_vectors", Names(place=place, own=own, got=got), outs, scratch, 1000)


class Program:
    def __init__(self, place, spot, lengths_row, n, starts, params):
        wq, bq, wk, bk, wv, bv, wo, bo, g1, c1, wi, bi, wu, bu, g2, c2 = params
        self.weights = Names(wq=wq, wk=wk, wv=wv, wo=wo, wi=wi, wu=wu)
        self.spot, self.n = spot, n
        self.vec = jnp.stack([bq, bk, bv, bo, g1, c1, bu, g2, c2], axis=1).astype(F32)
        self.bi = bi.astype(F32)[:, None, :]
        index = (starts[:, None] + jnp.arange(n, dtype=jnp.int32)).reshape(-1)
        segment, position = doc_layout(lengths_row, index)
        self.segments = segment[:n, None], segment[None, :]
        self.cos, self.sin = rotary_tables(position)
        self.own_cos, self.own_sin = rotary_tables(position[:n])

    def project(self, layer, rows):
        w = self.weights
        return project(rows, layer, w["wq"], w["wk"], w["wv"], self.vec, self.cos, self.sin)

    def forward(self, layer, x, blocks, qkv=None, cotangent=None, after=()):
        kept = layer_forward(
            layer, self.spot, x, blocks, self.weights, self.bi, self.vec, self.cos, self.sin, *self.segments, qkv, cotangent, after
        )
        kept.blocks = blocks
        if qkv:
            kept.update(zip("qkv", qkv), own_k=qkv[1][: self.n], own_v=qkv[2][: self.n])
        return kept

    def queries(self, kept, back, after=()):
        return query_back(
            kept.q, kept.k, kept.v, back.pack, kept.lse, back.delta, *self.segments, self.own_cos, self.own_sin, after
        )[0]

    def back(self, layer, kept, back, dq, packs, below=None, after=()):
        return layer_back(
            layer, self.spot, kept, back, dq, packs, self.weights, self.vec, self.own_cos, self.own_sin, *self.segments, below, after
        )


def large_body(tokens, lengths, cotangent, *params):
    place = Large()
    n = tokens.shape[1]
    run = Program(place, place.spot, lengths[0], n, place.starts(n), params)

    def step(layer, x, x_b, cotangent=None):
        blocks = place.gather(x_b)
        return run.forward(layer, x, blocks, run.project(layer, blocks[0]), cotangent)

    first = step(0, tokens[0], tokens[0])
    second = step(1, first.result, first.result_b, cotangent[0])
    dq_two = run.queries(second, second)
    back_one = run.back(1, second, second, dq_two, place.gather(second.pack), first)
    dq_one = run.queries(first, back_one)
    back_none = run.back(0, first, back_one, dq_one, place.gather(back_one.pack))
    grads_one = place.grads(first, back_one, back_none, dq_one)
    grads_two = place.grads(second, second, back_one, dq_two)
    m = Names((name, jnp.stack([grads_one[name], grads_two[name]])) for name in grads_one)
    total = lax.psum(all_sums(second, back_one, back_one, back_none), BOTH).reshape(LAYERS, LAYER_ROWS, D)
    me, shards = lax.axis_index("seq"), lax.axis_size("seq")
    v = Names(
        (name, lax.dynamic_slice_in_dim(total[:, row], me * (D // shards), D // shards, 1))
        for name, row in VECTOR_ROWS.items()
    )
    v.bi = lax.dynamic_slice_in_dim(total[:, 6:10].reshape(LAYERS, FF), me * (FF // shards), FF // shards, 1)
    return result(second.result_b, back_none.grad, m, v)


def small_body(tokens, lengths, cotangent, *params):
    place = Small()
    spot, n = place.spot, tokens.shape[1]
    current = move(tokens[0], to_plane)
    run = Program(place, spot, move(lengths, to_plane)[0], n, place.starts(n), params)
    blocks = place.share(place.reach(current))
    grad = move(gate(cotangent[0], current), to_plane)
    first = run.forward(0, current, blocks, after=(grad,))
    a_near = both_cores(first.keep_pack)
    blocks = place.share(place.reach(first.result_b))
    second = run.forward(1, first.result, blocks, cotangent=grad, after=(a_near[1],))

    packs = place.reach(second.pack)
    dq_two = run.queries(second, second)
    packs = place.share(gate(packs, dq_two))
    names = "to_y", "to_x", "send"
    to_y, to_x, send, side, active = gate([second[k] for k in names] + [first[k] for k in ("side", "active")], packs)
    from_y, from_x, near = move(to_y, other_y), move(to_x, other_x), (second.near, move(send, other_core))
    a_side, a_cross = move(side, other_y), move(active, other_x)
    back_one = run.back(1, second, second, dq_two, packs, first)

    packs = place.reach(gate(back_one.pack, from_y, from_x, a_side, a_cross, near[1]))
    side, cross = [both_cores(gate(a, back_one.pack)) for a in (from_y, from_x)]
    dq_one = run.queries(first, back_one)
    packs = place.share(gate(packs, dq_one))
    to_y, to_x, send, result_b, a_side, a_cross = gate([back_one[k] for k in names] + [second.result_b, a_side, a_cross], packs)
    from_y, from_x = move(to_y, other_y), move(to_x, other_x)
    there = [(a, SIDE, b, D) for a, b in zip(side, cross)]
    two = feed_pieces(spot, ([(a, NEAR_PACK) for a in near], there), near, side, cross, after=(dq_one, *packs))
    near, a_side, a_cross = (back_one.near, move(send, other_core)), both_cores(a_side), both_cores(a_cross)
    two_io, two_u = move(two.io_send, other_x), move(two.u_send, other_y)
    output = move(result_b, to_plane)
    back_none = run.back(0, first, back_one, dq_one, packs, after=(two.io_send, near[1], a_side[1], a_cross[1]))

    done = back_none.grad
    tokens_grad = move(done, to_plane)
    sums = all_sums(second, back_one, back_one, back_none)
    sums = sums + move(sums, other_core)
    two_sum = first_sum(spot, ((two.io_keep, two_io), (two.u_keep, two_u)), after=(done, output))
    two_near = move(two_sum.send, near_z)
    side, cross = [both_cores(gate(a, done)) for a in (from_y, from_x)]
    there = [(a, 0, b, 0) for a, b in zip(a_side, a_cross)]
    q_side, q_near = move(back_one.qkv_y, other_y), (back_one.qkv_near, move(back_one.qkv_send, other_core))
    q_side_one, q_near_one = move(back_none.qkv_y, other_y), (back_none.qkv_near, move(back_none.qkv_send, other_core))
    one = feed_pieces(spot, ([(a, 0) for a in a_near], there), near, side, cross, after=(two_sum.send,))
    done = one.io_send
    one_io, one_u = move(one.io_send, other_x), move(one.u_send, other_y)
    sums = sums + move(gate(sums, done), other_x)
    two_qkv = qkv_pieces(spot, second.blocks, q_near, both_cores(q_side), after=(done, tokens_grad))
    two_q = move(two_qkv.send, other_x)
    one_qkv = qkv_pieces(spot, first.blocks, q_near_one, both_cores(q_side_one), after=(two_qkv.send,))
    one_q = move(one_qkv.send, other_x)
    one_sum = first_sum(spot, ((one.io_keep, one_io), (one.u_keep, one_u)), after=(one_qkv.send,))
    one_near = move(one_sum.send, near_z)
    two_z = second_sum(spot, two_sum.keep, two_near, after=(one_sum.send,))
    two_far = move(two_z.send, far_z)
    two_qs = first_sum(spot, ((two_qkv.keep, two_q),), after=(two_z.send,))
    two_q_near = move(two_qs.send, near_z)
    one_qs = first_sum(spot, ((one_qkv.keep, one_q),), after=(two_qs.send,))
    one_q_near = move(one_qs.send, near_z)
    one_z = second_sum(spot, one_sum.keep, one_near, after=(one_qs.send,))
    one_far = move(one_z.send, far_z)
    two_qz = second_sum(spot, two_qs.keep, two_q_near, after=(one_z.send,))
    two_q_far = move(two_qz.send, far_z)
    one_qz = second_sum(spot, one_qs.keep, one_q_near, after=(two_qz.send,))
    one_q_far = move(one_qz.send, far_z)
    sums = sums + move(sums, other_y)
    sums = sums + move(sums, near_z)
    v = last_vectors(spot, sums, move(sums, far_z))
    m = last_sum(True, ((one_z.keep, one_far), (two_z.keep, two_far)))
    m.outer = m.outer.swapaxes(1, 2)
    m.update(last_sum(False, ((one_qz.keep, one_q_far), (two_qz.keep, two_q_far))))
    return result(output, tokens_grad, m, v)


def result(output, tokens_grad, m, v):
    return (
        output[None], tokens_grad[None],
        m.query, v.bq, m.key, v.bk, m.value, v.bv, m.out, v.bo, v.g1, v.c1,
        m.inner, v.bi, m.outer, v.bu, v.g2, v.c2,
    )


def solution(mesh):
    token = P("rows", "seq", None)
    mat, vec = P(None, "seq", "rows"), P(None, "seq")
    small = (mesh.shape["seq"], mesh.shape["rows"]) == (8, 4)
    return jax.shard_map(
        small_body if small else large_body,
        mesh=mesh,
        in_specs=(token, P("rows", None), token) + (P(),) * 16,
        out_specs=(token, token, mat, vec, mat, vec, mat, vec, mat, vec, vec, vec, mat, vec, mat, vec, vec, vec),
        check_vma=False,
    )
```

```python
import jax
import jax.numpy as jnp
from jax import lax
from jax.experimental import pallas as pl
from jax.experimental.pallas import tpu as pltpu
from jax.sharding import PartitionSpec as P

D = 768
HEADS = 12
HEAD_DIM = 64
FF = 3072
LAYERS = 2
LANES = 128
PAIRS = D // LANES
CHUNK = D // 4
NEG_FILL = -1e30
NORM_EPS = 1e-12
SCALE = HEAD_DIM**-0.5
BF = jnp.bfloat16
F32 = jnp.float32
BOTH = ("seq", "rows")
MIB = 1 << 20

BQ, BK, BV, BO, G1, C1, BU, G2, C2 = range(9)
FB = 768
WIDTH = D // 8
ACTIVE = FF // 8
QKV = 3 * CHUNK
IO = FB + CHUNK
IO_PAD = FB + 2 * LANES

NEAR_OUTER, NEAR_OUT, NEAR = FB, FB + 2 * CHUNK, FB + 3 * CHUNK
NEAR_PACK = NEAR + 64
SIDE_OUT, SIDE = 2 * FB, 2 * FB + 2 * CHUNK
PACK = 2 * D + FF // 2

LSE_HI, LSE_LO, DELTA_HI, DELTA_LO = 0, 16, 32, 48


class Names(dict):
    __getattr__ = dict.__getitem__
    __setattr__ = dict.__setitem__


def dot(a, b):
    return jnp.dot(a, b, preferred_element_type=F32)


def dot_nt(a, b):
    return lax.dot_general(a, b, (((1,), (1,)), ((), ())), preferred_element_type=F32)


def call(kernel, name, grid, in_specs, out_specs, out_shape, args, flops, scratch=(), scalars=(), vmem=60, after=(), aliases=None):
    size = sum(a.size * a.dtype.itemsize for a in args) + sum(
        s.size * s.dtype.itemsize for s in jax.tree.leaves(out_shape)
    )
    lead, many = len(scalars) + len(args), len(after)

    def run(*refs):
        kernel(*refs[:lead], *refs[lead + many :])

    return pl.pallas_call(
        run,
        name=name,
        grid_spec=pltpu.PrefetchScalarGridSpec(
            num_scalar_prefetch=len(scalars),
            grid=grid,
            in_specs=list(in_specs) + [pl.BlockSpec(memory_space=pl.ANY)] * many,
            out_specs=out_specs,
            scratch_shapes=list(scratch),
        ),
        out_shape=out_shape,
        input_output_aliases=aliases or {},
        compiler_params=pltpu.CompilerParams(
            dimension_semantics=("arbitrary",) * len(grid), vmem_limit_bytes=vmem * MIB
        ),
        cost_estimate=pl.CostEstimate(flops=int(flops), bytes_accessed=int(size), transcendentals=0),
    )(*scalars, *args, *after)


def whole(array):
    return pl.BlockSpec(array.shape, lambda *_: (0,) * array.ndim)


def layer_block(array, layer):
    return pl.BlockSpec((None,) + array.shape[1:], lambda *_: (layer,) + (0,) * (array.ndim - 1))


def sds(shape, dtype):
    return jax.ShapeDtypeStruct(shape, dtype)


def lane_is_even(shape):
    return lax.broadcasted_iota(jnp.int32, shape, 1) % 2 == 0


def swap_pairs(v):
    return jnp.where(lane_is_even(v.shape), pltpu.roll(v, LANES - 1, 1), pltpu.roll(v, 1, 1))


def lanes(j):
    return slice(j * LANES, (j + 1) * LANES)


def qkv_kernel(x_ref, wq_ref, wk_ref, wv_ref, vec_ref, cos_ref, sin_ref, q_ref, k_ref, v_ref):
    x, cos, sin = x_ref[...], cos_ref[...], sin_ref[...]
    for w_ref, row, o_ref in ((wq_ref, BQ, q_ref), (wk_ref, BK, k_ref)):
        y = dot(x, w_ref[...]) + vec_ref[row : row + 1, :]
        for j in range(PAIRS):
            t = y[:, lanes(j)]
            o_ref[:, lanes(j)] = (t * cos + swap_pairs(t) * sin).astype(BF)
    v_ref[...] = (dot(x, wv_ref[...]) + vec_ref[BV : BV + 1, :]).astype(BF)


def project(rows, layer, wq, wk, wv, vec, cos, sin):
    total = rows.shape[0]
    block = min(256, total)
    tok = lambda w: pl.BlockSpec((block, w), lambda i: (i, 0))
    return call(
        qkv_kernel, "qkv", (total // block,),
        [tok(D)] + [layer_block(w, layer) for w in (wq, wk, wv, vec)] + [tok(LANES), tok(LANES)],
        [tok(D)] * 3, [sds((total, D), BF)] * 3,
        (rows, wq, wk, wv, vec, cos, sin), 6 * total * D * D,
    )


def over_chunks(total, body, carry):
    size = min(total, 1024)
    if size == total:
        return body(slice(None), carry)
    return lax.fori_loop(
        0, total // size, lambda i, c: body(pl.ds(pl.multiple_of(i * size, size), size), c), carry
    )


def two_heads(v):
    low = lax.broadcasted_iota(jnp.int32, v.shape, 1) < HEAD_DIM
    zero = jnp.zeros_like(v)
    return jnp.concatenate([jnp.where(low, v, zero), jnp.where(low, zero, v)], axis=0)


def join_heads(v):
    n = v.shape[0] // 2
    low = lax.broadcasted_iota(jnp.int32, (n, LANES), 1) < HEAD_DIM
    return jnp.where(low, v[:n], v[n:])


def normalize(values):
    centered = values - jnp.mean(values, axis=-1, keepdims=True)
    rstd = lax.rsqrt(jnp.mean(centered * centered, axis=-1, keepdims=True) + NORM_EPS)
    return centered * rstd, rstd


def column_sum(v):
    return jnp.sum(v.astype(F32), axis=0, keepdims=True)


def norm_back(grad, normed, rstd, gain):
    scaled = grad * gain
    centered = scaled - jnp.mean(scaled, axis=-1, keepdims=True)
    return rstd * (centered - normed * jnp.mean(scaled * normed, axis=-1, keepdims=True))


def either(first, a, b):
    return jnp.where(first, a, b), jnp.where(first, b, a)


def cat(*parts):
    return jnp.concatenate(parts, axis=1)


def quarters(v, y, c):
    part = [v[:, k * CHUNK : (k + 1) * CHUNK] for k in range(4)]
    mine0, theirs0 = either(c == 0, part[0], part[1])
    mine1, theirs1 = either(c == 0, part[2], part[3])
    mine, mine_y = either(y == 0, mine0, mine1)
    theirs, theirs_y = either(y == 0, theirs0, theirs1)
    return mine, theirs, mine_y, theirs_y


def hi_lo(v):
    hi = v.astype(BF)
    return hi, (v - hi.astype(F32)).astype(BF)


def unrotate(v, cos, sin):
    t = v * sin
    return v * cos + swap_pairs(t)


def lane_of(v, lane):
    at = lax.broadcasted_iota(jnp.int32, v.shape, 1)
    return jnp.sum(jnp.where(at == lane, v, 0.0), axis=1, keepdims=True)


def query_back_kernel(
    q_ref, k_ref, v_ref, g_ref, lse_ref, delta_ref, own_ref, all_ref, cos_ref, sin_ref,
    dq_ref, sum_ref,
):
    pair = pl.program_id(0)
    n, total = q_ref.shape[0], k_ref.shape[0]
    q = two_heads(q_ref[...] * jnp.asarray(SCALE, BF))
    g = two_heads(g_ref[...])
    own = own_ref[...]
    lse = jnp.concatenate([lane_of(lse_ref[...], 2 * pair), lane_of(lse_ref[...], 2 * pair + 1)], axis=0)
    delta = jnp.concatenate([lane_of(delta_ref[...], 2 * pair), lane_of(delta_ref[...], 2 * pair + 1)], axis=0)

    def body(at, acc):
        same = own == all_ref[:, at]
        k = k_ref[at, :]
        s = jnp.where(jnp.concatenate([same, same], axis=0), dot_nt(q, k) - lse, NEG_FILL)
        ds = (jnp.exp(s) * (dot_nt(g, v_ref[at, :]) - delta)).astype(BF)
        return acc + dot(ds, k)

    acc = join_heads(over_chunks(total, body, jnp.zeros((2 * n, LANES), F32))) * SCALE
    dq = unrotate(acc, cos_ref[...], sin_ref[...]).astype(BF)
    dq_ref[...] = dq
    sum_ref[...] = column_sum(dq)


def query_back(q, k, v, pack, lse, delta, own_seg, all_seg, cos, sin, after=()):
    n, total = pack.shape[0], k.shape[0]
    own = pl.BlockSpec((n, LANES), lambda p: (0, p))
    row = pl.BlockSpec((total, LANES), lambda p: (0, p))
    fixed = lambda w: pl.BlockSpec((n, w), lambda p: (0, 0))
    return call(
        query_back_kernel, "query_back", (PAIRS,),
        [own, row, row, own, fixed(LANES), fixed(LANES), whole(own_seg), whole(all_seg), fixed(LANES), fixed(LANES)],
        [own, pl.BlockSpec((1, LANES), lambda p: (0, p))],
        [sds((n, D), BF), sds((1, D), F32)],
        (q, k, v, pack, lse, delta, own_seg, all_seg, cos, sin), 6 * n * total * D * 2, after=after,
    )


def turned(ref, *parts):
    n = parts[0].shape[0]
    for i, part in enumerate(parts):
        ref[:, i * n : (i + 1) * n] = part.T


def shard_rows(ref, x):
    width = WIDTH
    return jnp.concatenate(
        [ref[pl.ds(pl.multiple_of((2 * z + x) * width, 32), width), :] for z in range(4)], axis=0
    )


def mega(kernel, name, ins, outs, scratch, flops, hbm=(), after=(), vmem=60):
    flat_in, tree_in = jax.tree.flatten(dict(ins))
    flat_out, tree_out = jax.tree.flatten(dict(outs))

    def spec_of(key):
        space = pl.ANY if key in hbm else pltpu.SMEM if key == "place" else pltpu.VMEM
        return pl.BlockSpec(memory_space=space)

    specs_in = jax.tree.leaves({k: jax.tree.map(lambda _: spec_of(k), v) for k, v in ins.items()})
    specs_out = jax.tree.leaves({k: jax.tree.map(lambda _: spec_of(k), v) for k, v in outs.items()})
    many_in, many_out = len(flat_in), len(flat_out)

    def run(*refs):
        lead = many_in + len(after)
        named = Names(tree_in.unflatten(refs[:many_in]))
        named.update(tree_out.unflatten(refs[lead : lead + many_out]))
        named.update(zip(scratch, refs[lead + many_out :]))
        kernel(named)

    size = sum(a.size * a.dtype.itemsize for a in flat_out) + sum(
        a.size * a.dtype.itemsize for k, v in ins.items() if k not in hbm for a in jax.tree.leaves(v)
    )
    out = pl.pallas_call(
        run,
        name=name,
        in_specs=specs_in + [pl.BlockSpec(memory_space=pl.ANY)] * len(after),
        out_specs=specs_out,
        out_shape=flat_out,
        scratch_shapes=list(scratch.values()),
        compiler_params=pltpu.CompilerParams(vmem_limit_bytes=vmem * MIB),
        cost_estimate=pl.CostEstimate(flops=int(flops), bytes_accessed=int(size), transcendentals=0),
    )(*flat_in, *after)
    return Names(tree_out.unflatten(out))


SHAPES = Names(wq=(D, D), wk=(D, D), wv=(D, D), wo=(D, D), wi=(D, FF), wu=(FF, D))


def rooms(names):
    found = Names(("m_" + name, pltpu.VMEM(SHAPES[name], BF)) for name in names)
    found.sems = pltpu.SemaphoreType.DMA((16,))
    return found


def units(j):
    return pl.ds(j * FB, FB)


class Copies:
    def __init__(self, sems):
        self.sems, self.copies = sems, {}

    def start(self, name, src, dst):
        self.copies[name] = pltpu.make_async_copy(src, dst, self.sems.at[len(self.copies)])
        self.copies[name].start()

    def weights(self, r, layer, names):
        for name in names:
            src, dst = r["w_" + name].at[layer], r["m_" + name]
            if name not in ("wi", "wu"):
                self.start(name, src, dst)
                continue
            for j in range(FF // FB):
                at = (slice(None), units(j)) if name == "wi" else (units(j), slice(None))
                self.start(f"{name}{j}", src.at[at], dst.at[at])

    def wait(self, *names):
        for name in names:
            if name in self.copies:
                self.copies.pop(name).wait()


def join(dst, refs, columns):
    at = 0
    for ref in refs:
        dst[at : at + ref.shape[0], :] = ref[:, columns]
        at += ref.shape[0]


def row_of(r, index):
    return r.vec[index : index + 1, :]


def qkv_phase(r, copies):
    rows, cos, sin = r.s_rows, r.cos, r.sin
    total = rows.shape[0]
    block = min(256, total)
    for name, bias in (("k", BK), ("v", BV), ("q", BQ)):
        copies.wait("w" + name)
        for i in range(total // block):
            at = pl.ds(i * block, block)
            y = dot(rows[at, :], r["m_w" + name][...]) + row_of(r, bias)
            if name == "v":
                r.s_v[at, :] = y.astype(BF)
                continue
            for j in range(PAIRS):
                t = y[:, lanes(j)]
                r["s_" + name][at, lanes(j)] = (t * cos[at, :] + swap_pairs(t) * sin[at, :]).astype(BF)


def attend_phase(r):
    n, total = r.attn.shape[0], r.s_k.shape[0]
    own = r.own[...]
    lane = lax.broadcasted_iota(jnp.int32, (n, LANES), 1)
    lse = jnp.zeros((n, LANES), F32)
    for p in range(PAIRS):
        q = two_heads(r.s_q[:n, lanes(p)] * jnp.asarray(SCALE, BF))

        def body(at, carry):
            top, tot, acc = carry
            same = own == r.all[:, at]
            s = dot_nt(q, r.s_k[at, lanes(p)])
            s = jnp.where(jnp.concatenate([same, same], axis=0), s, NEG_FILL)
            fresh = jnp.maximum(top, jnp.max(s, axis=1, keepdims=True))
            e = jnp.exp(s - fresh)
            keep = jnp.exp(top - fresh)
            tot = tot * keep + jnp.sum(e, axis=1, keepdims=True)
            acc = acc * keep + dot(e.astype(BF), r.s_v[at, lanes(p)])
            return fresh, tot, acc

        zero = jnp.zeros((2 * n, 1), F32)
        top, tot, acc = over_chunks(total, body, (zero + NEG_FILL, zero, jnp.zeros((2 * n, LANES), F32)))
        r.attn[:, lanes(p)] = join_heads(acc / tot)
        part = top + jnp.log(tot)
        lse = jnp.where(lane == 2 * p, part[:n], jnp.where(lane == 2 * p + 1, part[n:], lse))
    r.lse[...] = lse


def ffn_phase(r, copies):
    stat_ref = r.stat
    lane = lax.broadcasted_iota(jnp.int32, stat_ref.shape, 1)
    copies.wait("wo")
    branch = dot(r.attn[...].astype(BF), r.m_wo[...]) + row_of(r, BO)
    n1, r1 = normalize(r.x[...].astype(F32) + branch)
    hidden = n1 * row_of(r, G1) + row_of(r, C1)
    r.n1[...] = n1
    hidden_b = hidden.astype(BF)
    r.s_hidden[...] = hidden_b
    total = hidden + row_of(r, BU)
    for j in range(FF // FB):
        copies.wait(f"wi{j}")
        inner = dot(hidden_b, r.m_wi[:, units(j)]) + r.bi[:, units(j)]
        half = 0.5 + 0.5 * lax.erf(inner * (0.5**0.5))
        active = (inner * half).astype(BF)
        r.slope[:, units(j)] = (half + inner * jnp.exp(-0.5 * inner * inner) * 0.3989422804014327).astype(BF)
        r.s_active[:, units(j)] = active
        copies.wait(f"wu{j}")
        total = total + dot(active, r.m_wu[units(j), :])
    n2, r2 = normalize(total)
    r.n2[...] = n2
    stat_ref[...] = jnp.where(lane == 0, r1, jnp.where(lane == 1, r2, 0.0))
    return n2 * row_of(r, G2) + row_of(r, C2)


def store_active(r, ref, at, x):
    for z in range(4):
        src = pl.ds(pl.multiple_of((2 * z + x) * ACTIVE, LANES), ACTIVE)
        ref[:, at + z * ACTIVE : at + (z + 1) * ACTIVE] = r.s_active[:, src]


def store_pack(r, ref, at, x):
    ref[:, at : at + D] = r.s_hidden[...]
    ref[:, at + D : at + 2 * D] = r.attn[...].astype(BF)
    store_active(r, ref, at + 2 * D, x)


def feed_back_phase(r, copies, grad):
    place = r.place
    y, c = place[1], place[2]
    n2 = r.n2[...]
    sums = r.sums
    sums[0:1, :] = column_sum(grad * n2)
    sums[1:2, :] = column_sum(grad)
    grad = norm_back(grad, n2, r.stat[:, 1:2], row_of(r, G2))
    outer = grad.astype(BF)
    sums[2:3, :] = column_sum(outer)
    mine, theirs, mine_y, theirs_y = quarters(outer, 0, c)
    mine, theirs = cat(mine, mine_y), cat(theirs, theirs_y)
    r.near[:, NEAR_OUTER:NEAR_OUT] = mine
    r.send[:, NEAR_OUTER:NEAR_OUT] = theirs
    r.to_x[:, : 2 * CHUNK] = mine
    r.to_x[:, 2 * CHUNK : D] = theirs
    for j in range(FF // FB):
        copies.wait(f"wu{j}")
        inner = (dot_nt(outer, r.m_wu[units(j), :]) * r.slope[:, units(j)].astype(F32)).astype(BF)
        sums[6 + j : 7 + j, :] = column_sum(inner)
        r.s_inner[:, units(j)] = inner
        copies.wait(f"wi{j}")
        grad = grad + dot_nt(inner, r.m_wi[:, units(j)])
    n1 = r.n1[...]
    sums[3:4, :] = column_sum(grad * n1)
    sums[4:5, :] = column_sum(grad)
    pre_one = norm_back(grad, n1, r.stat[:, 0:1], row_of(r, G1))
    r.pre[...] = pre_one
    branch = pre_one.astype(BF)
    sums[5:6, :] = column_sum(branch)
    sums[10:16, :] = jnp.zeros((6, D), F32)
    mine, theirs, mine_y, theirs_y = quarters(branch, y, c)
    r.near[:, NEAR_OUT:NEAR] = mine
    r.send[:, NEAR_OUT:NEAR] = theirs
    r.to_y[:, SIDE_OUT:SIDE] = cat(mine_y, theirs_y)
    copies.wait("wo")
    attn_grad = dot_nt(branch, r.m_wo[...]).astype(BF)
    r.pack[:, :D] = attn_grad
    feature = lax.broadcasted_iota(jnp.int32, (D, LANES), 0) // HEAD_DIM
    member = (feature == lax.broadcasted_iota(jnp.int32, (D, LANES), 1)).astype(BF)
    hi, lo = hi_lo(attn_grad.astype(F32) * r.attn[...])
    delta = dot(hi, member) + dot(lo, member)
    r.delta[...] = delta
    lse_hi, lse_lo = hi_lo(r.lse[...])
    delta_hi, delta_lo = hi_lo(delta)
    extra = lse_hi.astype(F32)
    for v, at in ((lse_lo, LSE_LO), (delta_hi, DELTA_HI), (delta_lo, DELTA_LO)):
        extra = extra + pltpu.roll(v.astype(F32), at, 1)
    r.pack[:, D:] = extra.astype(BF)
    shard = 2 * y + c
    for ref, at, k in (
        (r.near, 0, shard), (r.send, 0, 2 * y + 1 - c), (r.to_y, 0, 2 - 2 * y + c), (r.to_y, FB, 3 - 2 * y - c),
    ):
        ref[:, at : at + FB] = r.s_inner[:, pl.ds(pl.multiple_of(k * FB, LANES), FB)]


def key_back_phase(r, copies):
    place = r.place
    n, total = r.k.shape[0], r.s_g.shape[0]
    row = lax.broadcasted_iota(jnp.int32, (32, LANES), 0)
    lane = lax.broadcasted_iota(jnp.int32, (32, LANES), 1)
    first = jnp.where(row < 16, LSE_HI, DELTA_HI - 16) + row
    pick = ((lane == first) | (lane == first + 16)).astype(BF)
    rows_ref, own = r.s_stats, r.own[...]

    def fill(at, carry):
        rows_ref[:, at] = dot_nt(pick, r.s_extra[at, :])
        return carry

    over_chunks(total, fill, 0)
    for p in range(PAIRS):
        copies.wait(f"q{p}")
        k = two_heads(r.k[:, lanes(p)] * jnp.asarray(SCALE, BF))
        v = two_heads(r.v[:, lanes(p)])

        def body(at, carry):
            dk, dv = carry
            same = own == r.all[:, at]
            q, g = r.s_q[at, lanes(p)], r.s_g[at, lanes(p)]
            s, dp = dot_nt(k, q), dot_nt(v, g)
            probs, ds = [], []
            for h in range(2):
                half = slice(h * n, (h + 1) * n)
                lse, delta = rows_ref[2 * p + h : 2 * p + h + 1, at], rows_ref[16 + 2 * p + h : 17 + 2 * p + h, at]
                prob = jnp.exp(jnp.where(same, s[half] - lse, NEG_FILL))
                probs.append(prob.astype(BF))
                ds.append((prob * (dp[half] - delta)).astype(BF))
            return dk + dot(jnp.concatenate(ds, axis=0), q), dv + dot(jnp.concatenate(probs, axis=0), g)

        zero = jnp.zeros((2 * n, LANES), F32)
        dk, dv = over_chunks(total, body, (zero, zero))
        r.s_dk[:, lanes(p)] = unrotate(join_heads(dk) * SCALE, r.cos[...], r.sin[...]).astype(BF)
        r.s_dv[:, lanes(p)] = join_heads(dv).astype(BF)
    dq, dk, dv = r.dq[...], r.s_dk[...], r.s_dv[...]
    for i, v in enumerate((dq, dk, dv)):
        r.qkv_sums[i : i + 1, :] = column_sum(v)
    r.qkv_sums[3:8, :] = jnp.zeros((5, D), F32)
    mine, theirs, mine_y, theirs_y = zip(*[quarters(v, place[1], place[2]) for v in (dq, dk, dv)])
    for ref, v, above in ((r.qkv_near, mine, "above_near"), (r.qkv_send, theirs, "above_send"), (r.qkv_side, mine_y + theirs_y, "above_side")):
        ref[...] = cat(*v, r[above][...]) if above in r else cat(*v)


def input_back_phase(r, copies):
    total = r.pre_above[...]
    for name, ref in (("wq", r.dq), ("wk", r.s_dk), ("wv", r.s_dv)):
        copies.wait(name)
        total = total + dot_nt(ref[...], r["m_" + name][...])
    return total


def layer_forward(layer, place, x, blocks, weights, bi, vec, cos, sin, own_seg, all_seg, qkv=None, cotangent=None, after=()):
    n = x.shape[0]
    total = all_seg.shape[1]
    last = cotangent is not None
    names = ("wo", "wi", "wu") if qkv else ("wk", "wv", "wq", "wo", "wi", "wu")
    ins = Names(place=place, x=x, own=own_seg, all=all_seg, bi=bi[layer], vec=vec[layer])
    ins.update({"w_" + name: weights[name] for name in names})
    hbm = {"w_" + name for name in names}
    outs = Names(attn=sds((n, D), F32), lse=sds((n, LANES), F32), result_b=sds((n, D), BF))
    scratch = Names(
        s_hidden=pltpu.VMEM((n, D), BF), s_active=pltpu.VMEM((n, FF), BF), **rooms(names),
    )
    inner = Names(
        n1=sds((n, D), F32), n2=sds((n, D), F32), stat=sds((n, LANES), F32), slope=sds((n, FF), BF),
    )
    flops = 2 * n * (D * D + 2 * D * FF) + 4 * n * total * D * 2
    if qkv:
        ins.update(zip(("s_q", "s_k", "s_v"), qkv))
    else:
        ins.update(blocks=blocks, cos=cos, sin=sin)
        for name in "qkv":
            outs[name] = sds((total, D), BF)
            hbm.add(name)
            if name != "q":
                outs["own_" + name] = sds((n, D), BF)
            scratch["s_" + name] = pltpu.VMEM((total, D), BF)
        scratch.s_rows = pltpu.VMEM((total, D), BF)
        scratch.out_sems = pltpu.SemaphoreType.DMA((3,))
        flops += 6 * total * D * D
    if last:
        scratch.update({k: pltpu.VMEM(v.shape, v.dtype) for k, v in inner.items()})
        scratch.s_inner = pltpu.VMEM((n, FF), BF)
        ins.cotangent = cotangent
        outs.update(feed_back_outs(n, True))
        flops += 2 * n * (D * D + 2 * D * FF)
    else:
        outs.update(inner)
        outs.result = sds((n, D), F32)
        outs.update(keep_pack=sds((n, PACK), BF), side=sds((n, 2 * D), BF), active=sds((n, FF // 2), BF))

    def kernel(r):
        copies = Copies(r.sems)
        copies.weights(r, layer, names)
        if not qkv:
            join(r.s_rows, r.blocks, slice(0, D))
            qkv_phase(r, copies)
            back = Copies(r.out_sems)
            for name in "qkv":
                back.start(name, r["s_" + name], r[name])
            for name in "kv":
                r["own_" + name][...] = r["s_" + name][:n, :]
        attend_phase(r)
        result = ffn_phase(r, copies)
        r.result_b[...] = result.astype(BF)
        x = r.place[0]
        if last:
            feed_back_phase(r, copies, r.cotangent[...].astype(F32))
            for ref, at in ((r.near, NEAR_PACK), (r.send, NEAR_PACK)):
                ref[:, NEAR:NEAR_PACK] = jnp.zeros((n, NEAR_PACK - NEAR), BF)
                store_pack(r, ref, at, x)
            r.to_y[:, SIDE : SIDE + D] = r.s_hidden[...]
            r.to_y[:, SIDE + D :] = r.attn[...].astype(BF)
            store_active(r, r.to_x, D, 1 - x)
        else:
            r.result[...] = result
            store_pack(r, r.keep_pack, 0, x)
            r.side[:, :D] = r.s_hidden[...]
            r.side[:, D:] = r.attn[...].astype(BF)
            store_active(r, r.active, 0, 1 - x)
        if not qkv:
            back.wait(*"qkv")

    return mega(kernel, "forward_last" if last else "forward", ins, outs, scratch, flops, hbm=hbm, after=after)


def feed_back_outs(n, last):
    return Names(
        near=sds((n, NEAR_PACK + PACK if last else NEAR), BF), send=sds((n, NEAR_PACK + PACK), BF),
        to_x=sds((n, D + FF // 2 if last else D), BF), to_y=sds((n, SIDE + 2 * D if last else SIDE), BF),
        pre=sds((n, D), F32), pack=sds((n, D + LANES), BF), delta=sds((n, LANES), F32),
        sums=sds((16, D), F32),
    )


def layer_back(layer, place, kept, back, dq, blocks, weights, vec, cos, sin, own_seg, all_seg, below=None, far=(), after=()):
    n, total = dq.shape[0], all_seg.shape[1]
    names = ("wq", "wk", "wv") + (("wo", "wi", "wu") if below else ())
    ins = Names(
        place=place, k=kept.own_k, v=kept.own_v, q=kept.q, dq=dq, pre_above=back.pre, blocks=blocks,
        own=own_seg, all=all_seg, cos=cos, sin=sin,
    )
    ins.update({"w_" + name: weights[name] for name in names})
    hbm = {"w_" + name for name in names} | {"q"}
    single = len(blocks) == 1
    if single:
        hbm.add("blocks")
    wide = 1 if below else 2
    outs = Names(
        qkv_near=sds((n, wide * QKV), BF), qkv_send=sds((n, wide * QKV), BF), qkv_side=sds((n, wide * 2 * QKV), BF), qkv_sums=sds((8, D), F32),
        dk=sds((n, D), BF), dv=sds((n, D), BF),
    )
    scratch = Names(
        s_q=pltpu.VMEM((total, D), BF), s_g=pltpu.VMEM((total, D), BF), s_extra=pltpu.VMEM((total, LANES), BF),
        s_stats=pltpu.VMEM((32, total), F32), s_dk=pltpu.VMEM((n, D), BF), s_dv=pltpu.VMEM((n, D), BF),
        q_sems=pltpu.SemaphoreType.DMA((PAIRS + 2,)), **rooms(names),
    )
    if below:
        ins.update({k: below[k] for k in ("n1", "n2", "stat", "slope", "attn", "lse")}, vec=vec[layer - 1])
        outs.update(feed_back_outs(n, False))
        ins.far = list(far)
        scratch.s_inner = pltpu.VMEM((n, FF), BF)
    else:
        outs.grad = sds((n, D), BF)
        ins.update(above_near=back.qkv_near, above_send=back.qkv_send, above_side=back.qkv_side)

    def kernel(r):
        queries = Copies(r.q_sems)
        if single:
            queries.start("g", r.blocks[0].at[:, :D], r.s_g)
            queries.start("extra", r.blocks[0].at[:, D:], r.s_extra)
        for p in range(PAIRS):
            queries.start(f"q{p}", r.q.at[:, lanes(p)], r.s_q.at[:, lanes(p)])
        copies = Copies(r.sems)
        copies.weights(r, layer, names[:3])
        if below:
            copies.weights(r, layer - 1, names[3:])
        if single:
            queries.wait("g", "extra")
        else:
            join(r.s_g, r.blocks, slice(0, D))
            join(r.s_extra, r.blocks, slice(D, D + LANES))
        key_back_phase(r, queries)
        r.dk[...] = r.s_dk[...]
        r.dv[...] = r.s_dv[...]
        grad = input_back_phase(r, copies)
        if below:
            feed_back_phase(r, copies, grad)
            r.send[:, NEAR:NEAR_PACK] = jnp.zeros((n, NEAR_PACK - NEAR), BF)
            for i, ref in enumerate(r.far):
                at = NEAR_PACK + i * 2 * D
                r.send[:, at : at + 2 * D] = ref[...]
        else:
            r.grad[...] = grad.astype(BF)

    flops = 8 * n * total * D * 2 + 6 * n * D * D + (2 * n * (D * D + 2 * D * FF) if below else 0)
    return mega(kernel, "layer_back" if below else "layer_back_first", ins, outs, scratch, flops, hbm=hbm, after=after)


def feed_pieces(place, packs, near, side, cross, after=()):
    n = near[0].shape[0]
    here, there = packs
    ins = Names(
        place=place, here=[a for a, _ in here], att=[a for a, _, _, _ in there], act=[a for _, _, a, _ in there],
        near=list(near), side=list(side), cross=list(cross),
    )
    io, u = sds((4, WIDTH, IO), BF), sds((4, WIDTH, 2 * ACTIVE), BF)
    scratch = Names(
        t_hidden=pltpu.VMEM((D, 4 * n), BF), t_attn=pltpu.VMEM((D, 4 * n), BF), t_outer=pltpu.VMEM((2, CHUNK, 4 * n), BF),
    )

    def kernel(r):
        hidden = [(ref, at) for ref, (_, at) in zip(r.here, here)] + [(ref, at) for ref, (_, at, _, _) in zip(r.att, there)]
        turned(r.t_hidden, *[ref[:, at : at + D] for ref, at in hidden])
        turned(r.t_attn, *[ref[:, at + D : at + 2 * D] for ref, at in hidden])
        n0, n1 = r.near
        y0, y1 = r.side
        x0, x1 = r.cross
        inner = jnp.concatenate([n0[:, :FB], n1[:, :FB], y0[:, :FB], y1[:, FB : 2 * FB]], axis=0)
        out = jnp.concatenate(
            [n0[:, NEAR_OUT:NEAR], n1[:, NEAR_OUT:NEAR], y0[:, SIDE_OUT : SIDE_OUT + CHUNK], y1[:, SIDE_OUT + CHUNK : SIDE]], axis=0
        )
        x, y = r.place[0], r.place[1]
        for name, side_x in (("io_send", 1 - x), ("io_keep", x)):
            r[name][:, :, :FB] = dot(shard_rows(r.t_hidden, side_x), inner).astype(BF).reshape(4, WIDTH, FB)
            r[name][:, :, FB:] = dot(shard_rows(r.t_attn, side_x), out).astype(BF).reshape(4, WIDTH, CHUNK)
        sources = [(n0, NEAR_OUTER), (n1, NEAR_OUTER), (x0, 0), (x1, 2 * CHUNK)]
        for h in range(2):
            turned(r.t_outer.at[h], *[ref[:, at + h * CHUNK : at + (h + 1) * CHUNK] for ref, at in sources])
        active = [ref[:, at + 2 * D : at + PACK] for ref, (_, at) in zip(r.here, here)]
        active += [ref[:, at : at + FF // 2] for ref, (_, _, _, at) in zip(r.act, there)]
        active = jnp.concatenate(active, axis=0)
        for name, side_y in (("u_send", 1 - y), ("u_keep", y)):
            t = dot(r.t_outer[side_y], active).astype(BF)
            for z in range(4):
                part = t[:, z * ACTIVE : (z + 1) * ACTIVE]
                r[name][z, :, :ACTIVE] = part[:WIDTH]
                r[name][z, :, ACTIVE:] = part[WIDTH:]

    outs = Names(io_keep=io, io_send=io, u_keep=u, u_send=u)
    return mega(kernel, "feed_pieces", ins, outs, scratch, 8 * n * (D * IO + FF * CHUNK), after=after, vmem=32)


def qkv_pieces(place, blocks, near, side, after=()):
    n = near[0].shape[0]
    ins = Names(place=place, blocks=[b[k] for b in blocks for k in (0, 4, 2, 6)], near=list(near), side=list(side))
    o = sds((4, WIDTH, padded(QKV) + QKV), BF)

    def kernel(r):
        (g0, g1), (y0, y1) = r.near, r.side
        x = r.place[0]
        for layer in range(LAYERS):
            turned(r.t_rows.at[layer], *[ref[...] for ref in r.blocks[4 * layer : 4 * layer + 4]])
            parts = (g0, layer * QKV), (g1, layer * QKV), (y0, 2 * layer * QKV), (y1, (2 * layer + 1) * QKV)
            g = jnp.concatenate([ref[:, at : at + QKV] for ref, at in parts], axis=0)
            at = layer * padded(QKV)
            for name, side_x in (("send", 1 - x), ("keep", x)):
                found = dot(shard_rows(r.t_rows.at[layer], side_x), g).astype(BF)
                r[name][:, :, at : at + QKV] = found.reshape(4, WIDTH, QKV)

    scratch = Names(t_rows=pltpu.VMEM((LAYERS, D, 4 * n), BF))
    return mega(kernel, "qkv_pieces", ins, Names(keep=o, send=o), scratch, 16 * n * D * QKV, after=after, vmem=24)


def padded(w):
    return -(-w // LANES) * LANES


def first_sum(place, pairs, after=()):
    width = sum(padded(a.shape[2]) for a, _ in pairs)
    o = sds((2, WIDTH, width), BF)

    def kernel(r):
        bit = r.place[3] % 2
        for name, side in (("keep", bit), ("send", 1 - bit)):
            for i in range(2):
                at = 0
                for a, b in zip(r.own, r.got):
                    w = a.shape[2]
                    r[name][i, :, at : at + w] = (a[2 * i + side].astype(F32) + b[2 * i + side].astype(F32)).astype(BF)
                    at += padded(w)

    ins = Names(place=place, own=[a for a, _ in pairs], got=[b for _, b in pairs])
    return mega(kernel, "first_sum", ins, Names(keep=o, send=o), {}, 1000, after=after, vmem=24)


def second_sum(place, keep, got, after=()):
    o = sds(keep.shape[1:], BF)

    def kernel(r):
        bit = r.place[3] // 2
        for name, side in (("keep", bit), ("send", 1 - bit)):
            r[name][...] = (r.own[side].astype(F32) + r.got[side].astype(F32)).astype(BF)

    return mega(kernel, "second_sum", Names(place=place, own=keep, got=got), Names(keep=o, send=o), {}, 1000, after=after, vmem=24)


FEED_SHAPES = Names(inner=(WIDTH, FB), out=(WIDTH, CHUNK), outer=(CHUNK, ACTIVE))
QKV_SHAPES = Names(query=(WIDTH, CHUNK), key=(WIDTH, CHUNK), value=(WIDTH, CHUNK))


def last_feed(layers):
    outs = Names((k, sds((LAYERS,) + v, F32)) for k, v in FEED_SHAPES.items())

    def kernel(r):
        for layer, (a, b) in enumerate(zip(r.own, r.got)):
            total = a[...].astype(F32) + b[...].astype(F32)
            r.inner[layer] = total[:, :FB]
            r.out[layer] = total[:, FB:IO]
            r.outer[layer, :WIDTH] = total[:, IO_PAD : IO_PAD + ACTIVE]
            r.outer[layer, WIDTH:] = total[:, IO_PAD + ACTIVE :]

    return mega(kernel, "last_feed", Names(own=[a for a, _ in layers], got=[b for _, b in layers]), outs, {}, 1000, vmem=24)


def last_qkv(keep, got):
    outs = Names((k, sds((LAYERS,) + v, F32)) for k, v in QKV_SHAPES.items())

    def kernel(r):
        total = r.own[...].astype(F32) + r.got[...].astype(F32)
        for layer in range(LAYERS):
            for i, name in enumerate(QKV_SHAPES):
                at = layer * padded(QKV) + i * CHUNK
                r[name][layer] = total[:, at : at + CHUNK]

    return mega(kernel, "last_qkv", Names(own=keep, got=got), outs, {}, 1000, vmem=24)


def linear(z, x, y, c):
    return (z * 2 + x) * 4 + y * 2 + c


PLACES = [(z, x, y, c) for z in range(4) for x in range(2) for y in range(2) for c in range(2)]


def move(array, where):
    pairs = [(linear(*place), linear(*where(*place))) for place in PLACES]
    return lax.ppermute(array, BOTH, pairs)


def to_plane(z, x, y, c):
    return (2 * y + c, x, z >> 1, z & 1)


def other_core(z, x, y, c):
    return (z, x, y, 1 - c)


def other_x(z, x, y, c):
    return (z, 1 - x, y, c)


def other_y(z, x, y, c):
    return (z, x, 1 - y, c)


def other_xy(z, x, y, c):
    return (z, 1 - x, 1 - y, c)


def near_z(z, x, y, c):
    return (z ^ 1, x, y, c)


def far_z(z, x, y, c):
    return (z ^ 2, x, y, c)


def gate(arrays, *others):
    return lax.optimization_barrier((arrays, others))[0]


def pick(array, index, axis):
    return lax.dynamic_index_in_dim(array, index, axis, keepdims=False)


class Small:
    def __init__(self):
        seq, rows = lax.axis_index("seq"), lax.axis_index("rows")
        self.z, self.x, self.y, self.c = seq // 2, seq % 2, rows // 2, rows % 2
        self.spot = jnp.stack([self.x, self.y, self.c, self.z]).astype(jnp.int32)

    def starts(self, count):
        out = []
        for dc in (0, 1):
            for dx, dy in ((0, 0), (1, 0), (0, 1), (1, 1)):
                x, y, c = self.x ^ dx, self.y ^ dy, self.c ^ dc
                out.append(((2 * y + c) * 2 + x) * count)
        return jnp.stack(out)

    def reach(self, array):
        return [array, move(array, other_x), move(array, other_y), move(array, other_xy)]

    def share(self, mine):
        return mine + [move(a, other_core) for a in mine]


class Large:
    def __init__(self):
        self.shards = lax.axis_size("seq")
        self.spot = jnp.zeros((4,), jnp.int32)

    def starts(self, count):
        me = lax.axis_index("seq")
        return (me + jnp.arange(self.shards, dtype=jnp.int32)) % self.shards * count

    def gather(self, array):
        whole_row = lax.all_gather(array, "seq", axis=0, tiled=True)
        return [jnp.roll(whole_row, -lax.axis_index("seq") * array.shape[0], axis=0)]

    def spread(self, left, right):
        grad = lax.dot_general(left, right, (((0,), (0,)), ((), ())), preferred_element_type=F32).astype(BF)
        grad = lax.psum_scatter(grad, "seq", scatter_dimension=0, tiled=True)
        return lax.psum_scatter(grad, "rows", scatter_dimension=1, tiled=True).astype(F32)

    def grads(self, kept, back, tail, dq):
        near, send, to_x, to_y = back.near, back.send, back.to_x, back.to_y
        inner = cat(near[:, :FB], send[:, :FB], to_y[:, : 2 * FB])
        out = cat(near[:, NEAR_OUT:NEAR], send[:, NEAR_OUT:NEAR], to_y[:, SIDE_OUT:SIDE])
        outer = cat(*[to_x[:, i * CHUNK : (i + 1) * CHUNK] for i in (0, 2, 1, 3)])
        if "active" in kept:
            hidden, attn = kept.side[:, :D], kept.side[:, D:]
            mine, other = kept.keep_pack[:, 2 * D :], kept.active
        else:
            hidden, attn = to_y[:, SIDE : SIDE + D], to_y[:, SIDE + D :]
            mine, other = near[:, NEAR_PACK + 2 * D :], to_x[:, D:]
        active = jnp.stack([v.reshape(-1, 4, ACTIVE) for v in (mine, other)], axis=2).reshape(-1, FF)
        own = kept.blocks[0][: dq.shape[0]]
        return Names(
            inner=self.spread(hidden, inner), out=self.spread(attn, out), outer=self.spread(active, outer),
            query=self.spread(own, dq), key=self.spread(own, tail.dk), value=self.spread(own, tail.dv),
        )


def doc_layout(lengths_row, index):
    ends = jnp.cumsum(lengths_row, dtype=jnp.int32)
    passed = (index[:, None] >= ends[None, :]).astype(jnp.int32)
    segment = jnp.sum(passed, axis=1, dtype=jnp.int32)
    begin = jnp.sum(passed * lengths_row[None, :], axis=1, dtype=jnp.int32)
    return (segment, (index - begin).astype(jnp.int32))


def rotary_tables(position):
    lane = jnp.arange(LANES, dtype=jnp.int32)
    pairs = (lane % HEAD_DIM // 2).astype(F32)
    inverse = jnp.power(jnp.float32(10000.0), -2.0 * pairs / HEAD_DIM)
    angle = position.astype(F32)[:, None] * inverse[None, :]
    return jnp.cos(angle), jnp.sin(angle) * jnp.where(lane % 2 == 0, -1.0, 1.0)[None, :]


def both_cores(array):
    return array, move(array, other_core)


def all_sums(two, tail_two, one, tail_one):
    return jnp.concatenate([one.sums[:10], tail_one.qkv_sums[:3], two.sums[:10], tail_two.qkv_sums[:3]], axis=0)


VECTOR_ROWS = Names(g2=0, c2=1, bu=2, g1=3, c1=4, bo=5, bq=10, bk=11, bv=12)
LAYER_ROWS = 13


def last_vectors(place, own, got):
    outs = Names((name, sds((LAYERS, WIDTH), F32)) for name in VECTOR_ROWS)
    outs.bi = sds((LAYERS, ACTIVE), F32)

    def kernel(r):
        x, z = r.place[0], r.place[3]
        total = r.own[...] + r.got[...]
        r.s_total[...] = total
        shard = 2 * z + x
        turn = pltpu.roll(total, (D - shard * WIDTH) % D, 1)[:, :WIDTH]
        for layer in range(LAYERS):
            for name, row in VECTOR_ROWS.items():
                at = LAYER_ROWS * layer + row
                r[name][layer : layer + 1, :] = turn[at : at + 1]
            row = r.s_total[pl.ds(LAYER_ROWS * layer + 6 + z, 1), :]
            r.bi[layer : layer + 1, :] = jnp.where(x == 0, row[:, :ACTIVE], row[:, ACTIVE:])

    scratch = Names(s_total=pltpu.VMEM(own.shape, F32))
    return mega(kernel, "last_vectors", Names(place=place, own=own, got=got), outs, scratch, 1000, vmem=24)


class Program:
    def __init__(self, place, spot, lengths_row, n, starts, params):
        wq, bq, wk, bk, wv, bv, wo, bo, g1, c1, wi, bi, wu, bu, g2, c2 = params
        self.weights = Names(wq=wq, wk=wk, wv=wv, wo=wo, wi=wi, wu=wu)
        self.spot, self.n = spot, n
        self.vec = jnp.stack([bq, bk, bv, bo, g1, c1, bu, g2, c2], axis=1).astype(F32)
        self.bi = bi.astype(F32)[:, None, :]
        index = (starts[:, None] + jnp.arange(n, dtype=jnp.int32)).reshape(-1)
        segment, position = doc_layout(lengths_row, index)
        self.segments = segment[:n, None], segment[None, :]
        self.cos, self.sin = rotary_tables(position)
        self.own_cos, self.own_sin = rotary_tables(position[:n])

    def project(self, layer, rows):
        w = self.weights
        return project(rows, layer, w["wq"], w["wk"], w["wv"], self.vec, self.cos, self.sin)

    def forward(self, layer, x, blocks, qkv=None, cotangent=None, after=()):
        kept = layer_forward(
            layer, self.spot, x, blocks, self.weights, self.bi, self.vec, self.cos, self.sin, *self.segments, qkv, cotangent, after
        )
        kept.blocks = blocks
        if qkv:
            kept.update(zip("qkv", qkv), own_k=qkv[1][: self.n], own_v=qkv[2][: self.n])
        return kept

    def queries(self, kept, back, after=()):
        return query_back(
            kept.q, kept.k, kept.v, back.pack, kept.lse, back.delta, *self.segments, self.own_cos, self.own_sin, after
        )[0]

    def back(self, layer, kept, back, dq, packs, below=None, far=(), after=()):
        return layer_back(
            layer, self.spot, kept, back, dq, packs, self.weights, self.vec, self.own_cos, self.own_sin, *self.segments, below, far, after
        )


def large_body(tokens, lengths, cotangent, *params):
    place = Large()
    n = tokens.shape[1]
    run = Program(place, place.spot, lengths[0], n, place.starts(n), params)

    def step(layer, x, x_b, cotangent=None):
        blocks = place.gather(x_b)
        return run.forward(layer, x, blocks, run.project(layer, blocks[0]), cotangent)

    first = step(0, tokens[0], tokens[0])
    second = step(1, first.result, first.result_b, cotangent[0])
    dq_two = run.queries(second, second)
    back_one = run.back(1, second, second, dq_two, place.gather(second.pack), first)
    dq_one = run.queries(first, back_one)
    back_none = run.back(0, first, back_one, dq_one, place.gather(back_one.pack))
    grads_one = place.grads(first, back_one, back_none, dq_one)
    grads_two = place.grads(second, second, back_one, dq_two)
    m = Names((name, jnp.stack([grads_one[name], grads_two[name]])) for name in grads_one)
    total = lax.psum(all_sums(second, back_one, back_one, back_none), BOTH).reshape(LAYERS, LAYER_ROWS, D)
    me, shards = lax.axis_index("seq"), lax.axis_size("seq")
    v = Names(
        (name, lax.dynamic_slice_in_dim(total[:, row], me * (D // shards), D // shards, 1))
        for name, row in VECTOR_ROWS.items()
    )
    v.bi = lax.dynamic_slice_in_dim(total[:, 6:10].reshape(LAYERS, FF), me * (FF // shards), FF // shards, 1)
    return result(second.result_b, back_none.grad, m, v)


def small_body(tokens, lengths, cotangent, *params):
    place = Small()
    spot, n = place.spot, tokens.shape[1]
    current = move(tokens[0], to_plane)
    run = Program(place, spot, move(lengths, to_plane)[0], n, place.starts(n), params)
    blocks = place.share(gate(place.reach(current), run.cos, run.sin, run.own_cos, run.own_sin, run.vec, run.bi))
    grad = move(gate(cotangent[0], current), to_plane)
    first = run.forward(0, current, blocks, after=(grad,))
    a_near = both_cores(first.keep_pack)
    blocks = place.share(place.reach(first.result_b))
    side, active = gate((first.side, first.active), blocks)
    a_side, a_cross = move(side, other_y), move(active, other_x)
    second = run.forward(1, first.result, blocks, cotangent=grad, after=(a_near[1],))

    reached = place.reach(second.pack)
    dq_two = run.queries(second, second, after=(a_side, a_cross))
    packs = place.share(gate(reached, dq_two))
    to_y, to_x, send, result_b = gate((second.to_y, second.to_x, second.send, second.result_b), packs)
    from_y, from_x, near = move(to_y, other_y), move(to_x, other_x), (second.near, move(send, other_core))
    output = move(result_b, to_plane)
    back_one = run.back(1, second, second, dq_two, packs, first, (a_side, a_cross))

    pack, from_y, from_x, near_got = gate((back_one.pack, from_y, from_x, near[1]), output)
    near = near[0], near_got
    reached = place.reach(pack)
    side, cross = [both_cores(a) for a in gate((from_y, from_x), pack)]
    dq_one = run.queries(first, back_one)
    packs = place.share(gate(reached, dq_one))
    to_y, to_x = gate((back_one.to_y, back_one.to_x), reached, dq_one)
    one_y, one_x = move(to_y, other_y), move(to_x, other_x)
    there = [(a, SIDE, b, D) for a, b in zip(side, cross)]
    two = feed_pieces(spot, ([(a, NEAR_PACK) for a in near], there), near, side, cross, after=(dq_one, *reached))
    two_io, two_u = move(two.io_send, other_x), move(two.u_send, other_y)
    near = back_one.near, move(gate(back_one.send, reached, dq_one), other_core)
    back_none = run.back(0, first, back_one, dq_one, packs, after=(two.io_send, near[1], one_x))

    two_sum = first_sum(spot, ((two.io_keep, two_io), (two.u_keep, two_u)), after=(back_none.grad, one_y, near[1]))
    side, cross = [both_cores(a) for a in gate((one_y, one_x), back_none.grad)]
    q_side = move(back_none.qkv_side, other_y)
    sums = all_sums(second, back_one, back_one, back_none)
    from_sums = move(sums, other_core)
    two_near = move(two_sum.send, near_z)
    there = [(a_side, 0, a_cross, 0), (near[1], NEAR_PACK, near[1], NEAR_PACK + 2 * D)]
    one = feed_pieces(spot, ([(a, 0) for a in a_near], there), near, side, cross, after=(two_sum.send,))
    one_io, one_u = move(one.io_send, other_x), move(one.u_send, other_y)
    sums = gate(sums + from_sums, two_sum.send)
    from_sums = move(sums, near_z)
    qkv_send, q_side = gate((back_none.qkv_send, q_side), one.io_send)
    q_near, q_side = (back_none.qkv_near, move(qkv_send, other_core)), both_cores(q_side)
    qkv = qkv_pieces(spot, (first.blocks, second.blocks), q_near, q_side, after=(one.io_send, from_sums))
    q_x = move(qkv.send, other_x)
    two_z = second_sum(spot, two_sum.keep, two_near, after=(qkv.send, one_io))
    two_far = move(two_z.send, far_z)
    sums = gate(sums + from_sums, qkv.send)
    from_sums = move(sums, far_z)
    one_sum = first_sum(spot, ((one.io_keep, one_io), (one.u_keep, one_u)), after=(two_z.send, from_sums))
    one_near = move(one_sum.send, near_z)
    sums = gate(sums + from_sums, one_sum.send)
    from_sums = move(sums, other_x)
    tokens_grad = move(gate(back_none.grad, qkv.send), to_plane)
    q_sum = first_sum(spot, ((qkv.keep, q_x),), after=(one_sum.send, tokens_grad, two_far))
    q_near = move(q_sum.send, near_z)
    sums = gate(sums + from_sums, q_sum.send)
    from_sums = move(sums, other_y)
    one_z = second_sum(spot, one_sum.keep, one_near, after=(q_sum.send,))
    one_far = move(one_z.send, far_z)
    q_z = second_sum(spot, q_sum.keep, q_near, after=(one_z.send,))
    q_far = move(q_z.send, far_z)
    v = last_vectors(spot, sums, from_sums)
    m = last_feed(((one_z.keep, one_far), (two_z.keep, two_far)))
    m.outer = m.outer.swapaxes(1, 2)
    m.update(last_qkv(q_z.keep, q_far))
    return result(output, tokens_grad, m, v)


def result(output, tokens_grad, m, v):
    return (
        output[None], tokens_grad[None],
        m.query, v.bq, m.key, v.bk, m.value, v.bv, m.out, v.bo, v.g1, v.c1,
        m.inner, v.bi, m.outer, v.bu, v.g2, v.c2,
    )


def solution(mesh):
    token = P("rows", "seq", None)
    mat, vec = P(None, "seq", "rows"), P(None, "seq")
    small = (mesh.shape["seq"], mesh.shape["rows"]) == (8, 4)
    return jax.shard_map(
        small_body if small else large_body,
        mesh=mesh,
        in_specs=(token, P("rows", None), token) + (P(),) * 16,
        out_specs=(token, token, mat, vec, mat, vec, mat, vec, mat, vec, vec, vec, mat, vec, mat, vec, vec, vec),
        check_vma=False,
    )
```

```python
import jax
import jax.numpy as jnp
from jax import lax
from jax.experimental import pallas as pl
from jax.experimental.pallas import tpu as pltpu
from jax.sharding import PartitionSpec as P

D = 768
HEADS = 12
HEAD_DIM = 64
FF = 3072
LAYERS = 2
LANES = 128
PAIRS = D // LANES
CHUNK = D // 4
NEG_FILL = -1e30
NORM_EPS = 1e-12
SCALE = HEAD_DIM**-0.5
BF = jnp.bfloat16
F32 = jnp.float32
BOTH = ("seq", "rows")
MIB = 1 << 20

BQ, BK, BV, BO, G1, C1, BU, G2, C2 = range(9)
FB = 768
WIDTH = D // 8
ACTIVE = FF // 8
QKV = 3 * CHUNK
IO = FB + CHUNK
IO_PAD = FB + 2 * LANES

NEAR_OUTER, NEAR_OUT, NEAR = FB, FB + 2 * CHUNK, FB + 3 * CHUNK
NEAR_PACK = NEAR + 64
SIDE_OUT, SIDE = 2 * FB, 2 * FB + 2 * CHUNK
PACK = 2 * D + FF // 2

LSE_HI, LSE_LO, DELTA_HI, DELTA_LO = 0, 16, 32, 48


class Names(dict):
    __getattr__ = dict.__getitem__
    __setattr__ = dict.__setitem__


def dot(a, b):
    return jnp.dot(a, b, preferred_element_type=F32)


def dot_nt(a, b):
    return lax.dot_general(a, b, (((1,), (1,)), ((), ())), preferred_element_type=F32)


def call(kernel, name, grid, in_specs, out_specs, out_shape, args, flops, scratch=(), scalars=(), vmem=60, after=(), aliases=None):
    size = sum(a.size * a.dtype.itemsize for a in args) + sum(
        s.size * s.dtype.itemsize for s in jax.tree.leaves(out_shape)
    )
    lead, many = len(scalars) + len(args), len(after)

    def run(*refs):
        kernel(*refs[:lead], *refs[lead + many :])

    return pl.pallas_call(
        run,
        name=name,
        grid_spec=pltpu.PrefetchScalarGridSpec(
            num_scalar_prefetch=len(scalars),
            grid=grid,
            in_specs=list(in_specs) + [pl.BlockSpec(memory_space=pl.ANY)] * many,
            out_specs=out_specs,
            scratch_shapes=list(scratch),
        ),
        out_shape=out_shape,
        input_output_aliases=aliases or {},
        compiler_params=pltpu.CompilerParams(
            dimension_semantics=("arbitrary",) * len(grid), vmem_limit_bytes=vmem * MIB
        ),
        cost_estimate=pl.CostEstimate(flops=int(flops), bytes_accessed=int(size), transcendentals=0),
    )(*scalars, *args, *after)


def whole(array):
    return pl.BlockSpec(array.shape, lambda *_: (0,) * array.ndim)


def layer_block(array, layer):
    return pl.BlockSpec((None,) + array.shape[1:], lambda *_: (layer,) + (0,) * (array.ndim - 1))


def sds(shape, dtype):
    return jax.ShapeDtypeStruct(shape, dtype)


def lane_is_even(shape):
    return lax.broadcasted_iota(jnp.int32, shape, 1) % 2 == 0


def swap_pairs(v):
    return jnp.where(lane_is_even(v.shape), pltpu.roll(v, LANES - 1, 1), pltpu.roll(v, 1, 1))


def lanes(j):
    return slice(j * LANES, (j + 1) * LANES)


def qkv_kernel(x_ref, wq_ref, wk_ref, wv_ref, vec_ref, cos_ref, sin_ref, q_ref, k_ref, v_ref):
    x, cos, sin = x_ref[...], cos_ref[...], sin_ref[...]
    for w_ref, row, o_ref in ((wq_ref, BQ, q_ref), (wk_ref, BK, k_ref)):
        y = dot(x, w_ref[...]) + vec_ref[row : row + 1, :]
        for j in range(PAIRS):
            t = y[:, lanes(j)]
            o_ref[:, lanes(j)] = (t * cos + swap_pairs(t) * sin).astype(BF)
    v_ref[...] = (dot(x, wv_ref[...]) + vec_ref[BV : BV + 1, :]).astype(BF)


def project(rows, layer, wq, wk, wv, vec, cos, sin):
    total = rows.shape[0]
    block = min(256, total)
    tok = lambda w: pl.BlockSpec((block, w), lambda i: (i, 0))
    return call(
        qkv_kernel, "qkv", (total // block,),
        [tok(D)] + [layer_block(w, layer) for w in (wq, wk, wv, vec)] + [tok(LANES), tok(LANES)],
        [tok(D)] * 3, [sds((total, D), BF)] * 3,
        (rows, wq, wk, wv, vec, cos, sin), 6 * total * D * D,
    )


def over_chunks(total, body, carry):
    size = min(total, 1024)
    if size == total:
        return body(slice(None), carry)
    return lax.fori_loop(
        0, total // size, lambda i, c: body(pl.ds(pl.multiple_of(i * size, size), size), c), carry
    )


def two_heads(v):
    low = lax.broadcasted_iota(jnp.int32, v.shape, 1) < HEAD_DIM
    zero = jnp.zeros_like(v)
    return jnp.concatenate([jnp.where(low, v, zero), jnp.where(low, zero, v)], axis=0)


def join_heads(v):
    n = v.shape[0] // 2
    low = lax.broadcasted_iota(jnp.int32, (n, LANES), 1) < HEAD_DIM
    return jnp.where(low, v[:n], v[n:])


def normalize(values):
    centered = values - jnp.mean(values, axis=-1, keepdims=True)
    rstd = lax.rsqrt(jnp.mean(centered * centered, axis=-1, keepdims=True) + NORM_EPS)
    return centered * rstd, rstd


def column_sum(v):
    return jnp.sum(v.astype(F32), axis=0, keepdims=True)


def norm_back(grad, normed, rstd, gain):
    scaled = grad * gain
    centered = scaled - jnp.mean(scaled, axis=-1, keepdims=True)
    return rstd * (centered - normed * jnp.mean(scaled * normed, axis=-1, keepdims=True))


def either(first, a, b):
    return jnp.where(first, a, b), jnp.where(first, b, a)


def cat(*parts):
    return jnp.concatenate(parts, axis=1)


def quarters(v, y, c):
    part = [v[:, k * CHUNK : (k + 1) * CHUNK] for k in range(4)]
    mine0, theirs0 = either(c == 0, part[0], part[1])
    mine1, theirs1 = either(c == 0, part[2], part[3])
    mine, mine_y = either(y == 0, mine0, mine1)
    theirs, theirs_y = either(y == 0, theirs0, theirs1)
    return mine, theirs, mine_y, theirs_y


def hi_lo(v):
    hi = v.astype(BF)
    return hi, (v - hi.astype(F32)).astype(BF)


def unrotate(v, cos, sin):
    t = v * sin
    return v * cos + swap_pairs(t)


def lane_of(v, lane):
    at = lax.broadcasted_iota(jnp.int32, v.shape, 1)
    return jnp.sum(jnp.where(at == lane, v, 0.0), axis=1, keepdims=True)


def query_back_kernel(
    q_ref, k_ref, v_ref, g_ref, lse_ref, delta_ref, own_ref, all_ref, cos_ref, sin_ref,
    dq_ref, sum_ref,
):
    pair = pl.program_id(0)
    n, total = q_ref.shape[0], k_ref.shape[0]
    q = two_heads(q_ref[...] * jnp.asarray(SCALE, BF))
    g = two_heads(g_ref[...])
    own = own_ref[...]
    lse = jnp.concatenate([lane_of(lse_ref[...], 2 * pair), lane_of(lse_ref[...], 2 * pair + 1)], axis=0)
    delta = jnp.concatenate([lane_of(delta_ref[...], 2 * pair), lane_of(delta_ref[...], 2 * pair + 1)], axis=0)

    def body(at, acc):
        same = own == all_ref[:, at]
        k = k_ref[at, :]
        s = jnp.where(jnp.concatenate([same, same], axis=0), dot_nt(q, k) - lse, NEG_FILL)
        ds = (jnp.exp(s) * (dot_nt(g, v_ref[at, :]) - delta)).astype(BF)
        return acc + dot(ds, k)

    acc = join_heads(over_chunks(total, body, jnp.zeros((2 * n, LANES), F32))) * SCALE
    dq = unrotate(acc, cos_ref[...], sin_ref[...]).astype(BF)
    dq_ref[...] = dq
    sum_ref[...] = column_sum(dq)


def query_back(q, k, v, pack, lse, delta, own_seg, all_seg, cos, sin, after=()):
    n, total = pack.shape[0], k.shape[0]
    own = pl.BlockSpec((n, LANES), lambda p: (0, p))
    row = pl.BlockSpec((total, LANES), lambda p: (0, p))
    fixed = lambda w: pl.BlockSpec((n, w), lambda p: (0, 0))
    return call(
        query_back_kernel, "query_back", (PAIRS,),
        [own, row, row, own, fixed(LANES), fixed(LANES), whole(own_seg), whole(all_seg), fixed(LANES), fixed(LANES)],
        [own, pl.BlockSpec((1, LANES), lambda p: (0, p))],
        [sds((n, D), BF), sds((1, D), F32)],
        (q, k, v, pack, lse, delta, own_seg, all_seg, cos, sin), 6 * n * total * D * 2, after=after,
    )


def turned(ref, *parts):
    n = parts[0].shape[0]
    for i, part in enumerate(parts):
        ref[:, i * n : (i + 1) * n] = part.T


def shard_rows(ref, x):
    width = WIDTH
    return jnp.concatenate(
        [ref[pl.ds(pl.multiple_of((2 * z + x) * width, 32), width), :] for z in range(4)], axis=0
    )


def mega(kernel, name, ins, outs, scratch, flops, hbm=(), after=(), vmem=60):
    flat_in, tree_in = jax.tree.flatten(dict(ins))
    flat_out, tree_out = jax.tree.flatten(dict(outs))

    def spec_of(key):
        space = pl.ANY if key in hbm else pltpu.SMEM if key == "place" else pltpu.VMEM
        return pl.BlockSpec(memory_space=space)

    specs_in = jax.tree.leaves({k: jax.tree.map(lambda _: spec_of(k), v) for k, v in ins.items()})
    specs_out = jax.tree.leaves({k: jax.tree.map(lambda _: spec_of(k), v) for k, v in outs.items()})
    many_in, many_out = len(flat_in), len(flat_out)

    def run(*refs):
        lead = many_in + len(after)
        named = Names(tree_in.unflatten(refs[:many_in]))
        named.update(tree_out.unflatten(refs[lead : lead + many_out]))
        named.update(zip(scratch, refs[lead + many_out :]))
        kernel(named)

    size = sum(a.size * a.dtype.itemsize for a in flat_out) + sum(
        a.size * a.dtype.itemsize for k, v in ins.items() if k not in hbm for a in jax.tree.leaves(v)
    )
    out = pl.pallas_call(
        run,
        name=name,
        in_specs=specs_in + [pl.BlockSpec(memory_space=pl.ANY)] * len(after),
        out_specs=specs_out,
        out_shape=flat_out,
        scratch_shapes=list(scratch.values()),
        compiler_params=pltpu.CompilerParams(vmem_limit_bytes=vmem * MIB),
        cost_estimate=pl.CostEstimate(flops=int(flops), bytes_accessed=int(size), transcendentals=0),
    )(*flat_in, *after)
    return Names(tree_out.unflatten(out))


SHAPES = Names(wq=(D, D), wk=(D, D), wv=(D, D), wo=(D, D), wi=(D, FF), wu=(FF, D))


def rooms(names):
    found = Names(("m_" + name, pltpu.VMEM(SHAPES[name], BF)) for name in names)
    found.sems = pltpu.SemaphoreType.DMA((16,))
    return found


def units(j):
    return pl.ds(j * FB, FB)


class Copies:
    def __init__(self, sems):
        self.sems, self.copies = sems, {}

    def start(self, name, src, dst):
        self.copies[name] = pltpu.make_async_copy(src, dst, self.sems.at[len(self.copies)])
        self.copies[name].start()

    def weights(self, r, layer, names):
        for name in names:
            src, dst = r["w_" + name].at[layer], r["m_" + name]
            if name not in ("wi", "wu"):
                self.start(name, src, dst)
                continue
            for j in range(FF // FB):
                at = (slice(None), units(j)) if name == "wi" else (units(j), slice(None))
                self.start(f"{name}{j}", src.at[at], dst.at[at])

    def wait(self, *names):
        for name in names:
            if name in self.copies:
                self.copies.pop(name).wait()


def join(dst, refs, columns):
    at = 0
    for ref in refs:
        dst[at : at + ref.shape[0], :] = ref[:, columns]
        at += ref.shape[0]


def row_of(r, index):
    return r.vec[index : index + 1, :]


def qkv_phase(r, copies):
    rows, cos, sin = r.s_rows, r.cos, r.sin
    total = rows.shape[0]
    block = min(256, total)
    for name, bias in (("k", BK), ("v", BV), ("q", BQ)):
        copies.wait("w" + name)
        for i in range(total // block):
            at = pl.ds(i * block, block)
            y = dot(rows[at, :], r["m_w" + name][...]) + row_of(r, bias)
            if name == "v":
                r.s_v[at, :] = y.astype(BF)
                continue
            for j in range(PAIRS):
                t = y[:, lanes(j)]
                r["s_" + name][at, lanes(j)] = (t * cos[at, :] + swap_pairs(t) * sin[at, :]).astype(BF)


def attend_phase(r):
    n, total = r.attn.shape[0], r.s_k.shape[0]
    own = r.own[...]
    lane = lax.broadcasted_iota(jnp.int32, (n, LANES), 1)
    lse = jnp.zeros((n, LANES), F32)
    for p in range(PAIRS):
        q = two_heads(r.s_q[:n, lanes(p)] * jnp.asarray(SCALE, BF))

        def body(at, carry):
            top, tot, acc = carry
            same = own == r.all[:, at]
            s = dot_nt(q, r.s_k[at, lanes(p)])
            s = jnp.where(jnp.concatenate([same, same], axis=0), s, NEG_FILL)
            fresh = jnp.maximum(top, jnp.max(s, axis=1, keepdims=True))
            e = jnp.exp(s - fresh)
            keep = jnp.exp(top - fresh)
            tot = tot * keep + jnp.sum(e, axis=1, keepdims=True)
            acc = acc * keep + dot(e.astype(BF), r.s_v[at, lanes(p)])
            return fresh, tot, acc

        zero = jnp.zeros((2 * n, 1), F32)
        top, tot, acc = over_chunks(total, body, (zero + NEG_FILL, zero, jnp.zeros((2 * n, LANES), F32)))
        r.attn[:, lanes(p)] = join_heads(acc / tot)
        part = top + jnp.log(tot)
        lse = jnp.where(lane == 2 * p, part[:n], jnp.where(lane == 2 * p + 1, part[n:], lse))
    r.lse[...] = lse


def ffn_phase(r, copies):
    stat_ref = r.stat
    lane = lax.broadcasted_iota(jnp.int32, stat_ref.shape, 1)
    copies.wait("wo")
    branch = dot(r.attn[...].astype(BF), r.m_wo[...]) + row_of(r, BO)
    n1, r1 = normalize(r.x[...].astype(F32) + branch)
    hidden = n1 * row_of(r, G1) + row_of(r, C1)
    r.n1[...] = n1
    hidden_b = hidden.astype(BF)
    r.s_hidden[...] = hidden_b
    total = hidden + row_of(r, BU)
    for j in range(FF // FB):
        copies.wait(f"wi{j}")
        inner = dot(hidden_b, r.m_wi[:, units(j)]) + r.bi[:, units(j)]
        half = 0.5 + 0.5 * lax.erf(inner * (0.5**0.5))
        active = (inner * half).astype(BF)
        r.slope[:, units(j)] = (half + inner * jnp.exp(-0.5 * inner * inner) * 0.3989422804014327).astype(BF)
        r.s_active[:, units(j)] = active
        copies.wait(f"wu{j}")
        total = total + dot(active, r.m_wu[units(j), :])
    n2, r2 = normalize(total)
    r.n2[...] = n2
    stat_ref[...] = jnp.where(lane == 0, r1, jnp.where(lane == 1, r2, 0.0))
    return n2 * row_of(r, G2) + row_of(r, C2)


def store_active(r, ref, at, x):
    for z in range(4):
        src = pl.ds(pl.multiple_of((2 * z + x) * ACTIVE, LANES), ACTIVE)
        ref[:, at + z * ACTIVE : at + (z + 1) * ACTIVE] = r.s_active[:, src]


def store_pack(r, ref, at, x):
    ref[:, at : at + D] = r.s_hidden[...]
    ref[:, at + D : at + 2 * D] = r.attn[...].astype(BF)
    store_active(r, ref, at + 2 * D, x)


def feed_back_phase(r, copies, grad):
    place = r.place
    y, c = place[1], place[2]
    n2 = r.n2[...]
    sums = r.sums
    sums[0:1, :] = column_sum(grad * n2)
    sums[1:2, :] = column_sum(grad)
    grad = norm_back(grad, n2, r.stat[:, 1:2], row_of(r, G2))
    outer = grad.astype(BF)
    sums[2:3, :] = column_sum(outer)
    mine, theirs, mine_y, theirs_y = quarters(outer, 0, c)
    mine, theirs = cat(mine, mine_y), cat(theirs, theirs_y)
    r.near[:, NEAR_OUTER:NEAR_OUT] = mine
    r.send[:, NEAR_OUTER:NEAR_OUT] = theirs
    r.to_x[:, : 2 * CHUNK] = mine
    r.to_x[:, 2 * CHUNK : D] = theirs
    for j in range(FF // FB):
        copies.wait(f"wu{j}")
        inner = (dot_nt(outer, r.m_wu[units(j), :]) * r.slope[:, units(j)].astype(F32)).astype(BF)
        sums[6 + j : 7 + j, :] = column_sum(inner)
        r.s_inner[:, units(j)] = inner
        copies.wait(f"wi{j}")
        grad = grad + dot_nt(inner, r.m_wi[:, units(j)])
    n1 = r.n1[...]
    sums[3:4, :] = column_sum(grad * n1)
    sums[4:5, :] = column_sum(grad)
    pre_one = norm_back(grad, n1, r.stat[:, 0:1], row_of(r, G1))
    r.pre[...] = pre_one
    branch = pre_one.astype(BF)
    sums[5:6, :] = column_sum(branch)
    sums[10:16, :] = jnp.zeros((6, D), F32)
    mine, theirs, mine_y, theirs_y = quarters(branch, y, c)
    r.near[:, NEAR_OUT:NEAR] = mine
    r.send[:, NEAR_OUT:NEAR] = theirs
    r.to_y[:, SIDE_OUT:SIDE] = cat(mine_y, theirs_y)
    copies.wait("wo")
    attn_grad = dot_nt(branch, r.m_wo[...]).astype(BF)
    r.pack[:, :D] = attn_grad
    feature = lax.broadcasted_iota(jnp.int32, (D, LANES), 0) // HEAD_DIM
    member = (feature == lax.broadcasted_iota(jnp.int32, (D, LANES), 1)).astype(BF)
    hi, lo = hi_lo(attn_grad.astype(F32) * r.attn[...])
    delta = dot(hi, member) + dot(lo, member)
    r.delta[...] = delta
    lse_hi, lse_lo = hi_lo(r.lse[...])
    delta_hi, delta_lo = hi_lo(delta)
    extra = lse_hi.astype(F32)
    for v, at in ((lse_lo, LSE_LO), (delta_hi, DELTA_HI), (delta_lo, DELTA_LO)):
        extra = extra + pltpu.roll(v.astype(F32), at, 1)
    r.pack[:, D:] = extra.astype(BF)
    shard = 2 * y + c
    for ref, at, k in (
        (r.near, 0, shard), (r.send, 0, 2 * y + 1 - c), (r.to_y, 0, 2 - 2 * y + c), (r.to_y, FB, 3 - 2 * y - c),
    ):
        ref[:, at : at + FB] = r.s_inner[:, pl.ds(pl.multiple_of(k * FB, LANES), FB)]


def key_back_phase(r, copies):
    place = r.place
    n, total = r.k.shape[0], r.s_g.shape[0]
    row = lax.broadcasted_iota(jnp.int32, (32, LANES), 0)
    lane = lax.broadcasted_iota(jnp.int32, (32, LANES), 1)
    first = jnp.where(row < 16, LSE_HI, DELTA_HI - 16) + row
    pick = ((lane == first) | (lane == first + 16)).astype(BF)
    rows_ref, own = r.s_stats, r.own[...]

    def fill(at, carry):
        rows_ref[:, at] = dot_nt(pick, r.s_extra[at, :])
        return carry

    over_chunks(total, fill, 0)
    for p in range(PAIRS):
        copies.wait(f"q{p}")
        k = two_heads(r.k[:, lanes(p)] * jnp.asarray(SCALE, BF))
        v = two_heads(r.v[:, lanes(p)])

        def body(at, carry):
            dk, dv = carry
            same = own == r.all[:, at]
            q, g = r.s_q[at, lanes(p)], r.s_g[at, lanes(p)]
            s, dp = dot_nt(k, q), dot_nt(v, g)
            probs, ds = [], []
            for h in range(2):
                half = slice(h * n, (h + 1) * n)
                lse, delta = rows_ref[2 * p + h : 2 * p + h + 1, at], rows_ref[16 + 2 * p + h : 17 + 2 * p + h, at]
                prob = jnp.exp(jnp.where(same, s[half] - lse, NEG_FILL))
                probs.append(prob.astype(BF))
                ds.append((prob * (dp[half] - delta)).astype(BF))
            return dk + dot(jnp.concatenate(ds, axis=0), q), dv + dot(jnp.concatenate(probs, axis=0), g)

        zero = jnp.zeros((2 * n, LANES), F32)
        dk, dv = over_chunks(total, body, (zero, zero))
        r.s_dk[:, lanes(p)] = unrotate(join_heads(dk) * SCALE, r.cos[...], r.sin[...]).astype(BF)
        r.s_dv[:, lanes(p)] = join_heads(dv).astype(BF)
    dq, dk, dv = r.dq[...], r.s_dk[...], r.s_dv[...]
    for i, v in enumerate((dq, dk, dv)):
        r.qkv_sums[i : i + 1, :] = column_sum(v)
    r.qkv_sums[3:8, :] = jnp.zeros((5, D), F32)
    mine, theirs, mine_y, theirs_y = zip(*[quarters(v, place[1], place[2]) for v in (dq, dk, dv)])
    for ref, v, above in ((r.qkv_near, mine, "above_near"), (r.qkv_send, theirs, "above_send"), (r.qkv_side, mine_y + theirs_y, "above_side")):
        ref[...] = cat(*v, r[above][...]) if above in r else cat(*v)


def input_back_phase(r, copies):
    total = r.pre_above[...]
    for name, ref in (("wq", r.dq), ("wk", r.s_dk), ("wv", r.s_dv)):
        copies.wait(name)
        total = total + dot_nt(ref[...], r["m_" + name][...])
    return total


def layer_forward(layer, place, x, blocks, weights, bi, vec, cos, sin, own_seg, all_seg, qkv=None, cotangent=None, after=()):
    n = x.shape[0]
    total = all_seg.shape[1]
    last = cotangent is not None
    names = ("wo", "wi", "wu") if qkv else ("wk", "wv", "wq", "wo", "wi", "wu")
    ins = Names(place=place, x=x, own=own_seg, all=all_seg, bi=bi[layer], vec=vec[layer])
    ins.update({"w_" + name: weights[name] for name in names})
    hbm = {"w_" + name for name in names}
    outs = Names(attn=sds((n, D), F32), lse=sds((n, LANES), F32), result_b=sds((n, D), BF))
    scratch = Names(
        s_hidden=pltpu.VMEM((n, D), BF), s_active=pltpu.VMEM((n, FF), BF), **rooms(names),
    )
    inner = Names(
        n1=sds((n, D), F32), n2=sds((n, D), F32), stat=sds((n, LANES), F32), slope=sds((n, FF), BF),
    )
    flops = 2 * n * (D * D + 2 * D * FF) + 4 * n * total * D * 2
    if qkv:
        ins.update(zip(("s_q", "s_k", "s_v"), qkv))
    else:
        ins.update(blocks=blocks, cos=cos, sin=sin)
        for name in "qkv":
            outs[name] = sds((total, D), BF)
            hbm.add(name)
            if name != "q":
                outs["own_" + name] = sds((n, D), BF)
            scratch["s_" + name] = pltpu.VMEM((total, D), BF)
        scratch.s_rows = pltpu.VMEM((total, D), BF)
        scratch.out_sems = pltpu.SemaphoreType.DMA((3,))
        flops += 6 * total * D * D
    if last:
        scratch.update({k: pltpu.VMEM(v.shape, v.dtype) for k, v in inner.items()})
        scratch.s_inner = pltpu.VMEM((n, FF), BF)
        ins.cotangent = cotangent
        outs.update(feed_back_outs(n, True))
        flops += 2 * n * (D * D + 2 * D * FF)
    else:
        outs.update(inner)
        outs.result = sds((n, D), F32)
        outs.update(keep_pack=sds((n, PACK), BF), side=sds((n, 2 * D), BF), active=sds((n, FF // 2), BF))

    def kernel(r):
        copies = Copies(r.sems)
        copies.weights(r, layer, names)
        if not qkv:
            join(r.s_rows, r.blocks, slice(0, D))
            qkv_phase(r, copies)
            back = Copies(r.out_sems)
            for name in "qkv":
                back.start(name, r["s_" + name], r[name])
            for name in "kv":
                r["own_" + name][...] = r["s_" + name][:n, :]
        attend_phase(r)
        result = ffn_phase(r, copies)
        r.result_b[...] = result.astype(BF)
        x = r.place[0]
        if last:
            feed_back_phase(r, copies, r.cotangent[...].astype(F32))
            for ref, at in ((r.near, NEAR_PACK), (r.send, NEAR_PACK)):
                ref[:, NEAR:NEAR_PACK] = jnp.zeros((n, NEAR_PACK - NEAR), BF)
                store_pack(r, ref, at, x)
            r.to_y[:, SIDE : SIDE + D] = r.s_hidden[...]
            r.to_y[:, SIDE + D :] = r.attn[...].astype(BF)
            store_active(r, r.to_x, D, 1 - x)
        else:
            r.result[...] = result
            store_pack(r, r.keep_pack, 0, x)
            r.side[:, :D] = r.s_hidden[...]
            r.side[:, D:] = r.attn[...].astype(BF)
            store_active(r, r.active, 0, 1 - x)
        if not qkv:
            back.wait(*"qkv")

    return mega(kernel, "forward_last" if last else "forward", ins, outs, scratch, flops, hbm=hbm, after=after)


def feed_back_outs(n, last):
    return Names(
        near=sds((n, NEAR_PACK + PACK if last else NEAR), BF), send=sds((n, NEAR_PACK + PACK), BF),
        to_x=sds((n, D + FF // 2 if last else D), BF), to_y=sds((n, SIDE + 2 * D if last else SIDE), BF),
        pre=sds((n, D), F32), pack=sds((n, D + LANES), BF), delta=sds((n, LANES), F32),
        sums=sds((16, D), F32),
    )


def layer_back(layer, place, kept, back, dq, blocks, weights, vec, cos, sin, own_seg, all_seg, below=None, far=(), after=()):
    n, total = dq.shape[0], all_seg.shape[1]
    names = ("wq", "wk", "wv") + (("wo", "wi", "wu") if below else ())
    ins = Names(
        place=place, k=kept.own_k, v=kept.own_v, q=kept.q, dq=dq, pre_above=back.pre, blocks=blocks,
        own=own_seg, all=all_seg, cos=cos, sin=sin,
    )
    ins.update({"w_" + name: weights[name] for name in names})
    hbm = {"w_" + name for name in names} | {"q"}
    single = len(blocks) == 1
    if single:
        hbm.add("blocks")
    wide = 1 if below else 2
    outs = Names(
        qkv_near=sds((n, wide * QKV), BF), qkv_send=sds((n, wide * QKV), BF), qkv_side=sds((n, wide * 2 * QKV), BF), qkv_sums=sds((8, D), F32),
        dk=sds((n, D), BF), dv=sds((n, D), BF),
    )
    scratch = Names(
        s_q=pltpu.VMEM((total, D), BF), s_g=pltpu.VMEM((total, D), BF), s_extra=pltpu.VMEM((total, LANES), BF),
        s_stats=pltpu.VMEM((32, total), F32), s_dk=pltpu.VMEM((n, D), BF), s_dv=pltpu.VMEM((n, D), BF),
        q_sems=pltpu.SemaphoreType.DMA((PAIRS + 2,)), **rooms(names),
    )
    if below:
        ins.update({k: below[k] for k in ("n1", "n2", "stat", "slope", "attn", "lse")}, vec=vec[layer - 1])
        outs.update(feed_back_outs(n, False))
        ins.far = list(far)
        scratch.s_inner = pltpu.VMEM((n, FF), BF)
    else:
        outs.grad = sds((n, D), BF)
        ins.update(above_near=back.qkv_near, above_send=back.qkv_send, above_side=back.qkv_side)

    def kernel(r):
        queries = Copies(r.q_sems)
        if single:
            queries.start("g", r.blocks[0].at[:, :D], r.s_g)
            queries.start("extra", r.blocks[0].at[:, D:], r.s_extra)
        for p in range(PAIRS):
            queries.start(f"q{p}", r.q.at[:, lanes(p)], r.s_q.at[:, lanes(p)])
        copies = Copies(r.sems)
        copies.weights(r, layer, names[:3])
        if below:
            copies.weights(r, layer - 1, names[3:])
        if single:
            queries.wait("g", "extra")
        else:
            join(r.s_g, r.blocks, slice(0, D))
            join(r.s_extra, r.blocks, slice(D, D + LANES))
        key_back_phase(r, queries)
        r.dk[...] = r.s_dk[...]
        r.dv[...] = r.s_dv[...]
        grad = input_back_phase(r, copies)
        if below:
            feed_back_phase(r, copies, grad)
            r.send[:, NEAR:NEAR_PACK] = jnp.zeros((n, NEAR_PACK - NEAR), BF)
            for i, ref in enumerate(r.far):
                at = NEAR_PACK + i * 2 * D
                r.send[:, at : at + 2 * D] = ref[...]
        else:
            r.grad[...] = grad.astype(BF)

    flops = 8 * n * total * D * 2 + 6 * n * D * D + (2 * n * (D * D + 2 * D * FF) if below else 0)
    return mega(kernel, "layer_back" if below else "layer_back_first", ins, outs, scratch, flops, hbm=hbm, after=after)


def feed_pieces(place, packs, near, side, cross, after=(), vmem=32):
    n = near[0].shape[0]
    here, there = packs
    ins = Names(
        place=place, here=[a for a, _ in here], att=[a for a, _, _, _ in there], act=[a for _, _, a, _ in there],
        near=list(near), side=list(side), cross=list(cross),
    )
    io, u = sds((4, WIDTH, IO), BF), sds((4, WIDTH, 2 * ACTIVE), BF)
    scratch = Names(
        t_hidden=pltpu.VMEM((D, 4 * n), BF), t_attn=pltpu.VMEM((D, 4 * n), BF), t_outer=pltpu.VMEM((2, CHUNK, 4 * n), BF),
    )

    def kernel(r):
        hidden = [(ref, at) for ref, (_, at) in zip(r.here, here)] + [(ref, at) for ref, (_, at, _, _) in zip(r.att, there)]
        turned(r.t_hidden, *[ref[:, at : at + D] for ref, at in hidden])
        turned(r.t_attn, *[ref[:, at + D : at + 2 * D] for ref, at in hidden])
        n0, n1 = r.near
        y0, y1 = r.side
        x0, x1 = r.cross
        inner = jnp.concatenate([n0[:, :FB], n1[:, :FB], y0[:, :FB], y1[:, FB : 2 * FB]], axis=0)
        out = jnp.concatenate(
            [n0[:, NEAR_OUT:NEAR], n1[:, NEAR_OUT:NEAR], y0[:, SIDE_OUT : SIDE_OUT + CHUNK], y1[:, SIDE_OUT + CHUNK : SIDE]], axis=0
        )
        x, y = r.place[0], r.place[1]
        for name, side_x in (("io_send", 1 - x), ("io_keep", x)):
            r[name][:, :, :FB] = dot(shard_rows(r.t_hidden, side_x), inner).astype(BF).reshape(4, WIDTH, FB)
            r[name][:, :, FB:] = dot(shard_rows(r.t_attn, side_x), out).astype(BF).reshape(4, WIDTH, CHUNK)
        sources = [(n0, NEAR_OUTER), (n1, NEAR_OUTER), (x0, 0), (x1, 2 * CHUNK)]
        for h in range(2):
            turned(r.t_outer.at[h], *[ref[:, at + h * CHUNK : at + (h + 1) * CHUNK] for ref, at in sources])
        active = [ref[:, at + 2 * D : at + PACK] for ref, (_, at) in zip(r.here, here)]
        active += [ref[:, at : at + FF // 2] for ref, (_, _, _, at) in zip(r.act, there)]
        active = jnp.concatenate(active, axis=0)
        for name, side_y in (("u_send", 1 - y), ("u_keep", y)):
            t = dot(r.t_outer[side_y], active).astype(BF)
            for z in range(4):
                part = t[:, z * ACTIVE : (z + 1) * ACTIVE]
                r[name][z, :, :ACTIVE] = part[:WIDTH]
                r[name][z, :, ACTIVE:] = part[WIDTH:]

    outs = Names(io_keep=io, io_send=io, u_keep=u, u_send=u)
    return mega(kernel, "feed_pieces", ins, outs, scratch, 8 * n * (D * IO + FF * CHUNK), after=after, vmem=vmem)


def qkv_pieces(place, blocks, near, side, after=()):
    n = near[0].shape[0]
    ins = Names(place=place, blocks=[b[k] for b in blocks for k in (0, 4, 2, 6)], near=list(near), side=list(side))
    o = sds((4, WIDTH, padded(QKV) + QKV), BF)

    def kernel(r):
        (g0, g1), (y0, y1) = r.near, r.side
        x = r.place[0]
        for layer in range(LAYERS):
            turned(r.t_rows.at[layer], *[ref[...] for ref in r.blocks[4 * layer : 4 * layer + 4]])
            parts = (g0, layer * QKV), (g1, layer * QKV), (y0, 2 * layer * QKV), (y1, (2 * layer + 1) * QKV)
            g = jnp.concatenate([ref[:, at : at + QKV] for ref, at in parts], axis=0)
            at = layer * padded(QKV)
            for name, side_x in (("send", 1 - x), ("keep", x)):
                found = dot(shard_rows(r.t_rows.at[layer], side_x), g).astype(BF)
                r[name][:, :, at : at + QKV] = found.reshape(4, WIDTH, QKV)

    scratch = Names(t_rows=pltpu.VMEM((LAYERS, D, 4 * n), BF))
    return mega(kernel, "qkv_pieces", ins, Names(keep=o, send=o), scratch, 16 * n * D * QKV, after=after, vmem=24)


def padded(w):
    return -(-w // LANES) * LANES


def first_sum(place, pairs, after=(), vmem=24):
    width = sum(padded(a.shape[2]) for a, _ in pairs)
    o = sds((2, WIDTH, width), BF)

    def kernel(r):
        bit = r.place[3] % 2
        for name, side in (("keep", bit), ("send", 1 - bit)):
            for i in range(2):
                at = 0
                for a, b in zip(r.own, r.got):
                    w = a.shape[2]
                    r[name][i, :, at : at + w] = (a[2 * i + side].astype(F32) + b[2 * i + side].astype(F32)).astype(BF)
                    at += padded(w)

    ins = Names(place=place, own=[a for a, _ in pairs], got=[b for _, b in pairs])
    return mega(kernel, "first_sum", ins, Names(keep=o, send=o), {}, 1000, after=after, vmem=vmem)


def second_sum(place, keep, got, after=()):
    o = sds(keep.shape[1:], BF)

    def kernel(r):
        bit = r.place[3] // 2
        for name, side in (("keep", bit), ("send", 1 - bit)):
            r[name][...] = (r.own[side].astype(F32) + r.got[side].astype(F32)).astype(BF)

    return mega(kernel, "second_sum", Names(place=place, own=keep, got=got), Names(keep=o, send=o), {}, 1000, after=after, vmem=24)


FEED_SHAPES = Names(inner=(WIDTH, FB), out=(WIDTH, CHUNK), outer=(CHUNK, ACTIVE))
QKV_SHAPES = Names(query=(WIDTH, CHUNK), key=(WIDTH, CHUNK), value=(WIDTH, CHUNK))


def last_feed(layers):
    outs = Names((k, sds((LAYERS,) + v, F32)) for k, v in FEED_SHAPES.items())

    def kernel(r):
        for layer, (a, b) in enumerate(zip(r.own, r.got)):
            total = a[...].astype(F32) + b[...].astype(F32)
            r.inner[layer] = total[:, :FB]
            r.out[layer] = total[:, FB:IO]
            r.outer[layer, :WIDTH] = total[:, IO_PAD : IO_PAD + ACTIVE]
            r.outer[layer, WIDTH:] = total[:, IO_PAD + ACTIVE :]

    return mega(kernel, "last_feed", Names(own=[a for a, _ in layers], got=[b for _, b in layers]), outs, {}, 1000, vmem=24)


def last_qkv(keep, got):
    outs = Names((k, sds((LAYERS,) + v, F32)) for k, v in QKV_SHAPES.items())

    def kernel(r):
        total = r.own[...].astype(F32) + r.got[...].astype(F32)
        for layer in range(LAYERS):
            for i, name in enumerate(QKV_SHAPES):
                at = layer * padded(QKV) + i * CHUNK
                r[name][layer] = total[:, at : at + CHUNK]

    return mega(kernel, "last_qkv", Names(own=keep, got=got), outs, {}, 1000, vmem=24)


def linear(z, x, y, c):
    return (z * 2 + x) * 4 + y * 2 + c


PLACES = [(z, x, y, c) for z in range(4) for x in range(2) for y in range(2) for c in range(2)]


def move(array, where):
    pairs = [(linear(*place), linear(*where(*place))) for place in PLACES]
    return lax.ppermute(array, BOTH, pairs)


def to_plane(z, x, y, c):
    return (2 * y + c, x, z >> 1, z & 1)


def other_core(z, x, y, c):
    return (z, x, y, 1 - c)


def other_x(z, x, y, c):
    return (z, 1 - x, y, c)


def other_y(z, x, y, c):
    return (z, x, 1 - y, c)


def other_xy(z, x, y, c):
    return (z, 1 - x, 1 - y, c)


def near_z(z, x, y, c):
    return (z ^ 1, x, y, c)


def far_z(z, x, y, c):
    return (z ^ 2, x, y, c)


def gate(arrays, *others):
    return lax.optimization_barrier((arrays, others))[0]


def pick(array, index, axis):
    return lax.dynamic_index_in_dim(array, index, axis, keepdims=False)


class Small:
    def __init__(self):
        seq, rows = lax.axis_index("seq"), lax.axis_index("rows")
        self.z, self.x, self.y, self.c = seq // 2, seq % 2, rows // 2, rows % 2
        self.spot = jnp.stack([self.x, self.y, self.c, self.z]).astype(jnp.int32)

    def share_few(self, mine):
        far = jnp.concatenate(mine[1:], axis=0)
        return [mine[0], far, move(mine[0], other_core), move(far, other_core)]

    def starts(self, count):
        out = []
        for dc in (0, 1):
            for dx, dy in ((0, 0), (1, 0), (0, 1), (1, 1)):
                x, y, c = self.x ^ dx, self.y ^ dy, self.c ^ dc
                out.append(((2 * y + c) * 2 + x) * count)
        return jnp.stack(out)

    def reach(self, array):
        return [array, move(array, other_x), move(array, other_y), move(array, other_xy)]

    def share(self, mine):
        return mine + [move(a, other_core) for a in mine]


class Large:
    def __init__(self):
        self.shards = lax.axis_size("seq")
        self.spot = jnp.zeros((4,), jnp.int32)

    def starts(self, count):
        me = lax.axis_index("seq")
        return (me + jnp.arange(self.shards, dtype=jnp.int32)) % self.shards * count

    def gather(self, array):
        whole_row = lax.all_gather(array, "seq", axis=0, tiled=True)
        return [jnp.roll(whole_row, -lax.axis_index("seq") * array.shape[0], axis=0)]

    def spread(self, left, right):
        grad = lax.dot_general(left, right, (((0,), (0,)), ((), ())), preferred_element_type=F32).astype(BF)
        grad = lax.psum_scatter(grad, "seq", scatter_dimension=0, tiled=True)
        return lax.psum_scatter(grad, "rows", scatter_dimension=1, tiled=True).astype(F32)

    def grads(self, kept, back, tail, dq):
        near, send, to_x, to_y = back.near, back.send, back.to_x, back.to_y
        inner = cat(near[:, :FB], send[:, :FB], to_y[:, : 2 * FB])
        out = cat(near[:, NEAR_OUT:NEAR], send[:, NEAR_OUT:NEAR], to_y[:, SIDE_OUT:SIDE])
        outer = cat(*[to_x[:, i * CHUNK : (i + 1) * CHUNK] for i in (0, 2, 1, 3)])
        if "active" in kept:
            hidden, attn = kept.side[:, :D], kept.side[:, D:]
            mine, other = kept.keep_pack[:, 2 * D :], kept.active
        else:
            hidden, attn = to_y[:, SIDE : SIDE + D], to_y[:, SIDE + D :]
            mine, other = near[:, NEAR_PACK + 2 * D :], to_x[:, D:]
        active = jnp.stack([v.reshape(-1, 4, ACTIVE) for v in (mine, other)], axis=2).reshape(-1, FF)
        own = kept.blocks[0][: dq.shape[0]]
        return Names(
            inner=self.spread(hidden, inner), out=self.spread(attn, out), outer=self.spread(active, outer),
            query=self.spread(own, dq), key=self.spread(own, tail.dk), value=self.spread(own, tail.dv),
        )


def doc_layout(lengths_row, index):
    ends = jnp.cumsum(lengths_row, dtype=jnp.int32)
    passed = (index[:, None] >= ends[None, :]).astype(jnp.int32)
    segment = jnp.sum(passed, axis=1, dtype=jnp.int32)
    begin = jnp.sum(passed * lengths_row[None, :], axis=1, dtype=jnp.int32)
    return (segment, (index - begin).astype(jnp.int32))


def rotary_tables(position):
    lane = jnp.arange(LANES, dtype=jnp.int32)
    pairs = (lane % HEAD_DIM // 2).astype(F32)
    inverse = jnp.power(jnp.float32(10000.0), -2.0 * pairs / HEAD_DIM)
    angle = position.astype(F32)[:, None] * inverse[None, :]
    return jnp.cos(angle), jnp.sin(angle) * jnp.where(lane % 2 == 0, -1.0, 1.0)[None, :]


def both_cores(array):
    return array, move(array, other_core)


def all_sums(two, tail_two, one, tail_one):
    return jnp.concatenate([one.sums[:10], tail_one.qkv_sums[:3], two.sums[:10], tail_two.qkv_sums[:3]], axis=0)


VECTOR_ROWS = Names(g2=0, c2=1, bu=2, g1=3, c1=4, bo=5, bq=10, bk=11, bv=12)
LAYER_ROWS = 13


def last_vectors(place, own, got, whole):
    outs = Names((name, sds((LAYERS, WIDTH), F32)) for name in VECTOR_ROWS)
    outs.bi = sds((LAYERS, ACTIVE), F32)
    outs.passed = [sds(a.shape, a.dtype) for a in whole]

    def kernel(r):
        for a, b in zip(r.whole, r.passed):
            b[...] = a[...]
        x, z = r.place[0], r.place[3]
        total = r.own[...] + r.got[...]
        r.s_total[...] = total
        shard = 2 * z + x
        turn = pltpu.roll(total, (D - shard * WIDTH) % D, 1)[:, :WIDTH]
        for layer in range(LAYERS):
            for name, row in VECTOR_ROWS.items():
                at = LAYER_ROWS * layer + row
                r[name][layer : layer + 1, :] = turn[at : at + 1]
            row = r.s_total[pl.ds(LAYER_ROWS * layer + 6 + z, 1), :]
            r.bi[layer : layer + 1, :] = jnp.where(x == 0, row[:, :ACTIVE], row[:, ACTIVE:])

    scratch = Names(s_total=pltpu.VMEM(own.shape, F32))
    return mega(kernel, "last_vectors", Names(place=place, own=own, got=got, whole=list(whole)), outs, scratch, 1000, vmem=24)


class Program:
    def __init__(self, place, spot, lengths_row, n, starts, params):
        wq, bq, wk, bk, wv, bv, wo, bo, g1, c1, wi, bi, wu, bu, g2, c2 = params
        self.weights = Names(wq=wq, wk=wk, wv=wv, wo=wo, wi=wi, wu=wu)
        self.spot, self.n = spot, n
        self.vec = jnp.stack([bq, bk, bv, bo, g1, c1, bu, g2, c2], axis=1).astype(F32)
        self.bi = bi.astype(F32)[:, None, :]
        index = (starts[:, None] + jnp.arange(n, dtype=jnp.int32)).reshape(-1)
        segment, position = doc_layout(lengths_row, index)
        self.segments = segment[:n, None], segment[None, :]
        self.cos, self.sin = rotary_tables(position)
        self.own_cos, self.own_sin = rotary_tables(position[:n])

    def project(self, layer, rows):
        w = self.weights
        return project(rows, layer, w["wq"], w["wk"], w["wv"], self.vec, self.cos, self.sin)

    def forward(self, layer, x, blocks, qkv=None, cotangent=None, after=()):
        kept = layer_forward(
            layer, self.spot, x, blocks, self.weights, self.bi, self.vec, self.cos, self.sin, *self.segments, qkv, cotangent, after
        )
        kept.blocks = blocks
        if qkv:
            kept.update(zip("qkv", qkv), own_k=qkv[1][: self.n], own_v=qkv[2][: self.n])
        return kept

    def queries(self, kept, back, after=()):
        return query_back(
            kept.q, kept.k, kept.v, back.pack, kept.lse, back.delta, *self.segments, self.own_cos, self.own_sin, after
        )[0]

    def back(self, layer, kept, back, dq, packs, below=None, far=(), after=()):
        return layer_back(
            layer, self.spot, kept, back, dq, packs, self.weights, self.vec, self.own_cos, self.own_sin, *self.segments, below, far, after
        )


def large_body(tokens, lengths, cotangent, *params):
    place = Large()
    n = tokens.shape[1]
    run = Program(place, place.spot, lengths[0], n, place.starts(n), params)

    def step(layer, x, x_b, cotangent=None):
        blocks = place.gather(x_b)
        return run.forward(layer, x, blocks, run.project(layer, blocks[0]), cotangent)

    first = step(0, tokens[0], tokens[0])
    second = step(1, first.result, first.result_b, cotangent[0])
    dq_two = run.queries(second, second)
    back_one = run.back(1, second, second, dq_two, place.gather(second.pack), first)
    dq_one = run.queries(first, back_one)
    back_none = run.back(0, first, back_one, dq_one, place.gather(back_one.pack))
    grads_one = place.grads(first, back_one, back_none, dq_one)
    grads_two = place.grads(second, second, back_one, dq_two)
    m = Names((name, jnp.stack([grads_one[name], grads_two[name]])) for name in grads_one)
    total = lax.psum(all_sums(second, back_one, back_one, back_none), BOTH).reshape(LAYERS, LAYER_ROWS, D)
    me, shards = lax.axis_index("seq"), lax.axis_size("seq")
    v = Names(
        (name, lax.dynamic_slice_in_dim(total[:, row], me * (D // shards), D // shards, 1))
        for name, row in VECTOR_ROWS.items()
    )
    v.bi = lax.dynamic_slice_in_dim(total[:, 6:10].reshape(LAYERS, FF), me * (FF // shards), FF // shards, 1)
    return result(second.result_b, back_none.grad, m, v)


def small_body(tokens, lengths, cotangent, *params):
    place = Small()
    spot, n = place.spot, tokens.shape[1]
    current = move(tokens[0], to_plane)
    run = Program(place, spot, move(lengths, to_plane)[0], n, place.starts(n), params)
    blocks = place.share(gate(place.reach(current), run.cos, run.sin, run.own_cos, run.own_sin, run.vec, run.bi))
    grad = move(gate(cotangent[0], current), to_plane)
    first = run.forward(0, current, blocks, after=(grad,))
    a_near = both_cores(first.keep_pack)
    blocks = place.share(place.reach(first.result_b))
    side, active = gate((first.side, first.active), blocks)
    a_side, a_cross = move(side, other_y), move(active, other_x)
    second = run.forward(1, first.result, blocks, cotangent=grad, after=(a_near[1],))

    reached = place.reach(second.pack)
    dq_two = run.queries(second, second, after=(a_side, a_cross))
    packs = place.share(gate(reached, dq_two))
    to_y, to_x, send, result_b = gate((second.to_y, second.to_x, second.send, second.result_b), packs)
    from_y, from_x, near = move(to_y, other_y), move(to_x, other_x), (second.near, move(send, other_core))
    output = move(result_b, to_plane)
    back_one = run.back(1, second, second, dq_two, packs, first, (a_side, a_cross))

    pack, from_y, from_x, near_got = gate((back_one.pack, from_y, from_x, near[1]), output)
    near = near[0], near_got
    reached = place.reach(pack)
    side, cross = [both_cores(a) for a in gate((from_y, from_x), pack)]
    dq_one = run.queries(first, back_one)
    packs = place.share_few(gate(reached, dq_one))
    to_y, to_x = gate((back_one.to_y, back_one.to_x), reached, dq_one)
    one_y, one_x = move(to_y, other_y), move(to_x, other_x)
    there = [(a, SIDE, b, D) for a, b in zip(side, cross)]
    two = feed_pieces(spot, ([(a, NEAR_PACK) for a in near], there), near, side, cross, after=(dq_one, *reached), vmem=60)
    two_io, two_u = move(two.io_send, other_x), move(two.u_send, other_y)
    near = back_one.near, move(gate(back_one.send, reached, dq_one), other_core)
    back_none = run.back(0, first, back_one, dq_one, packs, after=(two.io_send, near[1], one_x))

    two_sum = first_sum(spot, ((two.io_keep, two_io), (two.u_keep, two_u)), vmem=60, after=(back_none.grad, one_y, near[1]))
    side, cross = [both_cores(a) for a in gate((one_y, one_x), back_none.grad)]
    q_side = move(back_none.qkv_side, other_y)
    tokens_grad = move(back_none.grad, to_plane)
    sums = all_sums(second, back_one, back_one, back_none)
    from_sums = move(sums, other_core)
    two_near = move(two_sum.send, near_z)
    there = [(a_side, 0, a_cross, 0), (near[1], NEAR_PACK, near[1], NEAR_PACK + 2 * D)]
    one = feed_pieces(spot, ([(a, 0) for a in a_near], there), near, side, cross, after=(two_sum.send, tokens_grad))
    one_io, one_u = move(one.io_send, other_x), move(one.u_send, other_y)
    sums = gate(sums + from_sums, two_sum.send)
    from_sums = move(sums, near_z)
    qkv_send, q_side = gate((back_none.qkv_send, q_side), one.io_send)
    q_near, q_side = (back_none.qkv_near, move(qkv_send, other_core)), both_cores(q_side)
    qkv = qkv_pieces(spot, (first.blocks, second.blocks), q_near, q_side, after=(one.io_send, from_sums))
    q_x = move(qkv.send, other_x)
    two_z = second_sum(spot, two_sum.keep, two_near, after=(qkv.send, one_io))
    two_far = move(two_z.send, far_z)
    sums = gate(sums + from_sums, qkv.send)
    from_sums = move(sums, far_z)
    one_sum = first_sum(spot, ((one.io_keep, one_io), (one.u_keep, one_u)), after=(two_z.send, from_sums))
    one_near = move(one_sum.send, near_z)
    sums = gate(sums + from_sums, one_sum.send)
    from_sums = move(sums, other_x)
    q_sum = first_sum(spot, ((qkv.keep, q_x),), after=(one_sum.send, two_far))
    q_near = move(q_sum.send, near_z)
    sums = gate(sums + from_sums, q_sum.send)
    from_sums = move(sums, other_y)
    one_z = second_sum(spot, one_sum.keep, one_near, after=(q_sum.send,))
    one_far = move(one_z.send, far_z)
    q_z = second_sum(spot, q_sum.keep, q_near, after=(one_z.send,))
    q_far = move(q_z.send, far_z)
    v = last_vectors(spot, sums, from_sums, (output, tokens_grad))
    m = last_feed(((one_z.keep, one_far), (two_z.keep, two_far)))
    m.outer = m.outer.swapaxes(1, 2)
    m.update(last_qkv(q_z.keep, q_far))
    return result(*v.passed, m, v)


def result(output, tokens_grad, m, v):
    return (
        output[None], tokens_grad[None],
        m.query, v.bq, m.key, v.bk, m.value, v.bv, m.out, v.bo, v.g1, v.c1,
        m.inner, v.bi, m.outer, v.bu, v.g2, v.c2,
    )


def solution(mesh):
    token = P("rows", "seq", None)
    mat, vec = P(None, "seq", "rows"), P(None, "seq")
    small = (mesh.shape["seq"], mesh.shape["rows"]) == (8, 4)
    return jax.shard_map(
        small_body if small else large_body,
        mesh=mesh,
        in_specs=(token, P("rows", None), token) + (P(),) * 16,
        out_specs=(token, token, mat, vec, mat, vec, mat, vec, mat, vec, vec, vec, mat, vec, mat, vec, vec, vec),
        check_vma=False,
    )
```

```python
import jax
import jax.numpy as jnp
from jax import lax
from jax.experimental import pallas as pl
from jax.experimental.pallas import tpu as pltpu
from jax.sharding import PartitionSpec as P

D = 768
HEADS = 12
HEAD_DIM = 64
FF = 3072
LAYERS = 2
LANES = 128
PAIRS = D // LANES
CHUNK = D // 4
NEG_FILL = -1e30
NORM_EPS = 1e-12
SCALE = HEAD_DIM**-0.5
BF = jnp.bfloat16
F32 = jnp.float32
BOTH = ("seq", "rows")
MIB = 1 << 20

BQ, BK, BV, BO, G1, C1, BU, G2, C2 = range(9)
FB = 768
WIDTH = D // 8
ACTIVE = FF // 8
QKV = 3 * CHUNK
IO = FB + CHUNK
IO_PAD = FB + 2 * LANES

NEAR_OUTER, NEAR_OUT, NEAR = FB, FB + 2 * CHUNK, FB + 3 * CHUNK
NEAR_PACK = NEAR + 64
SIDE_OUT, SIDE = 2 * FB, 2 * FB + 2 * CHUNK
PACK = 2 * D + FF // 2

LSE, DELTA, PIECE = 0, 48, 16


class Names(dict):
    __getattr__ = dict.__getitem__
    __setattr__ = dict.__setitem__


def dot(a, b):
    return jnp.dot(a, b, preferred_element_type=F32)


def dot_nt(a, b):
    return lax.dot_general(a, b, (((1,), (1,)), ((), ())), preferred_element_type=F32)


def call(kernel, name, grid, in_specs, out_specs, out_shape, args, flops, scratch=(), scalars=(), vmem=60, after=(), aliases=None):
    size = sum(a.size * a.dtype.itemsize for a in args) + sum(
        s.size * s.dtype.itemsize for s in jax.tree.leaves(out_shape)
    )
    lead, many = len(scalars) + len(args), len(after)

    def run(*refs):
        kernel(*refs[:lead], *refs[lead + many :])

    return pl.pallas_call(
        run,
        name=name,
        grid_spec=pltpu.PrefetchScalarGridSpec(
            num_scalar_prefetch=len(scalars),
            grid=grid,
            in_specs=list(in_specs) + [pl.BlockSpec(memory_space=pl.ANY)] * many,
            out_specs=out_specs,
            scratch_shapes=list(scratch),
        ),
        out_shape=out_shape,
        input_output_aliases=aliases or {},
        compiler_params=pltpu.CompilerParams(
            dimension_semantics=("arbitrary",) * len(grid), vmem_limit_bytes=vmem * MIB
        ),
        cost_estimate=pl.CostEstimate(flops=int(flops), bytes_accessed=int(size), transcendentals=0),
    )(*scalars, *args, *after)


def whole(array):
    return pl.BlockSpec(array.shape, lambda *_: (0,) * array.ndim)


def layer_block(array, layer):
    return pl.BlockSpec((None,) + array.shape[1:], lambda *_: (layer,) + (0,) * (array.ndim - 1))


def sds(shape, dtype):
    return jax.ShapeDtypeStruct(shape, dtype)


def lane_is_even(shape):
    return lax.broadcasted_iota(jnp.int32, shape, 1) % 2 == 0


def swap_pairs(v):
    return jnp.where(lane_is_even(v.shape), pltpu.roll(v, LANES - 1, 1), pltpu.roll(v, 1, 1))


def lanes(j):
    return slice(j * LANES, (j + 1) * LANES)


def qkv_kernel(x_ref, wq_ref, wk_ref, wv_ref, vec_ref, cos_ref, sin_ref, q_ref, k_ref, v_ref):
    x, cos, sin = x_ref[...], cos_ref[...], sin_ref[...]
    for w_ref, row, o_ref in ((wq_ref, BQ, q_ref), (wk_ref, BK, k_ref)):
        y = dot(x, w_ref[...]) + vec_ref[row : row + 1, :]
        for j in range(PAIRS):
            t = y[:, lanes(j)]
            o_ref[:, lanes(j)] = (t * cos + swap_pairs(t) * sin).astype(BF)
    v_ref[...] = (dot(x, wv_ref[...]) + vec_ref[BV : BV + 1, :]).astype(BF)


def project(rows, layer, wq, wk, wv, vec, cos, sin):
    total = rows.shape[0]
    block = min(256, total)
    tok = lambda w: pl.BlockSpec((block, w), lambda i: (i, 0))
    return call(
        qkv_kernel, "qkv", (total // block,),
        [tok(D)] + [layer_block(w, layer) for w in (wq, wk, wv, vec)] + [tok(LANES), tok(LANES)],
        [tok(D)] * 3, [sds((total, D), BF)] * 3,
        (rows, wq, wk, wv, vec, cos, sin), 6 * total * D * D,
    )


def over_chunks(total, body, carry):
    size = min(total, 1024)
    if size == total:
        return body(slice(None), carry)
    return lax.fori_loop(
        0, total // size, lambda i, c: body(pl.ds(pl.multiple_of(i * size, size), size), c), carry
    )


def two_heads(v):
    low = lax.broadcasted_iota(jnp.int32, v.shape, 1) < HEAD_DIM
    zero = jnp.zeros_like(v)
    return jnp.concatenate([jnp.where(low, v, zero), jnp.where(low, zero, v)], axis=0)


def join_heads(v):
    n = v.shape[0] // 2
    low = lax.broadcasted_iota(jnp.int32, (n, LANES), 1) < HEAD_DIM
    return jnp.where(low, v[:n], v[n:])


def normalize(values):
    centered = values - jnp.mean(values, axis=-1, keepdims=True)
    rstd = lax.rsqrt(jnp.mean(centered * centered, axis=-1, keepdims=True) + NORM_EPS)
    return centered * rstd, rstd


def column_sum(v):
    return jnp.sum(v.astype(F32), axis=0, keepdims=True)


def norm_back(grad, normed, rstd, gain):
    scaled = grad * gain
    centered = scaled - jnp.mean(scaled, axis=-1, keepdims=True)
    return rstd * (centered - normed * jnp.mean(scaled * normed, axis=-1, keepdims=True))


def either(first, a, b):
    return jnp.where(first, a, b), jnp.where(first, b, a)


def cat(*parts):
    return jnp.concatenate(parts, axis=1)


def quarters(v, y, c):
    part = [v[:, k * CHUNK : (k + 1) * CHUNK] for k in range(4)]
    mine0, theirs0 = either(c == 0, part[0], part[1])
    mine1, theirs1 = either(c == 0, part[2], part[3])
    mine, mine_y = either(y == 0, mine0, mine1)
    theirs, theirs_y = either(y == 0, theirs0, theirs1)
    return mine, theirs, mine_y, theirs_y


def hi_lo(v):
    hi = v.astype(BF)
    return hi, (v - hi.astype(F32)).astype(BF)


def unrotate(v, cos, sin):
    t = v * sin
    return v * cos + swap_pairs(t)


def lane_of(v, lane):
    at = lax.broadcasted_iota(jnp.int32, v.shape, 1)
    return jnp.sum(jnp.where(at == lane, v, 0.0), axis=1, keepdims=True)


def query_back_kernel(
    q_ref, k_ref, v_ref, g_ref, lse_ref, delta_ref, own_ref, all_ref, cos_ref, sin_ref,
    dq_ref, sum_ref,
):
    pair = pl.program_id(0)
    n, total = q_ref.shape[0], k_ref.shape[0]
    q = two_heads(q_ref[...] * jnp.asarray(SCALE, BF))
    g = two_heads(g_ref[...])
    own = own_ref[...]
    lse = jnp.concatenate([lane_of(lse_ref[...], 2 * pair), lane_of(lse_ref[...], 2 * pair + 1)], axis=0)
    delta = jnp.concatenate([lane_of(delta_ref[...], 2 * pair), lane_of(delta_ref[...], 2 * pair + 1)], axis=0)

    def body(at, acc):
        same = own == all_ref[:, at]
        k = k_ref[at, :]
        s = jnp.where(jnp.concatenate([same, same], axis=0), dot_nt(q, k) - lse, NEG_FILL)
        ds = (jnp.exp(s) * (dot_nt(g, v_ref[at, :]) - delta)).astype(BF)
        return acc + dot(ds, k)

    acc = join_heads(over_chunks(total, body, jnp.zeros((2 * n, LANES), F32))) * SCALE
    dq = unrotate(acc, cos_ref[...], sin_ref[...]).astype(BF)
    dq_ref[...] = dq
    sum_ref[...] = column_sum(dq)


def query_back(q, k, v, pack, lse, delta, own_seg, all_seg, cos, sin, after=()):
    n, total = pack.shape[0], k.shape[0]
    own = pl.BlockSpec((n, LANES), lambda p: (0, p))
    row = pl.BlockSpec((total, LANES), lambda p: (0, p))
    fixed = lambda w: pl.BlockSpec((n, w), lambda p: (0, 0))
    return call(
        query_back_kernel, "query_back", (PAIRS,),
        [own, row, row, own, fixed(LANES), fixed(LANES), whole(own_seg), whole(all_seg), fixed(LANES), fixed(LANES)],
        [own, pl.BlockSpec((1, LANES), lambda p: (0, p))],
        [sds((n, D), BF), sds((1, D), F32)],
        (q, k, v, pack, lse, delta, own_seg, all_seg, cos, sin), 6 * n * total * D * 2, after=after,
    )


def turned(ref, *parts):
    n = parts[0].shape[0]
    for i, part in enumerate(parts):
        ref[:, i * n : (i + 1) * n] = part.T


def shard_rows(ref, x):
    width = WIDTH
    return jnp.concatenate(
        [ref[pl.ds(pl.multiple_of((2 * z + x) * width, 32), width), :] for z in range(4)], axis=0
    )


def mega(kernel, name, ins, outs, scratch, flops, hbm=(), after=(), vmem=60):
    flat_in, tree_in = jax.tree.flatten(dict(ins))
    flat_out, tree_out = jax.tree.flatten(dict(outs))

    def spec_of(key):
        space = pl.ANY if key in hbm else pltpu.SMEM if key == "place" else pltpu.VMEM
        return pl.BlockSpec(memory_space=space)

    specs_in = jax.tree.leaves({k: jax.tree.map(lambda _: spec_of(k), v) for k, v in ins.items()})
    specs_out = jax.tree.leaves({k: jax.tree.map(lambda _: spec_of(k), v) for k, v in outs.items()})
    many_in, many_out = len(flat_in), len(flat_out)

    def run(*refs):
        lead = many_in + len(after)
        named = Names(tree_in.unflatten(refs[:many_in]))
        named.update(tree_out.unflatten(refs[lead : lead + many_out]))
        named.update(zip(scratch, refs[lead + many_out :]))
        kernel(named)

    size = sum(a.size * a.dtype.itemsize for a in flat_out) + sum(
        a.size * a.dtype.itemsize for k, v in ins.items() if k not in hbm for a in jax.tree.leaves(v)
    )
    out = pl.pallas_call(
        run,
        name=name,
        in_specs=specs_in + [pl.BlockSpec(memory_space=pl.ANY)] * len(after),
        out_specs=specs_out,
        out_shape=flat_out,
        scratch_shapes=list(scratch.values()),
        compiler_params=pltpu.CompilerParams(vmem_limit_bytes=vmem * MIB),
        cost_estimate=pl.CostEstimate(flops=int(flops), bytes_accessed=int(size), transcendentals=0),
    )(*flat_in, *after)
    return Names(tree_out.unflatten(out))


SHAPES = Names(wq=(D, D), wk=(D, D), wv=(D, D), wo=(D, D), wi=(D, FF), wu=(FF, D))


def rooms(names):
    found = Names(("m_" + name, pltpu.VMEM(SHAPES[name], BF)) for name in names)
    found.sems = pltpu.SemaphoreType.DMA((16,))
    return found


def units(j):
    return pl.ds(j * FB, FB)


class Copies:
    def __init__(self, sems):
        self.sems, self.copies = sems, {}

    def start(self, name, src, dst):
        self.copies[name] = pltpu.make_async_copy(src, dst, self.sems.at[len(self.copies)])
        self.copies[name].start()

    def weights(self, r, layer, names):
        for name in names:
            src, dst = r["w_" + name].at[layer], r["m_" + name]
            if name not in ("wi", "wu"):
                self.start(name, src, dst)
                continue
            for j in range(FF // FB):
                at = (slice(None), units(j)) if name == "wi" else (units(j), slice(None))
                self.start(f"{name}{j}", src.at[at], dst.at[at])

    def wait(self, *names):
        for name in names:
            if name in self.copies:
                self.copies.pop(name).wait()


def join(dst, refs, columns):
    at = 0
    for ref in refs:
        dst[at : at + ref.shape[0], :] = ref[:, columns]
        at += ref.shape[0]


def row_of(r, index):
    return r.vec[index : index + 1, :]


def qkv_phase(r, copies):
    rows, cos, sin = r.s_rows, r.cos, r.sin
    total = rows.shape[0]
    block = min(256, total)
    for name, bias in (("k", BK), ("v", BV), ("q", BQ)):
        copies.wait("w" + name)
        for i in range(total // block):
            at = pl.ds(i * block, block)
            y = dot(rows[at, :], r["m_w" + name][...]) + row_of(r, bias)
            if name == "v":
                r.s_v[at, :] = y.astype(BF)
                continue
            for j in range(PAIRS):
                t = y[:, lanes(j)]
                r["s_" + name][at, lanes(j)] = (t * cos[at, :] + swap_pairs(t) * sin[at, :]).astype(BF)


def attend_phase(r):
    n, total = r.attn.shape[0], r.s_k.shape[0]
    own = r.own[...]
    lane = lax.broadcasted_iota(jnp.int32, (n, LANES), 1)
    lse = jnp.zeros((n, LANES), F32)
    for p in range(PAIRS):
        q = two_heads(r.s_q[:n, lanes(p)] * jnp.asarray(SCALE, BF))

        def body(at, carry):
            top, tot, acc = carry
            same = own == r.all[:, at]
            s = dot_nt(q, r.s_k[at, lanes(p)])
            s = jnp.where(jnp.concatenate([same, same], axis=0), s, NEG_FILL)
            fresh = jnp.maximum(top, jnp.max(s, axis=1, keepdims=True))
            e = jnp.exp(s - fresh)
            keep = jnp.exp(top - fresh)
            tot = tot * keep + jnp.sum(e, axis=1, keepdims=True)
            acc = acc * keep + dot(e.astype(BF), r.s_v[at, lanes(p)])
            return fresh, tot, acc

        zero = jnp.zeros((2 * n, 1), F32)
        top, tot, acc = over_chunks(total, body, (zero + NEG_FILL, zero, jnp.zeros((2 * n, LANES), F32)))
        r.attn[:, lanes(p)] = join_heads(acc / tot)
        part = top + jnp.log(tot)
        lse = jnp.where(lane == 2 * p, part[:n], jnp.where(lane == 2 * p + 1, part[n:], lse))
    r.lse[...] = lse


def ffn_phase(r, copies):
    stat_ref = r.stat
    lane = lax.broadcasted_iota(jnp.int32, stat_ref.shape, 1)
    copies.wait("wo")
    branch = dot(r.attn[...].astype(BF), r.m_wo[...]) + row_of(r, BO)
    n1, r1 = normalize(r.x[...].astype(F32) + branch)
    hidden = n1 * row_of(r, G1) + row_of(r, C1)
    r.n1[...] = n1
    hidden_b = hidden.astype(BF)
    r.s_hidden[...] = hidden_b
    total = hidden + row_of(r, BU)
    for j in range(FF // FB):
        copies.wait(f"wi{j}")
        inner = dot(hidden_b, r.m_wi[:, units(j)]) + r.bi[:, units(j)]
        half = 0.5 + 0.5 * lax.erf(inner * (0.5**0.5))
        active = (inner * half).astype(BF)
        r.slope[:, units(j)] = (half + inner * jnp.exp(-0.5 * inner * inner) * 0.3989422804014327).astype(BF)
        r.s_active[:, units(j)] = active
        copies.wait(f"wu{j}")
        total = total + dot(active, r.m_wu[units(j), :])
    n2, r2 = normalize(total)
    r.n2[...] = n2
    stat_ref[...] = jnp.where(lane == 0, r1, jnp.where(lane == 1, r2, 0.0))
    return n2 * row_of(r, G2) + row_of(r, C2)


def store_active(r, ref, at, x):
    for z in range(4):
        src = pl.ds(pl.multiple_of((2 * z + x) * ACTIVE, LANES), ACTIVE)
        ref[:, at + z * ACTIVE : at + (z + 1) * ACTIVE] = r.s_active[:, src]


def store_pack(r, ref, at, x):
    ref[:, at : at + D] = r.s_hidden[...]
    ref[:, at + D : at + 2 * D] = r.attn[...].astype(BF)
    store_active(r, ref, at + 2 * D, x)


def feed_back_phase(r, copies, grad):
    place = r.place
    y, c = place[1], place[2]
    n2 = r.n2[...]
    sums = r.sums
    sums[0:1, :] = column_sum(grad * n2)
    sums[1:2, :] = column_sum(grad)
    grad = norm_back(grad, n2, r.stat[:, 1:2], row_of(r, G2))
    outer = grad.astype(BF)
    sums[2:3, :] = column_sum(outer)
    mine, theirs, mine_y, theirs_y = quarters(outer, 0, c)
    mine, theirs = cat(mine, mine_y), cat(theirs, theirs_y)
    r.near[:, NEAR_OUTER:NEAR_OUT] = mine
    r.send[:, NEAR_OUTER:NEAR_OUT] = theirs
    r.to_x[:, : 2 * CHUNK] = mine
    r.to_x[:, 2 * CHUNK : D] = theirs
    for j in range(FF // FB):
        copies.wait(f"wu{j}")
        inner = (dot_nt(outer, r.m_wu[units(j), :]) * r.slope[:, units(j)].astype(F32)).astype(BF)
        sums[6 + j : 7 + j, :] = column_sum(inner)
        r.s_inner[:, units(j)] = inner
        copies.wait(f"wi{j}")
        grad = grad + dot_nt(inner, r.m_wi[:, units(j)])
    n1 = r.n1[...]
    sums[3:4, :] = column_sum(grad * n1)
    sums[4:5, :] = column_sum(grad)
    pre_one = norm_back(grad, n1, r.stat[:, 0:1], row_of(r, G1))
    r.pre[...] = pre_one
    branch = pre_one.astype(BF)
    sums[5:6, :] = column_sum(branch)
    sums[10:16, :] = jnp.zeros((6, D), F32)
    mine, theirs, mine_y, theirs_y = quarters(branch, y, c)
    r.near[:, NEAR_OUT:NEAR] = mine
    r.send[:, NEAR_OUT:NEAR] = theirs
    r.to_y[:, SIDE_OUT:SIDE] = cat(mine_y, theirs_y)
    copies.wait("wo")
    attn_grad = dot_nt(branch, r.m_wo[...]).astype(BF)
    r.pack[:, :D] = attn_grad
    feature = lax.broadcasted_iota(jnp.int32, (D, LANES), 0) // HEAD_DIM
    member = (feature == lax.broadcasted_iota(jnp.int32, (D, LANES), 1)).astype(BF)
    hi, lo = hi_lo(attn_grad.astype(F32) * r.attn[...])
    delta = dot(hi, member) + dot(lo, member)
    r.delta[...] = delta
    extra = jnp.zeros(delta.shape, F32)
    for v, at in ((r.lse[...], LSE), (delta, DELTA)):
        for i in range(3):
            piece = v.astype(BF).astype(F32)
            extra = extra + (pltpu.roll(piece, at + i * PIECE, 1) if at + i else piece)
            v = v - piece
    r.pack[:, D:] = extra.astype(BF)
    shard = 2 * y + c
    for ref, at, k in (
        (r.near, 0, shard), (r.send, 0, 2 * y + 1 - c), (r.to_y, 0, 2 - 2 * y + c), (r.to_y, FB, 3 - 2 * y - c),
    ):
        ref[:, at : at + FB] = r.s_inner[:, pl.ds(pl.multiple_of(k * FB, LANES), FB)]


def key_back_phase(r, copies):
    place = r.place
    n, total = r.k.shape[0], r.s_g.shape[0]
    row = lax.broadcasted_iota(jnp.int32, (32, LANES), 0)
    lane = lax.broadcasted_iota(jnp.int32, (32, LANES), 1)
    first = jnp.where(row < 16, LSE, DELTA - 16) + row
    pick = ((lane == first) | (lane == first + PIECE) | (lane == first + 2 * PIECE)).astype(BF)
    rows_ref, own = r.s_stats, r.own[...]

    def fill(at, carry):
        rows_ref[:, at] = dot_nt(pick, r.s_extra[at, :])
        return carry

    over_chunks(total, fill, 0)
    for p in range(PAIRS):
        copies.wait(f"q{p}")
        k = two_heads(r.k[:, lanes(p)] * jnp.asarray(SCALE, BF))
        v = two_heads(r.v[:, lanes(p)])

        def body(at, carry):
            dk, dv = carry
            same = own == r.all[:, at]
            q, g = r.s_q[at, lanes(p)], r.s_g[at, lanes(p)]
            s, dp = dot_nt(k, q), dot_nt(v, g)
            probs, ds = [], []
            for h in range(2):
                half = slice(h * n, (h + 1) * n)
                lse, delta = rows_ref[2 * p + h : 2 * p + h + 1, at], rows_ref[16 + 2 * p + h : 17 + 2 * p + h, at]
                prob = jnp.exp(jnp.where(same, s[half] - lse, NEG_FILL))
                probs.append(prob.astype(BF))
                ds.append((prob * (dp[half] - delta)).astype(BF))
            return dk + dot(jnp.concatenate(ds, axis=0), q), dv + dot(jnp.concatenate(probs, axis=0), g)

        zero = jnp.zeros((2 * n, LANES), F32)
        dk, dv = over_chunks(total, body, (zero, zero))
        r.s_dk[:, lanes(p)] = unrotate(join_heads(dk) * SCALE, r.cos[...], r.sin[...]).astype(BF)
        r.s_dv[:, lanes(p)] = join_heads(dv).astype(BF)
    dq, dk, dv = r.dq[...], r.s_dk[...], r.s_dv[...]
    for i, v in enumerate((dq, dk, dv)):
        r.qkv_sums[i : i + 1, :] = column_sum(v)
    r.qkv_sums[3:8, :] = jnp.zeros((5, D), F32)
    mine, theirs, mine_y, theirs_y = zip(*[quarters(v, place[1], place[2]) for v in (dq, dk, dv)])
    for ref, v, above in ((r.qkv_near, mine, "above_near"), (r.qkv_send, theirs, "above_send"), (r.qkv_side, mine_y + theirs_y, "above_side")):
        ref[...] = cat(*v, r[above][...]) if above in r else cat(*v)


def input_back_phase(r, copies):
    total = r.pre_above[...]
    for name, ref in (("wq", r.dq), ("wk", r.s_dk), ("wv", r.s_dv)):
        copies.wait(name)
        total = total + dot_nt(ref[...], r["m_" + name][...])
    return total


def layer_forward(layer, place, x, blocks, weights, bi, vec, cos, sin, own_seg, all_seg, qkv=None, cotangent=None, after=()):
    n = x.shape[0]
    total = all_seg.shape[1]
    last = cotangent is not None
    names = ("wo", "wi", "wu") if qkv else ("wk", "wv", "wq", "wo", "wi", "wu")
    ins = Names(place=place, x=x, own=own_seg, all=all_seg, bi=bi[layer], vec=vec[layer])
    ins.update({"w_" + name: weights[name] for name in names})
    hbm = {"w_" + name for name in names}
    outs = Names(attn=sds((n, D), F32), lse=sds((n, LANES), F32), result_b=sds((n, D), BF))
    scratch = Names(
        s_hidden=pltpu.VMEM((n, D), BF), s_active=pltpu.VMEM((n, FF), BF), **rooms(names),
    )
    inner = Names(
        n1=sds((n, D), F32), n2=sds((n, D), F32), stat=sds((n, LANES), F32), slope=sds((n, FF), BF),
    )
    flops = 2 * n * (D * D + 2 * D * FF) + 4 * n * total * D * 2
    if qkv:
        ins.update(zip(("s_q", "s_k", "s_v"), qkv))
    else:
        ins.update(blocks=blocks, cos=cos, sin=sin)
        for name in "qkv":
            outs[name] = sds((total, D), BF)
            hbm.add(name)
            if name != "q":
                outs["own_" + name] = sds((n, D), BF)
            scratch["s_" + name] = pltpu.VMEM((total, D), BF)
        scratch.s_rows = pltpu.VMEM((total, D), BF)
        scratch.out_sems = pltpu.SemaphoreType.DMA((3,))
        flops += 6 * total * D * D
    if last:
        scratch.update({k: pltpu.VMEM(v.shape, v.dtype) for k, v in inner.items()})
        scratch.s_inner = pltpu.VMEM((n, FF), BF)
        ins.cotangent = cotangent
        outs.update(feed_back_outs(n, True))
        flops += 2 * n * (D * D + 2 * D * FF)
    else:
        outs.update(inner)
        outs.result = sds((n, D), F32)
        outs.update(keep_pack=sds((n, PACK), BF), side=sds((n, 2 * D), BF), active=sds((n, FF // 2), BF))

    def kernel(r):
        copies = Copies(r.sems)
        copies.weights(r, layer, names)
        if not qkv:
            join(r.s_rows, r.blocks, slice(0, D))
            qkv_phase(r, copies)
            back = Copies(r.out_sems)
            for name in "qkv":
                back.start(name, r["s_" + name], r[name])
            for name in "kv":
                r["own_" + name][...] = r["s_" + name][:n, :]
        attend_phase(r)
        result = ffn_phase(r, copies)
        r.result_b[...] = result.astype(BF)
        x = r.place[0]
        if last:
            feed_back_phase(r, copies, r.cotangent[...].astype(F32))
            for ref, at in ((r.near, NEAR_PACK), (r.send, NEAR_PACK)):
                ref[:, NEAR:NEAR_PACK] = jnp.zeros((n, NEAR_PACK - NEAR), BF)
                store_pack(r, ref, at, x)
            r.to_y[:, SIDE : SIDE + D] = r.s_hidden[...]
            r.to_y[:, SIDE + D :] = r.attn[...].astype(BF)
            store_active(r, r.to_x, D, 1 - x)
        else:
            r.result[...] = result
            store_pack(r, r.keep_pack, 0, x)
            r.side[:, :D] = r.s_hidden[...]
            r.side[:, D:] = r.attn[...].astype(BF)
            store_active(r, r.active, 0, 1 - x)
        if not qkv:
            back.wait(*"qkv")

    return mega(kernel, "forward_last" if last else "forward", ins, outs, scratch, flops, hbm=hbm, after=after)


def feed_back_outs(n, last):
    return Names(
        near=sds((n, NEAR_PACK + PACK if last else NEAR), BF), send=sds((n, NEAR_PACK + PACK), BF),
        to_x=sds((n, D + FF // 2 if last else D), BF), to_y=sds((n, SIDE + 2 * D if last else SIDE), BF),
        pre=sds((n, D), F32), pack=sds((n, D + LANES), BF), delta=sds((n, LANES), F32),
        sums=sds((16, D), F32),
    )


def layer_back(layer, place, kept, back, dq, blocks, weights, vec, cos, sin, own_seg, all_seg, below=None, far=(), after=()):
    n, total = dq.shape[0], all_seg.shape[1]
    names = ("wq", "wk", "wv") + (("wo", "wi", "wu") if below else ())
    ins = Names(
        place=place, k=kept.own_k, v=kept.own_v, q=kept.q, dq=dq, pre_above=back.pre, blocks=blocks,
        own=own_seg, all=all_seg, cos=cos, sin=sin,
    )
    ins.update({"w_" + name: weights[name] for name in names})
    hbm = {"w_" + name for name in names} | {"q"}
    single = len(blocks) == 1
    if single:
        hbm.add("blocks")
    wide = 1 if below else 2
    outs = Names(
        qkv_near=sds((n, wide * QKV), BF), qkv_send=sds((n, wide * QKV), BF), qkv_side=sds((n, wide * 2 * QKV), BF), qkv_sums=sds((8, D), F32),
        dk=sds((n, D), BF), dv=sds((n, D), BF),
    )
    scratch = Names(
        s_q=pltpu.VMEM((total, D), BF), s_g=pltpu.VMEM((total, D), BF), s_extra=pltpu.VMEM((total, LANES), BF),
        s_stats=pltpu.VMEM((32, total), F32), s_dk=pltpu.VMEM((n, D), BF), s_dv=pltpu.VMEM((n, D), BF),
        q_sems=pltpu.SemaphoreType.DMA((PAIRS + 2,)), **rooms(names),
    )
    if below:
        ins.update({k: below[k] for k in ("n1", "n2", "stat", "slope", "attn", "lse")}, vec=vec[layer - 1])
        outs.update(feed_back_outs(n, False))
        ins.far = list(far)
        scratch.s_inner = pltpu.VMEM((n, FF), BF)
    else:
        outs.grad = sds((n, D), BF)
        ins.update(above_near=back.qkv_near, above_send=back.qkv_send, above_side=back.qkv_side)

    def kernel(r):
        queries = Copies(r.q_sems)
        if single:
            queries.start("g", r.blocks[0].at[:, :D], r.s_g)
            queries.start("extra", r.blocks[0].at[:, D:], r.s_extra)
        for p in range(PAIRS):
            queries.start(f"q{p}", r.q.at[:, lanes(p)], r.s_q.at[:, lanes(p)])
        copies = Copies(r.sems)
        copies.weights(r, layer, names[:3])
        if below:
            copies.weights(r, layer - 1, names[3:])
        if single:
            queries.wait("g", "extra")
        else:
            join(r.s_g, r.blocks, slice(0, D))
            join(r.s_extra, r.blocks, slice(D, D + LANES))
        key_back_phase(r, queries)
        r.dk[...] = r.s_dk[...]
        r.dv[...] = r.s_dv[...]
        grad = input_back_phase(r, copies)
        if below:
            feed_back_phase(r, copies, grad)
            r.send[:, NEAR:NEAR_PACK] = jnp.zeros((n, NEAR_PACK - NEAR), BF)
            for i, ref in enumerate(r.far):
                at = NEAR_PACK + i * 2 * D
                r.send[:, at : at + 2 * D] = ref[...]
        else:
            r.grad[...] = grad.astype(BF)

    flops = 8 * n * total * D * 2 + 6 * n * D * D + (2 * n * (D * D + 2 * D * FF) if below else 0)
    return mega(kernel, "layer_back" if below else "layer_back_first", ins, outs, scratch, flops, hbm=hbm, after=after)


def feed_pieces(place, packs, near, side, cross, after=(), vmem=32):
    n = near[0].shape[0]
    here, there = packs
    ins = Names(
        place=place, here=[a for a, _ in here], att=[a for a, _, _, _ in there], act=[a for _, _, a, _ in there],
        near=list(near), side=list(side), cross=list(cross),
    )
    io, u = sds((4, WIDTH, IO), BF), sds((4, WIDTH, 2 * ACTIVE), BF)
    scratch = Names(
        t_hidden=pltpu.VMEM((D, 4 * n), BF), t_attn=pltpu.VMEM((D, 4 * n), BF), t_outer=pltpu.VMEM((2, CHUNK, 4 * n), BF),
    )

    def kernel(r):
        hidden = [(ref, at) for ref, (_, at) in zip(r.here, here)] + [(ref, at) for ref, (_, at, _, _) in zip(r.att, there)]
        turned(r.t_hidden, *[ref[:, at : at + D] for ref, at in hidden])
        turned(r.t_attn, *[ref[:, at + D : at + 2 * D] for ref, at in hidden])
        n0, n1 = r.near
        y0, y1 = r.side
        x0, x1 = r.cross
        inner = jnp.concatenate([n0[:, :FB], n1[:, :FB], y0[:, :FB], y1[:, FB : 2 * FB]], axis=0)
        out = jnp.concatenate(
            [n0[:, NEAR_OUT:NEAR], n1[:, NEAR_OUT:NEAR], y0[:, SIDE_OUT : SIDE_OUT + CHUNK], y1[:, SIDE_OUT + CHUNK : SIDE]], axis=0
        )
        x, y = r.place[0], r.place[1]
        for name, side_x in (("io_send", 1 - x), ("io_keep", x)):
            r[name][:, :, :FB] = dot(shard_rows(r.t_hidden, side_x), inner).astype(BF).reshape(4, WIDTH, FB)
            r[name][:, :, FB:] = dot(shard_rows(r.t_attn, side_x), out).astype(BF).reshape(4, WIDTH, CHUNK)
        sources = [(n0, NEAR_OUTER), (n1, NEAR_OUTER), (x0, 0), (x1, 2 * CHUNK)]
        for h in range(2):
            turned(r.t_outer.at[h], *[ref[:, at + h * CHUNK : at + (h + 1) * CHUNK] for ref, at in sources])
        active = [ref[:, at + 2 * D : at + PACK] for ref, (_, at) in zip(r.here, here)]
        active += [ref[:, at : at + FF // 2] for ref, (_, _, _, at) in zip(r.act, there)]
        active = jnp.concatenate(active, axis=0)
        for name, side_y in (("u_send", 1 - y), ("u_keep", y)):
            t = dot(r.t_outer[side_y], active).astype(BF)
            for z in range(4):
                part = t[:, z * ACTIVE : (z + 1) * ACTIVE]
                r[name][z, :, :ACTIVE] = part[:WIDTH]
                r[name][z, :, ACTIVE:] = part[WIDTH:]

    outs = Names(io_keep=io, io_send=io, u_keep=u, u_send=u)
    return mega(kernel, "feed_pieces", ins, outs, scratch, 8 * n * (D * IO + FF * CHUNK), after=after, vmem=vmem)


def qkv_pieces(place, blocks, near, side, after=()):
    n = near[0].shape[0]
    ins = Names(place=place, blocks=[b[k] for b in blocks for k in (0, 4, 2, 6)], near=list(near), side=list(side))
    o = sds((4, WIDTH, padded(QKV) + QKV), BF)

    def kernel(r):
        (g0, g1), (y0, y1) = r.near, r.side
        x = r.place[0]
        for layer in range(LAYERS):
            turned(r.t_rows.at[layer], *[ref[...] for ref in r.blocks[4 * layer : 4 * layer + 4]])
            parts = (g0, layer * QKV), (g1, layer * QKV), (y0, 2 * layer * QKV), (y1, (2 * layer + 1) * QKV)
            g = jnp.concatenate([ref[:, at : at + QKV] for ref, at in parts], axis=0)
            at = layer * padded(QKV)
            for name, side_x in (("send", 1 - x), ("keep", x)):
                found = dot(shard_rows(r.t_rows.at[layer], side_x), g).astype(BF)
                r[name][:, :, at : at + QKV] = found.reshape(4, WIDTH, QKV)

    scratch = Names(t_rows=pltpu.VMEM((LAYERS, D, 4 * n), BF))
    return mega(kernel, "qkv_pieces", ins, Names(keep=o, send=o), scratch, 16 * n * D * QKV, after=after, vmem=24)


def padded(w):
    return -(-w // LANES) * LANES


def first_sum(place, pairs, after=(), vmem=24):
    width = sum(padded(a.shape[2]) for a, _ in pairs)
    o = sds((2, WIDTH, width), BF)

    def kernel(r):
        bit = r.place[3] % 2
        for name, side in (("keep", bit), ("send", 1 - bit)):
            for i in range(2):
                at = 0
                for a, b in zip(r.own, r.got):
                    w = a.shape[2]
                    r[name][i, :, at : at + w] = (a[2 * i + side].astype(F32) + b[2 * i + side].astype(F32)).astype(BF)
                    at += padded(w)

    ins = Names(place=place, own=[a for a, _ in pairs], got=[b for _, b in pairs])
    return mega(kernel, "first_sum", ins, Names(keep=o, send=o), {}, 1000, after=after, vmem=vmem)


def second_sum(place, keep, got, after=()):
    o = sds(keep.shape[1:], BF)

    def kernel(r):
        bit = r.place[3] // 2
        for name, side in (("keep", bit), ("send", 1 - bit)):
            r[name][...] = (r.own[side].astype(F32) + r.got[side].astype(F32)).astype(BF)

    return mega(kernel, "second_sum", Names(place=place, own=keep, got=got), Names(keep=o, send=o), {}, 1000, after=after, vmem=24)


FEED_SHAPES = Names(inner=(WIDTH, FB), out=(WIDTH, CHUNK), outer=(CHUNK, ACTIVE))
QKV_SHAPES = Names(query=(WIDTH, CHUNK), key=(WIDTH, CHUNK), value=(WIDTH, CHUNK))


def last_feed(layers):
    outs = Names((k, sds((LAYERS,) + v, F32)) for k, v in FEED_SHAPES.items())

    def kernel(r):
        for layer, (a, b) in enumerate(zip(r.own, r.got)):
            total = a[...].astype(F32) + b[...].astype(F32)
            r.inner[layer] = total[:, :FB]
            r.out[layer] = total[:, FB:IO]
            r.outer[layer, :WIDTH] = total[:, IO_PAD : IO_PAD + ACTIVE]
            r.outer[layer, WIDTH:] = total[:, IO_PAD + ACTIVE :]

    return mega(kernel, "last_feed", Names(own=[a for a, _ in layers], got=[b for _, b in layers]), outs, {}, 1000, vmem=24)


def last_qkv(keep, got):
    outs = Names((k, sds((LAYERS,) + v, F32)) for k, v in QKV_SHAPES.items())

    def kernel(r):
        total = r.own[...].astype(F32) + r.got[...].astype(F32)
        for layer in range(LAYERS):
            for i, name in enumerate(QKV_SHAPES):
                at = layer * padded(QKV) + i * CHUNK
                r[name][layer] = total[:, at : at + CHUNK]

    return mega(kernel, "last_qkv", Names(own=keep, got=got), outs, {}, 1000, vmem=24)


def linear(z, x, y, c):
    return (z * 2 + x) * 4 + y * 2 + c


PLACES = [(z, x, y, c) for z in range(4) for x in range(2) for y in range(2) for c in range(2)]


def move(array, where):
    pairs = [(linear(*place), linear(*where(*place))) for place in PLACES]
    return lax.ppermute(array, BOTH, pairs)


def to_plane(z, x, y, c):
    return (2 * y + c, x, z >> 1, z & 1)


def other_core(z, x, y, c):
    return (z, x, y, 1 - c)


def other_x(z, x, y, c):
    return (z, 1 - x, y, c)


def other_y(z, x, y, c):
    return (z, x, 1 - y, c)


def other_xy(z, x, y, c):
    return (z, 1 - x, 1 - y, c)


def near_z(z, x, y, c):
    return (z ^ 1, x, y, c)


def far_z(z, x, y, c):
    return (z ^ 2, x, y, c)


def gate(arrays, *others):
    return lax.optimization_barrier((arrays, others))[0]


def pick(array, index, axis):
    return lax.dynamic_index_in_dim(array, index, axis, keepdims=False)


class Small:
    def __init__(self):
        seq, rows = lax.axis_index("seq"), lax.axis_index("rows")
        self.z, self.x, self.y, self.c = seq // 2, seq % 2, rows // 2, rows % 2
        self.spot = jnp.stack([self.x, self.y, self.c, self.z]).astype(jnp.int32)

    def share_few(self, mine):
        far = jnp.concatenate(mine[1:], axis=0)
        return [mine[0], far, move(mine[0], other_core), move(far, other_core)]

    def starts(self, count):
        out = []
        for dc in (0, 1):
            for dx, dy in ((0, 0), (1, 0), (0, 1), (1, 1)):
                x, y, c = self.x ^ dx, self.y ^ dy, self.c ^ dc
                out.append(((2 * y + c) * 2 + x) * count)
        return jnp.stack(out)

    def reach(self, array):
        return [array, move(array, other_x), move(array, other_y), move(array, other_xy)]

    def share(self, mine):
        return mine + [move(a, other_core) for a in mine]


class Large:
    def __init__(self):
        self.shards = lax.axis_size("seq")
        self.spot = jnp.zeros((4,), jnp.int32)

    def starts(self, count):
        me = lax.axis_index("seq")
        return (me + jnp.arange(self.shards, dtype=jnp.int32)) % self.shards * count

    def gather(self, array):
        whole_row = lax.all_gather(array, "seq", axis=0, tiled=True)
        return [jnp.roll(whole_row, -lax.axis_index("seq") * array.shape[0], axis=0)]

    def spread(self, left, right):
        grad = lax.dot_general(left, right, (((0,), (0,)), ((), ())), preferred_element_type=F32).astype(BF)
        grad = lax.psum_scatter(grad, "seq", scatter_dimension=0, tiled=True)
        return lax.psum_scatter(grad, "rows", scatter_dimension=1, tiled=True).astype(F32)

    def grads(self, kept, back, tail, dq):
        near, send, to_x, to_y = back.near, back.send, back.to_x, back.to_y
        inner = cat(near[:, :FB], send[:, :FB], to_y[:, : 2 * FB])
        out = cat(near[:, NEAR_OUT:NEAR], send[:, NEAR_OUT:NEAR], to_y[:, SIDE_OUT:SIDE])
        outer = cat(*[to_x[:, i * CHUNK : (i + 1) * CHUNK] for i in (0, 2, 1, 3)])
        if "active" in kept:
            hidden, attn = kept.side[:, :D], kept.side[:, D:]
            mine, other = kept.keep_pack[:, 2 * D :], kept.active
        else:
            hidden, attn = to_y[:, SIDE : SIDE + D], to_y[:, SIDE + D :]
            mine, other = near[:, NEAR_PACK + 2 * D :], to_x[:, D:]
        active = jnp.stack([v.reshape(-1, 4, ACTIVE) for v in (mine, other)], axis=2).reshape(-1, FF)
        own = kept.blocks[0][: dq.shape[0]]
        return Names(
            inner=self.spread(hidden, inner), out=self.spread(attn, out), outer=self.spread(active, outer),
            query=self.spread(own, dq), key=self.spread(own, tail.dk), value=self.spread(own, tail.dv),
        )


def doc_layout(lengths_row, index):
    ends = jnp.cumsum(lengths_row, dtype=jnp.int32)
    passed = (index[:, None] >= ends[None, :]).astype(jnp.int32)
    segment = jnp.sum(passed, axis=1, dtype=jnp.int32)
    begin = jnp.sum(passed * lengths_row[None, :], axis=1, dtype=jnp.int32)
    return (segment, (index - begin).astype(jnp.int32))


def rotary_tables(position):
    lane = jnp.arange(LANES, dtype=jnp.int32)
    pairs = (lane % HEAD_DIM // 2).astype(F32)
    inverse = jnp.power(jnp.float32(10000.0), -2.0 * pairs / HEAD_DIM)
    angle = position.astype(F32)[:, None] * inverse[None, :]
    return jnp.cos(angle), jnp.sin(angle) * jnp.where(lane % 2 == 0, -1.0, 1.0)[None, :]


def both_cores(array):
    return array, move(array, other_core)


def all_sums(two, tail_two, one, tail_one):
    return jnp.concatenate([one.sums[:10], tail_one.qkv_sums[:3], two.sums[:10], tail_two.qkv_sums[:3]], axis=0)


VECTOR_ROWS = Names(g2=0, c2=1, bu=2, g1=3, c1=4, bo=5, bq=10, bk=11, bv=12)
LAYER_ROWS = 13


def last_vectors(place, own, got, whole):
    outs = Names((name, sds((LAYERS, WIDTH), F32)) for name in VECTOR_ROWS)
    outs.bi = sds((LAYERS, ACTIVE), F32)
    outs.passed = [sds(a.shape, a.dtype) for a in whole]

    def kernel(r):
        for a, b in zip(r.whole, r.passed):
            b[...] = a[...]
        x, z = r.place[0], r.place[3]
        total = r.own[...] + r.got[...]
        r.s_total[...] = total
        shard = 2 * z + x
        turn = pltpu.roll(total, (D - shard * WIDTH) % D, 1)[:, :WIDTH]
        for layer in range(LAYERS):
            for name, row in VECTOR_ROWS.items():
                at = LAYER_ROWS * layer + row
                r[name][layer : layer + 1, :] = turn[at : at + 1]
            row = r.s_total[pl.ds(LAYER_ROWS * layer + 6 + z, 1), :]
            r.bi[layer : layer + 1, :] = jnp.where(x == 0, row[:, :ACTIVE], row[:, ACTIVE:])

    scratch = Names(s_total=pltpu.VMEM(own.shape, F32))
    return mega(kernel, "last_vectors", Names(place=place, own=own, got=got, whole=list(whole)), outs, scratch, 1000, vmem=24)


class Program:
    def __init__(self, place, spot, lengths_row, n, starts, params):
        wq, bq, wk, bk, wv, bv, wo, bo, g1, c1, wi, bi, wu, bu, g2, c2 = params
        self.weights = Names(wq=wq, wk=wk, wv=wv, wo=wo, wi=wi, wu=wu)
        self.spot, self.n = spot, n
        self.vec = jnp.stack([bq, bk, bv, bo, g1, c1, bu, g2, c2], axis=1).astype(F32)
        self.bi = bi.astype(F32)[:, None, :]
        index = (starts[:, None] + jnp.arange(n, dtype=jnp.int32)).reshape(-1)
        segment, position = doc_layout(lengths_row, index)
        self.segments = segment[:n, None], segment[None, :]
        self.cos, self.sin = rotary_tables(position)
        self.own_cos, self.own_sin = rotary_tables(position[:n])

    def project(self, layer, rows):
        w = self.weights
        return project(rows, layer, w["wq"], w["wk"], w["wv"], self.vec, self.cos, self.sin)

    def forward(self, layer, x, blocks, qkv=None, cotangent=None, after=()):
        kept = layer_forward(
            layer, self.spot, x, blocks, self.weights, self.bi, self.vec, self.cos, self.sin, *self.segments, qkv, cotangent, after
        )
        kept.blocks = blocks
        if qkv:
            kept.update(zip("qkv", qkv), own_k=qkv[1][: self.n], own_v=qkv[2][: self.n])
        return kept

    def queries(self, kept, back, after=()):
        return query_back(
            kept.q, kept.k, kept.v, back.pack, kept.lse, back.delta, *self.segments, self.own_cos, self.own_sin, after
        )[0]

    def back(self, layer, kept, back, dq, packs, below=None, far=(), after=()):
        return layer_back(
            layer, self.spot, kept, back, dq, packs, self.weights, self.vec, self.own_cos, self.own_sin, *self.segments, below, far, after
        )


def large_body(tokens, lengths, cotangent, *params):
    place = Large()
    n = tokens.shape[1]
    run = Program(place, place.spot, lengths[0], n, place.starts(n), params)

    def step(layer, x, x_b, cotangent=None):
        blocks = place.gather(x_b)
        return run.forward(layer, x, blocks, run.project(layer, blocks[0]), cotangent)

    first = step(0, tokens[0], tokens[0])
    second = step(1, first.result, first.result_b, cotangent[0])
    dq_two = run.queries(second, second)
    back_one = run.back(1, second, second, dq_two, place.gather(second.pack), first)
    dq_one = run.queries(first, back_one)
    back_none = run.back(0, first, back_one, dq_one, place.gather(back_one.pack))
    grads_one = place.grads(first, back_one, back_none, dq_one)
    grads_two = place.grads(second, second, back_one, dq_two)
    m = Names((name, jnp.stack([grads_one[name], grads_two[name]])) for name in grads_one)
    total = lax.psum(all_sums(second, back_one, back_one, back_none), BOTH).reshape(LAYERS, LAYER_ROWS, D)
    me, shards = lax.axis_index("seq"), lax.axis_size("seq")
    v = Names(
        (name, lax.dynamic_slice_in_dim(total[:, row], me * (D // shards), D // shards, 1))
        for name, row in VECTOR_ROWS.items()
    )
    v.bi = lax.dynamic_slice_in_dim(total[:, 6:10].reshape(LAYERS, FF), me * (FF // shards), FF // shards, 1)
    return result(second.result_b, back_none.grad, m, v)


def small_body(tokens, lengths, cotangent, *params):
    place = Small()
    spot, n = place.spot, tokens.shape[1]
    current = move(tokens[0], to_plane)
    run = Program(place, spot, move(lengths, to_plane)[0], n, place.starts(n), params)
    blocks = place.share(gate(place.reach(current), run.cos, run.sin, run.own_cos, run.own_sin, run.vec, run.bi))
    grad = move(gate(cotangent[0], current), to_plane)
    first = run.forward(0, current, blocks, after=(grad,))
    a_near = both_cores(first.keep_pack)
    blocks = place.share(place.reach(first.result_b))
    side, active = gate((first.side, first.active), blocks)
    a_side, a_cross = move(side, other_y), move(active, other_x)
    second = run.forward(1, first.result, blocks, cotangent=grad, after=(a_near[1],))

    reached = place.reach(second.pack)
    dq_two = run.queries(second, second, after=(a_side, a_cross))
    packs = place.share(gate(reached, dq_two))
    to_y, to_x, send, result_b = gate((second.to_y, second.to_x, second.send, second.result_b), packs)
    from_y, from_x, near = move(to_y, other_y), move(to_x, other_x), (second.near, move(send, other_core))
    output = move(result_b, to_plane)
    back_one = run.back(1, second, second, dq_two, packs, first, (a_side, a_cross))

    pack, from_y, from_x, near_got = gate((back_one.pack, from_y, from_x, near[1]), output)
    near = near[0], near_got
    reached = place.reach(pack)
    side, cross = [both_cores(a) for a in gate((from_y, from_x), pack)]
    dq_one = run.queries(first, back_one)
    packs = place.share_few(gate(reached, dq_one))
    to_y, to_x = gate((back_one.to_y, back_one.to_x), reached, dq_one)
    one_y, one_x = move(to_y, other_y), move(to_x, other_x)
    there = [(a, SIDE, b, D) for a, b in zip(side, cross)]
    two = feed_pieces(spot, ([(a, NEAR_PACK) for a in near], there), near, side, cross, after=(dq_one, *reached), vmem=60)
    two_io, two_u = move(two.io_send, other_x), move(two.u_send, other_y)
    near = back_one.near, move(gate(back_one.send, reached, dq_one), other_core)
    back_none = run.back(0, first, back_one, dq_one, packs, after=(two.io_send, near[1], one_x))

    two_sum = first_sum(spot, ((two.io_keep, two_io), (two.u_keep, two_u)), vmem=60, after=(back_none.grad, one_y, near[1]))
    side, cross = [both_cores(a) for a in gate((one_y, one_x), back_none.grad)]
    q_side = move(back_none.qkv_side, other_y)
    tokens_grad = move(back_none.grad, to_plane)
    sums = all_sums(second, back_one, back_one, back_none)
    from_sums = move(sums, other_core)
    two_near = move(two_sum.send, near_z)
    there = [(a_side, 0, a_cross, 0), (near[1], NEAR_PACK, near[1], NEAR_PACK + 2 * D)]
    one = feed_pieces(spot, ([(a, 0) for a in a_near], there), near, side, cross, after=(two_sum.send, tokens_grad))
    one_io, one_u = move(one.io_send, other_x), move(one.u_send, other_y)
    sums = gate(sums + from_sums, two_sum.send)
    from_sums = move(sums, near_z)
    qkv_send, q_side = gate((back_none.qkv_send, q_side), one.io_send)
    q_near, q_side = (back_none.qkv_near, move(qkv_send, other_core)), both_cores(q_side)
    qkv = qkv_pieces(spot, (first.blocks, second.blocks), q_near, q_side, after=(one.io_send, from_sums))
    q_x = move(qkv.send, other_x)
    two_z = second_sum(spot, two_sum.keep, two_near, after=(qkv.send, one_io))
    two_far = move(two_z.send, far_z)
    sums = gate(sums + from_sums, qkv.send)
    from_sums = move(sums, far_z)
    one_sum = first_sum(spot, ((one.io_keep, one_io), (one.u_keep, one_u)), after=(two_z.send, from_sums))
    one_near = move(one_sum.send, near_z)
    sums = gate(sums + from_sums, one_sum.send)
    from_sums = move(sums, other_x)
    q_sum = first_sum(spot, ((qkv.keep, q_x),), after=(one_sum.send, two_far))
    q_near = move(q_sum.send, near_z)
    sums = gate(sums + from_sums, q_sum.send)
    from_sums = move(sums, other_y)
    one_z = second_sum(spot, one_sum.keep, one_near, after=(q_sum.send,))
    one_far = move(one_z.send, far_z)
    q_z = second_sum(spot, q_sum.keep, q_near, after=(one_z.send,))
    q_far = move(q_z.send, far_z)
    v = last_vectors(spot, sums, from_sums, (output, tokens_grad))
    m = last_feed(((one_z.keep, one_far), (two_z.keep, two_far)))
    m.outer = m.outer.swapaxes(1, 2)
    m.update(last_qkv(q_z.keep, q_far))
    return result(*v.passed, m, v)


def result(output, tokens_grad, m, v):
    return (
        output[None], tokens_grad[None],
        m.query, v.bq, m.key, v.bk, m.value, v.bv, m.out, v.bo, v.g1, v.c1,
        m.inner, v.bi, m.outer, v.bu, v.g2, v.c2,
    )


def solution(mesh):
    token = P("rows", "seq", None)
    mat, vec = P(None, "seq", "rows"), P(None, "seq")
    small = (mesh.shape["seq"], mesh.shape["rows"]) == (8, 4)
    return jax.shard_map(
        small_body if small else large_body,
        mesh=mesh,
        in_specs=(token, P("rows", None), token) + (P(),) * 16,
        out_specs=(token, token, mat, vec, mat, vec, mat, vec, mat, vec, vec, vec, mat, vec, mat, vec, vec, vec),
        check_vma=False,
    )
```

```python
import jax
import jax.numpy as jnp
from jax import lax
from jax.experimental import pallas as pl
from jax.experimental.pallas import tpu as pltpu
from jax.sharding import PartitionSpec as P

D = 768
HEADS = 12
HEAD_DIM = 64
FF = 3072
LAYERS = 2
LANES = 128
PAIRS = D // LANES
CHUNK = D // 4
NEG_FILL = -1e30
NORM_EPS = 1e-12
SCALE = HEAD_DIM**-0.5
BF = jnp.bfloat16
F32 = jnp.float32
BOTH = ("seq", "rows")
MIB = 1 << 20

BQ, BK, BV, BO, G1, C1, BU, G2, C2 = range(9)
FB = 768
WIDTH = D // 8
ACTIVE = FF // 8
QKV = 3 * CHUNK
IO = FB + CHUNK
IO_PAD = FB + 2 * LANES

NEAR_OUTER, NEAR_OUT, NEAR = FB, FB + 2 * CHUNK, FB + 3 * CHUNK
NEAR_PACK = NEAR + 64
SIDE_OUT, SIDE = 2 * FB, 2 * FB + 2 * CHUNK
PACK = 2 * D + FF // 2

LSE, DELTA, PIECE = 0, 48, 16


class Names(dict):
    __getattr__ = dict.__getitem__
    __setattr__ = dict.__setitem__


def dot(a, b):
    return jnp.dot(a, b, preferred_element_type=F32)


def dot_nt(a, b):
    return lax.dot_general(a, b, (((1,), (1,)), ((), ())), preferred_element_type=F32)


def call(kernel, name, grid, in_specs, out_specs, out_shape, args, flops, scratch=(), scalars=(), vmem=60, after=(), aliases=None):
    size = sum(a.size * a.dtype.itemsize for a in args) + sum(
        s.size * s.dtype.itemsize for s in jax.tree.leaves(out_shape)
    )
    lead, many = len(scalars) + len(args), len(after)

    def run(*refs):
        kernel(*refs[:lead], *refs[lead + many :])

    return pl.pallas_call(
        run,
        name=name,
        grid_spec=pltpu.PrefetchScalarGridSpec(
            num_scalar_prefetch=len(scalars),
            grid=grid,
            in_specs=list(in_specs) + [pl.BlockSpec(memory_space=pl.ANY)] * many,
            out_specs=out_specs,
            scratch_shapes=list(scratch),
        ),
        out_shape=out_shape,
        input_output_aliases=aliases or {},
        compiler_params=pltpu.CompilerParams(
            dimension_semantics=("arbitrary",) * len(grid), vmem_limit_bytes=vmem * MIB
        ),
        cost_estimate=pl.CostEstimate(flops=int(flops), bytes_accessed=int(size), transcendentals=0),
    )(*scalars, *args, *after)


def whole(array):
    return pl.BlockSpec(array.shape, lambda *_: (0,) * array.ndim)


def layer_block(array, layer):
    return pl.BlockSpec((None,) + array.shape[1:], lambda *_: (layer,) + (0,) * (array.ndim - 1))


def sds(shape, dtype):
    return jax.ShapeDtypeStruct(shape, dtype)


def lane_is_even(shape):
    return lax.broadcasted_iota(jnp.int32, shape, 1) % 2 == 0


def swap_pairs(v):
    return jnp.where(lane_is_even(v.shape), pltpu.roll(v, LANES - 1, 1), pltpu.roll(v, 1, 1))


def lanes(j):
    return slice(j * LANES, (j + 1) * LANES)


def qkv_kernel(x_ref, wq_ref, wk_ref, wv_ref, vec_ref, cos_ref, sin_ref, q_ref, k_ref, v_ref):
    x, cos, sin = x_ref[...], cos_ref[...], sin_ref[...]
    for w_ref, row, o_ref in ((wq_ref, BQ, q_ref), (wk_ref, BK, k_ref)):
        y = dot(x, w_ref[...]) + vec_ref[row : row + 1, :]
        for j in range(PAIRS):
            t = y[:, lanes(j)]
            o_ref[:, lanes(j)] = (t * cos + swap_pairs(t) * sin).astype(BF)
    v_ref[...] = (dot(x, wv_ref[...]) + vec_ref[BV : BV + 1, :]).astype(BF)


def project(rows, layer, wq, wk, wv, vec, cos, sin):
    total = rows.shape[0]
    block = min(256, total)
    tok = lambda w: pl.BlockSpec((block, w), lambda i: (i, 0))
    return call(
        qkv_kernel, "qkv", (total // block,),
        [tok(D)] + [layer_block(w, layer) for w in (wq, wk, wv, vec)] + [tok(LANES), tok(LANES)],
        [tok(D)] * 3, [sds((total, D), BF)] * 3,
        (rows, wq, wk, wv, vec, cos, sin), 6 * total * D * D,
    )


def over_chunks(total, body, carry):
    size = min(total, 1024)
    if size == total:
        return body(slice(None), carry)
    return lax.fori_loop(
        0, total // size, lambda i, c: body(pl.ds(pl.multiple_of(i * size, size), size), c), carry
    )


def two_heads(v):
    low = lax.broadcasted_iota(jnp.int32, v.shape, 1) < HEAD_DIM
    zero = jnp.zeros_like(v)
    return jnp.concatenate([jnp.where(low, v, zero), jnp.where(low, zero, v)], axis=0)


def join_heads(v):
    n = v.shape[0] // 2
    low = lax.broadcasted_iota(jnp.int32, (n, LANES), 1) < HEAD_DIM
    return jnp.where(low, v[:n], v[n:])


def normalize(values):
    centered = values - jnp.mean(values, axis=-1, keepdims=True)
    rstd = lax.rsqrt(jnp.mean(centered * centered, axis=-1, keepdims=True) + NORM_EPS)
    return centered * rstd, rstd


def column_sum(v):
    return jnp.sum(v.astype(F32), axis=0, keepdims=True)


def norm_back(grad, normed, rstd, gain):
    scaled = grad * gain
    centered = scaled - jnp.mean(scaled, axis=-1, keepdims=True)
    return rstd * (centered - normed * jnp.mean(scaled * normed, axis=-1, keepdims=True))


def either(first, a, b):
    return jnp.where(first, a, b), jnp.where(first, b, a)


def cat(*parts):
    return jnp.concatenate(parts, axis=1)


def quarters(v, y, c):
    part = [v[:, k * CHUNK : (k + 1) * CHUNK] for k in range(4)]
    mine0, theirs0 = either(c == 0, part[0], part[1])
    mine1, theirs1 = either(c == 0, part[2], part[3])
    mine, mine_y = either(y == 0, mine0, mine1)
    theirs, theirs_y = either(y == 0, theirs0, theirs1)
    return mine, theirs, mine_y, theirs_y


def hi_lo(v):
    hi = v.astype(BF)
    return hi, (v - hi.astype(F32)).astype(BF)


def unrotate(v, cos, sin):
    t = v * sin
    return v * cos + swap_pairs(t)


def lane_of(v, lane):
    at = lax.broadcasted_iota(jnp.int32, v.shape, 1)
    return jnp.sum(jnp.where(at == lane, v, 0.0), axis=1, keepdims=True)


def query_back_kernel(
    q_ref, k_ref, v_ref, g_ref, lse_ref, delta_ref, own_ref, all_ref, cos_ref, sin_ref,
    dq_ref, sum_ref,
):
    pair = pl.program_id(0)
    n, total = q_ref.shape[0], k_ref.shape[0]
    q = two_heads(q_ref[...] * jnp.asarray(SCALE, BF))
    g = two_heads(g_ref[...])
    own = own_ref[...]
    lse = jnp.concatenate([lane_of(lse_ref[...], 2 * pair), lane_of(lse_ref[...], 2 * pair + 1)], axis=0)
    delta = jnp.concatenate([lane_of(delta_ref[...], 2 * pair), lane_of(delta_ref[...], 2 * pair + 1)], axis=0)

    def body(at, acc):
        same = own == all_ref[:, at]
        k = k_ref[at, :]
        s = jnp.where(jnp.concatenate([same, same], axis=0), dot_nt(q, k) - lse, NEG_FILL)
        ds = (jnp.exp(s) * (dot_nt(g, v_ref[at, :]) - delta)).astype(BF)
        return acc + dot(ds, k)

    acc = join_heads(over_chunks(total, body, jnp.zeros((2 * n, LANES), F32))) * SCALE
    dq = unrotate(acc, cos_ref[...], sin_ref[...]).astype(BF)
    dq_ref[...] = dq
    sum_ref[...] = column_sum(dq)


def query_back(q, k, v, pack, lse, delta, own_seg, all_seg, cos, sin, after=()):
    n, total = pack.shape[0], k.shape[0]
    own = pl.BlockSpec((n, LANES), lambda p: (0, p))
    row = pl.BlockSpec((total, LANES), lambda p: (0, p))
    fixed = lambda w: pl.BlockSpec((n, w), lambda p: (0, 0))
    return call(
        query_back_kernel, "query_back", (PAIRS,),
        [own, row, row, own, fixed(LANES), fixed(LANES), whole(own_seg), whole(all_seg), fixed(LANES), fixed(LANES)],
        [own, pl.BlockSpec((1, LANES), lambda p: (0, p))],
        [sds((n, D), BF), sds((1, D), F32)],
        (q, k, v, pack, lse, delta, own_seg, all_seg, cos, sin), 6 * n * total * D * 2, after=after,
    )


def turned(ref, *parts):
    n = parts[0].shape[0]
    for i, part in enumerate(parts):
        ref[:, i * n : (i + 1) * n] = part.T


def shard_rows(ref, x):
    width = WIDTH
    return jnp.concatenate(
        [ref[pl.ds(pl.multiple_of((2 * z + x) * width, 32), width), :] for z in range(4)], axis=0
    )


def mega(kernel, name, ins, outs, scratch, flops, hbm=(), after=(), vmem=60):
    flat_in, tree_in = jax.tree.flatten(dict(ins))
    flat_out, tree_out = jax.tree.flatten(dict(outs))

    def spec_of(key):
        space = pl.ANY if key in hbm else pltpu.SMEM if key == "place" else pltpu.VMEM
        return pl.BlockSpec(memory_space=space)

    specs_in = jax.tree.leaves({k: jax.tree.map(lambda _: spec_of(k), v) for k, v in ins.items()})
    specs_out = jax.tree.leaves({k: jax.tree.map(lambda _: spec_of(k), v) for k, v in outs.items()})
    many_in, many_out = len(flat_in), len(flat_out)

    def run(*refs):
        lead = many_in + len(after)
        named = Names(tree_in.unflatten(refs[:many_in]))
        named.update(tree_out.unflatten(refs[lead : lead + many_out]))
        named.update(zip(scratch, refs[lead + many_out :]))
        kernel(named)

    size = sum(a.size * a.dtype.itemsize for a in flat_out) + sum(
        a.size * a.dtype.itemsize for k, v in ins.items() if k not in hbm for a in jax.tree.leaves(v)
    )
    out = pl.pallas_call(
        run,
        name=name,
        in_specs=specs_in + [pl.BlockSpec(memory_space=pl.ANY)] * len(after),
        out_specs=specs_out,
        out_shape=flat_out,
        scratch_shapes=list(scratch.values()),
        compiler_params=pltpu.CompilerParams(vmem_limit_bytes=vmem * MIB),
        cost_estimate=pl.CostEstimate(flops=int(flops), bytes_accessed=int(size), transcendentals=0),
    )(*flat_in, *after)
    return Names(tree_out.unflatten(out))


SHAPES = Names(wq=(D, D), wk=(D, D), wv=(D, D), wo=(D, D), wi=(D, FF), wu=(FF, D))


def rooms(names):
    found = Names(("m_" + name, pltpu.VMEM(SHAPES[name], BF)) for name in names)
    found.sems = pltpu.SemaphoreType.DMA((16,))
    return found


def units(j):
    return pl.ds(j * FB, FB)


class Copies:
    def __init__(self, sems):
        self.sems, self.copies = sems, {}

    def start(self, name, src, dst):
        self.copies[name] = pltpu.make_async_copy(src, dst, self.sems.at[len(self.copies)])
        self.copies[name].start()

    def weights(self, r, layer, names):
        for name in names:
            src, dst = r["w_" + name].at[layer], r["m_" + name]
            if name not in ("wi", "wu"):
                self.start(name, src, dst)
                continue
            for j in range(FF // FB):
                at = (slice(None), units(j)) if name == "wi" else (units(j), slice(None))
                self.start(f"{name}{j}", src.at[at], dst.at[at])

    def wait(self, *names):
        for name in names:
            if name in self.copies:
                self.copies.pop(name).wait()


def join(dst, refs, columns):
    at = 0
    for ref in refs:
        dst[at : at + ref.shape[0], :] = ref[:, columns]
        at += ref.shape[0]


def row_of(r, index):
    return r.vec[index : index + 1, :]


def qkv_phase(r, copies):
    rows, cos, sin = r.s_rows, r.cos, r.sin
    total = rows.shape[0]
    block = min(256, total)
    for name, bias in (("k", BK), ("v", BV), ("q", BQ)):
        copies.wait("w" + name)
        for i in range(total // block):
            at = pl.ds(i * block, block)
            y = dot(rows[at, :], r["m_w" + name][...]) + row_of(r, bias)
            if name == "v":
                r.s_v[at, :] = y.astype(BF)
                continue
            for j in range(PAIRS):
                t = y[:, lanes(j)]
                r["s_" + name][at, lanes(j)] = (t * cos[at, :] + swap_pairs(t) * sin[at, :]).astype(BF)


def attend_phase(r):
    n, total = r.attn.shape[0], r.s_k.shape[0]
    own = r.own[...]
    lane = lax.broadcasted_iota(jnp.int32, (n, LANES), 1)
    lse = jnp.zeros((n, LANES), F32)
    for p in range(PAIRS):
        q = two_heads(r.s_q[:n, lanes(p)] * jnp.asarray(SCALE, BF))

        def body(at, carry):
            top, tot, acc = carry
            same = own == r.all[:, at]
            s = dot_nt(q, r.s_k[at, lanes(p)])
            s = jnp.where(jnp.concatenate([same, same], axis=0), s, NEG_FILL)
            fresh = jnp.max(s, axis=1, keepdims=True)
            if at == slice(None):
                e = jnp.exp(s - fresh)
                return fresh, jnp.sum(e, axis=1, keepdims=True), dot(e.astype(BF), r.s_v[at, lanes(p)])
            fresh = jnp.maximum(top, fresh)
            e = jnp.exp(s - fresh)
            keep = jnp.exp(top - fresh)
            tot = tot * keep + jnp.sum(e, axis=1, keepdims=True)
            acc = acc * keep + dot(e.astype(BF), r.s_v[at, lanes(p)])
            return fresh, tot, acc

        zero = jnp.zeros((2 * n, 1), F32)
        top, tot, acc = over_chunks(total, body, (zero + NEG_FILL, zero, jnp.zeros((2 * n, LANES), F32)))
        r.attn[:, lanes(p)] = join_heads(acc / tot)
        part = top + jnp.log(tot)
        lse = jnp.where(lane == 2 * p, part[:n], jnp.where(lane == 2 * p + 1, part[n:], lse))
    r.lse[...] = lse


def ffn_phase(r, copies):
    stat_ref = r.stat
    lane = lax.broadcasted_iota(jnp.int32, stat_ref.shape, 1)
    copies.wait("wo")
    branch = dot(r.attn[...].astype(BF), r.m_wo[...]) + row_of(r, BO)
    n1, r1 = normalize(r.x[...].astype(F32) + branch)
    hidden = n1 * row_of(r, G1) + row_of(r, C1)
    r.n1[...] = n1
    hidden_b = hidden.astype(BF)
    r.s_hidden[...] = hidden_b
    total = hidden + row_of(r, BU)
    for j in range(FF // FB):
        copies.wait(f"wi{j}")
        inner = dot(hidden_b, r.m_wi[:, units(j)]) + r.bi[:, units(j)]
        half = 0.5 + 0.5 * lax.erf(inner * (0.5**0.5))
        active = (inner * half).astype(BF)
        r.slope[:, units(j)] = (half + inner * jnp.exp(-0.5 * inner * inner) * 0.3989422804014327).astype(BF)
        r.s_active[:, units(j)] = active
        copies.wait(f"wu{j}")
        total = total + dot(active, r.m_wu[units(j), :])
    n2, r2 = normalize(total)
    r.n2[...] = n2
    stat_ref[...] = jnp.where(lane == 0, r1, jnp.where(lane == 1, r2, 0.0))
    return n2 * row_of(r, G2) + row_of(r, C2)


def store_active(r, ref, at, x):
    for z in range(4):
        src = pl.ds(pl.multiple_of((2 * z + x) * ACTIVE, LANES), ACTIVE)
        ref[:, at + z * ACTIVE : at + (z + 1) * ACTIVE] = r.s_active[:, src]


def store_pack(r, ref, at, x):
    ref[:, at : at + D] = r.s_hidden[...]
    ref[:, at + D : at + 2 * D] = r.attn[...].astype(BF)
    store_active(r, ref, at + 2 * D, x)


def feed_back_phase(r, copies, grad):
    place = r.place
    y, c = place[1], place[2]
    n2 = r.n2[...]
    sums = r.sums
    sums[0:1, :] = column_sum(grad * n2)
    sums[1:2, :] = column_sum(grad)
    grad = norm_back(grad, n2, r.stat[:, 1:2], row_of(r, G2))
    outer = grad.astype(BF)
    sums[2:3, :] = column_sum(outer)
    mine, theirs, mine_y, theirs_y = quarters(outer, 0, c)
    mine, theirs = cat(mine, mine_y), cat(theirs, theirs_y)
    r.near[:, NEAR_OUTER:NEAR_OUT] = mine
    r.send[:, NEAR_OUTER:NEAR_OUT] = theirs
    r.to_x[:, : 2 * CHUNK] = mine
    r.to_x[:, 2 * CHUNK : D] = theirs
    for j in range(FF // FB):
        copies.wait(f"wu{j}")
        inner = (dot_nt(outer, r.m_wu[units(j), :]) * r.slope[:, units(j)].astype(F32)).astype(BF)
        sums[6 + j : 7 + j, :] = column_sum(inner)
        r.s_inner[:, units(j)] = inner
        copies.wait(f"wi{j}")
        grad = grad + dot_nt(inner, r.m_wi[:, units(j)])
    n1 = r.n1[...]
    sums[3:4, :] = column_sum(grad * n1)
    sums[4:5, :] = column_sum(grad)
    pre_one = norm_back(grad, n1, r.stat[:, 0:1], row_of(r, G1))
    r.pre[...] = pre_one
    branch = pre_one.astype(BF)
    sums[5:6, :] = column_sum(branch)
    sums[10:16, :] = jnp.zeros((6, D), F32)
    mine, theirs, mine_y, theirs_y = quarters(branch, y, c)
    r.near[:, NEAR_OUT:NEAR] = mine
    r.send[:, NEAR_OUT:NEAR] = theirs
    r.to_y[:, SIDE_OUT:SIDE] = cat(mine_y, theirs_y)
    copies.wait("wo")
    attn_grad = dot_nt(branch, r.m_wo[...]).astype(BF)
    r.pack[:, :D] = attn_grad
    feature = lax.broadcasted_iota(jnp.int32, (D, LANES), 0) // HEAD_DIM
    member = (feature == lax.broadcasted_iota(jnp.int32, (D, LANES), 1)).astype(BF)
    hi, lo = hi_lo(attn_grad.astype(F32) * r.attn[...])
    delta = dot(hi, member) + dot(lo, member)
    r.delta[...] = delta
    extra = jnp.zeros(delta.shape, F32)
    for v, at in ((r.lse[...], LSE), (delta, DELTA)):
        for i in range(3):
            piece = v.astype(BF).astype(F32)
            extra = extra + (pltpu.roll(piece, at + i * PIECE, 1) if at + i else piece)
            v = v - piece
    r.pack[:, D:] = extra.astype(BF)
    shard = 2 * y + c
    for ref, at, k in (
        (r.near, 0, shard), (r.send, 0, 2 * y + 1 - c), (r.to_y, 0, 2 - 2 * y + c), (r.to_y, FB, 3 - 2 * y - c),
    ):
        ref[:, at : at + FB] = r.s_inner[:, pl.ds(pl.multiple_of(k * FB, LANES), FB)]


def key_back_phase(r, copies):
    place = r.place
    n, total = r.k.shape[0], r.s_g.shape[0]
    row = lax.broadcasted_iota(jnp.int32, (32, LANES), 0)
    lane = lax.broadcasted_iota(jnp.int32, (32, LANES), 1)
    first = jnp.where(row < 16, LSE, DELTA - 16) + row
    pick = ((lane == first) | (lane == first + PIECE) | (lane == first + 2 * PIECE)).astype(BF)
    rows_ref, own = r.s_stats, r.own[...]

    def fill(at, carry):
        rows_ref[:, at] = dot_nt(pick, r.s_extra[at, :])
        return carry

    over_chunks(total, fill, 0)
    for p in range(PAIRS):
        copies.wait(f"q{p}")
        k = two_heads(r.k[:, lanes(p)] * jnp.asarray(SCALE, BF))
        v = two_heads(r.v[:, lanes(p)])

        def body(at, carry):
            dk, dv = carry
            same = own == r.all[:, at]
            q, g = r.s_q[at, lanes(p)], r.s_g[at, lanes(p)]
            s, dp = dot_nt(k, q), dot_nt(v, g)
            probs, ds = [], []
            for h in range(2):
                half = slice(h * n, (h + 1) * n)
                lse, delta = rows_ref[2 * p + h : 2 * p + h + 1, at], rows_ref[16 + 2 * p + h : 17 + 2 * p + h, at]
                prob = jnp.exp(jnp.where(same, s[half] - lse, NEG_FILL))
                probs.append(prob.astype(BF))
                ds.append((prob * (dp[half] - delta)).astype(BF))
            return dk + dot(jnp.concatenate(ds, axis=0), q), dv + dot(jnp.concatenate(probs, axis=0), g)

        zero = jnp.zeros((2 * n, LANES), F32)
        dk, dv = over_chunks(total, body, (zero, zero))
        r.s_dk[:, lanes(p)] = unrotate(join_heads(dk) * SCALE, r.cos[...], r.sin[...]).astype(BF)
        r.s_dv[:, lanes(p)] = join_heads(dv).astype(BF)
    dq, dk, dv = r.dq[...], r.s_dk[...], r.s_dv[...]
    for i, v in enumerate((dq, dk, dv)):
        r.qkv_sums[i : i + 1, :] = column_sum(v)
    r.qkv_sums[3:8, :] = jnp.zeros((5, D), F32)
    mine, theirs, mine_y, theirs_y = zip(*[quarters(v, place[1], place[2]) for v in (dq, dk, dv)])
    for ref, v, above in ((r.qkv_near, mine, "above_near"), (r.qkv_send, theirs, "above_send"), (r.qkv_side, mine_y + theirs_y, "above_side")):
        ref[...] = cat(*v, r[above][...]) if above in r else cat(*v)


def input_back_phase(r, copies):
    total = r.pre_above[...]
    for name, ref in (("wq", r.dq), ("wk", r.s_dk), ("wv", r.s_dv)):
        copies.wait(name)
        total = total + dot_nt(ref[...], r["m_" + name][...])
    return total


def layer_forward(layer, place, x, blocks, weights, bi, vec, cos, sin, own_seg, all_seg, qkv=None, cotangent=None, after=()):
    n = x.shape[0]
    total = all_seg.shape[1]
    last = cotangent is not None
    names = ("wo", "wi", "wu") if qkv else ("wk", "wv", "wq", "wo", "wi", "wu")
    ins = Names(place=place, x=x, own=own_seg, all=all_seg, bi=bi[layer], vec=vec[layer])
    ins.update({"w_" + name: weights[name] for name in names})
    hbm = {"w_" + name for name in names}
    outs = Names(attn=sds((n, D), F32), lse=sds((n, LANES), F32), result_b=sds((n, D), BF))
    scratch = Names(
        s_hidden=pltpu.VMEM((n, D), BF), s_active=pltpu.VMEM((n, FF), BF), **rooms(names),
    )
    inner = Names(
        n1=sds((n, D), F32), n2=sds((n, D), F32), stat=sds((n, LANES), F32), slope=sds((n, FF), BF),
    )
    flops = 2 * n * (D * D + 2 * D * FF) + 4 * n * total * D * 2
    if qkv:
        ins.update(zip(("s_q", "s_k", "s_v"), qkv))
    else:
        ins.update(blocks=blocks, cos=cos, sin=sin)
        for name in "qkv":
            outs[name] = sds((total, D), BF)
            hbm.add(name)
            if name != "q":
                outs["own_" + name] = sds((n, D), BF)
            scratch["s_" + name] = pltpu.VMEM((total, D), BF)
        scratch.s_rows = pltpu.VMEM((total, D), BF)
        scratch.out_sems = pltpu.SemaphoreType.DMA((3,))
        flops += 6 * total * D * D
    if last:
        scratch.update({k: pltpu.VMEM(v.shape, v.dtype) for k, v in inner.items()})
        scratch.s_inner = pltpu.VMEM((n, FF), BF)
        ins.cotangent = cotangent
        outs.update(feed_back_outs(n, True))
        flops += 2 * n * (D * D + 2 * D * FF)
    else:
        outs.update(inner)
        outs.result = sds((n, D), F32)
        outs.update(keep_pack=sds((n, PACK), BF), side=sds((n, 2 * D), BF), active=sds((n, FF // 2), BF))

    def kernel(r):
        copies = Copies(r.sems)
        copies.weights(r, layer, names)
        if not qkv:
            join(r.s_rows, r.blocks, slice(0, D))
            qkv_phase(r, copies)
            back = Copies(r.out_sems)
            for name in "qkv":
                back.start(name, r["s_" + name], r[name])
            for name in "kv":
                r["own_" + name][...] = r["s_" + name][:n, :]
        attend_phase(r)
        result = ffn_phase(r, copies)
        r.result_b[...] = result.astype(BF)
        x = r.place[0]
        if last:
            feed_back_phase(r, copies, r.cotangent[...].astype(F32))
            for ref, at in ((r.near, NEAR_PACK), (r.send, NEAR_PACK)):
                ref[:, NEAR:NEAR_PACK] = jnp.zeros((n, NEAR_PACK - NEAR), BF)
                store_pack(r, ref, at, x)
            r.to_y[:, SIDE : SIDE + D] = r.s_hidden[...]
            r.to_y[:, SIDE + D :] = r.attn[...].astype(BF)
            store_active(r, r.to_x, D, 1 - x)
        else:
            r.result[...] = result
            store_pack(r, r.keep_pack, 0, x)
            r.side[:, :D] = r.s_hidden[...]
            r.side[:, D:] = r.attn[...].astype(BF)
            store_active(r, r.active, 0, 1 - x)
        if not qkv:
            back.wait(*"qkv")

    return mega(kernel, "forward_last" if last else "forward", ins, outs, scratch, flops, hbm=hbm, after=after)


def feed_back_outs(n, last):
    return Names(
        near=sds((n, NEAR_PACK + PACK if last else NEAR), BF), send=sds((n, NEAR_PACK + PACK), BF),
        to_x=sds((n, D + FF // 2 if last else D), BF), to_y=sds((n, SIDE + 2 * D if last else SIDE), BF),
        pre=sds((n, D), F32), pack=sds((n, D + LANES), BF), delta=sds((n, LANES), F32),
        sums=sds((16, D), F32),
    )


def layer_back(layer, place, kept, back, dq, blocks, weights, vec, cos, sin, own_seg, all_seg, below=None, far=(), after=()):
    n, total = dq.shape[0], all_seg.shape[1]
    names = ("wq", "wk", "wv") + (("wo", "wi", "wu") if below else ())
    ins = Names(
        place=place, k=kept.own_k, v=kept.own_v, q=kept.q, dq=dq, pre_above=back.pre, blocks=blocks,
        own=own_seg, all=all_seg, cos=cos, sin=sin,
    )
    ins.update({"w_" + name: weights[name] for name in names})
    hbm = {"w_" + name for name in names} | {"q"}
    single = len(blocks) == 1
    if single:
        hbm.add("blocks")
    wide = 1 if below else 2
    outs = Names(
        qkv_near=sds((n, wide * QKV), BF), qkv_send=sds((n, wide * QKV), BF), qkv_side=sds((n, wide * 2 * QKV), BF), qkv_sums=sds((8, D), F32),
    )
    if single:
        outs.update(dk=sds((n, D), BF), dv=sds((n, D), BF))
    scratch = Names(
        s_q=pltpu.VMEM((total, D), BF), s_g=pltpu.VMEM((total, D), BF), s_extra=pltpu.VMEM((total, LANES), BF),
        s_stats=pltpu.VMEM((32, total), F32), s_dk=pltpu.VMEM((n, D), BF), s_dv=pltpu.VMEM((n, D), BF),
        q_sems=pltpu.SemaphoreType.DMA((PAIRS + 2,)), **rooms(names),
    )
    if below:
        ins.update({k: below[k] for k in ("n1", "n2", "stat", "slope", "attn", "lse")}, vec=vec[layer - 1])
        outs.update(feed_back_outs(n, False))
        ins.far = list(far)
        scratch.s_inner = pltpu.VMEM((n, FF), BF)
    else:
        outs.grad = sds((n, D), BF)
        ins.update(above_near=back.qkv_near, above_send=back.qkv_send, above_side=back.qkv_side)

    def kernel(r):
        queries = Copies(r.q_sems)
        if single:
            queries.start("g", r.blocks[0].at[:, :D], r.s_g)
            queries.start("extra", r.blocks[0].at[:, D:], r.s_extra)
        for p in range(PAIRS):
            queries.start(f"q{p}", r.q.at[:, lanes(p)], r.s_q.at[:, lanes(p)])
        copies = Copies(r.sems)
        copies.weights(r, layer, names[:3])
        if below:
            copies.weights(r, layer - 1, names[3:])
        if single:
            queries.wait("g", "extra")
        else:
            join(r.s_g, r.blocks, slice(0, D))
            join(r.s_extra, r.blocks, slice(D, D + LANES))
        key_back_phase(r, queries)
        if single:
            r.dk[...] = r.s_dk[...]
            r.dv[...] = r.s_dv[...]
        grad = input_back_phase(r, copies)
        if below:
            feed_back_phase(r, copies, grad)
            r.send[:, NEAR:NEAR_PACK] = jnp.zeros((n, NEAR_PACK - NEAR), BF)
            for i, ref in enumerate(r.far):
                at = NEAR_PACK + i * 2 * D
                r.send[:, at : at + 2 * D] = ref[...]
        else:
            r.grad[...] = grad.astype(BF)

    flops = 8 * n * total * D * 2 + 6 * n * D * D + (2 * n * (D * D + 2 * D * FF) if below else 0)
    return mega(kernel, "layer_back" if below else "layer_back_first", ins, outs, scratch, flops, hbm=hbm, after=after)


def feed_pieces(place, packs, near, side, cross, after=(), vmem=32):
    n = near[0].shape[0]
    here, there = packs
    ins = Names(
        place=place, here=[a for a, _ in here], att=[a for a, _, _, _ in there], act=[a for _, _, a, _ in there],
        near=list(near), side=list(side), cross=list(cross),
    )
    io, u = sds((4, WIDTH, IO), BF), sds((4, WIDTH, 2 * ACTIVE), BF)
    scratch = Names(
        t_hidden=pltpu.VMEM((D, 4 * n), BF), t_attn=pltpu.VMEM((D, 4 * n), BF), t_outer=pltpu.VMEM((2, CHUNK, 4 * n), BF),
    )

    def kernel(r):
        hidden = [(ref, at) for ref, (_, at) in zip(r.here, here)] + [(ref, at) for ref, (_, at, _, _) in zip(r.att, there)]
        turned(r.t_hidden, *[ref[:, at : at + D] for ref, at in hidden])
        turned(r.t_attn, *[ref[:, at + D : at + 2 * D] for ref, at in hidden])
        n0, n1 = r.near
        y0, y1 = r.side
        x0, x1 = r.cross
        inner = jnp.concatenate([n0[:, :FB], n1[:, :FB], y0[:, :FB], y1[:, FB : 2 * FB]], axis=0)
        out = jnp.concatenate(
            [n0[:, NEAR_OUT:NEAR], n1[:, NEAR_OUT:NEAR], y0[:, SIDE_OUT : SIDE_OUT + CHUNK], y1[:, SIDE_OUT + CHUNK : SIDE]], axis=0
        )
        x, y = r.place[0], r.place[1]
        for name, side_x in (("io_send", 1 - x), ("io_keep", x)):
            r[name][:, :, :FB] = dot(shard_rows(r.t_hidden, side_x), inner).astype(BF).reshape(4, WIDTH, FB)
            r[name][:, :, FB:] = dot(shard_rows(r.t_attn, side_x), out).astype(BF).reshape(4, WIDTH, CHUNK)
        sources = [(n0, NEAR_OUTER), (n1, NEAR_OUTER), (x0, 0), (x1, 2 * CHUNK)]
        for h in range(2):
            turned(r.t_outer.at[h], *[ref[:, at + h * CHUNK : at + (h + 1) * CHUNK] for ref, at in sources])
        active = [ref[:, at + 2 * D : at + PACK] for ref, (_, at) in zip(r.here, here)]
        active += [ref[:, at : at + FF // 2] for ref, (_, _, _, at) in zip(r.act, there)]
        active = jnp.concatenate(active, axis=0)
        for name, side_y in (("u_send", 1 - y), ("u_keep", y)):
            t = dot(r.t_outer[side_y], active).astype(BF)
            for z in range(4):
                part = t[:, z * ACTIVE : (z + 1) * ACTIVE]
                r[name][z, :, :ACTIVE] = part[:WIDTH]
                r[name][z, :, ACTIVE:] = part[WIDTH:]

    outs = Names(io_keep=io, io_send=io, u_keep=u, u_send=u)
    return mega(kernel, "feed_pieces", ins, outs, scratch, 8 * n * (D * IO + FF * CHUNK), after=after, vmem=vmem)


def qkv_pieces(place, blocks, near, side, after=()):
    n = near[0].shape[0]
    ins = Names(place=place, blocks=[b[k] for b in blocks for k in (0, 4, 2, 6)], near=list(near), side=list(side))
    o = sds((4, WIDTH, padded(QKV) + QKV), BF)

    def kernel(r):
        (g0, g1), (y0, y1) = r.near, r.side
        x = r.place[0]
        for layer in range(LAYERS):
            turned(r.t_rows.at[layer], *[ref[...] for ref in r.blocks[4 * layer : 4 * layer + 4]])
            parts = (g0, layer * QKV), (g1, layer * QKV), (y0, 2 * layer * QKV), (y1, (2 * layer + 1) * QKV)
            g = jnp.concatenate([ref[:, at : at + QKV] for ref, at in parts], axis=0)
            at = layer * padded(QKV)
            for name, side_x in (("send", 1 - x), ("keep", x)):
                found = dot(shard_rows(r.t_rows.at[layer], side_x), g).astype(BF)
                r[name][:, :, at : at + QKV] = found.reshape(4, WIDTH, QKV)

    scratch = Names(t_rows=pltpu.VMEM((LAYERS, D, 4 * n), BF))
    return mega(kernel, "qkv_pieces", ins, Names(keep=o, send=o), scratch, 16 * n * D * QKV, after=after, vmem=24)


def padded(w):
    return -(-w // LANES) * LANES


def first_sum(place, pairs, after=(), vmem=24):
    width = sum(padded(a.shape[2]) for a, _ in pairs)
    o = sds((2, WIDTH, width), BF)

    def kernel(r):
        bit = r.place[3] % 2
        for name, side in (("keep", bit), ("send", 1 - bit)):
            for i in range(2):
                at = 0
                for a, b in zip(r.own, r.got):
                    w = a.shape[2]
                    r[name][i, :, at : at + w] = (a[2 * i + side].astype(F32) + b[2 * i + side].astype(F32)).astype(BF)
                    at += padded(w)

    ins = Names(place=place, own=[a for a, _ in pairs], got=[b for _, b in pairs])
    return mega(kernel, "first_sum", ins, Names(keep=o, send=o), {}, 1000, after=after, vmem=vmem)


def second_sum(place, keep, got, after=()):
    o = sds(keep.shape[1:], BF)

    def kernel(r):
        bit = r.place[3] // 2
        for name, side in (("keep", bit), ("send", 1 - bit)):
            r[name][...] = (r.own[side].astype(F32) + r.got[side].astype(F32)).astype(BF)

    return mega(kernel, "second_sum", Names(place=place, own=keep, got=got), Names(keep=o, send=o), {}, 1000, after=after, vmem=24)


FEED_SHAPES = Names(inner=(WIDTH, FB), out=(WIDTH, CHUNK), outer=(CHUNK, ACTIVE))
QKV_SHAPES = Names(query=(WIDTH, CHUNK), key=(WIDTH, CHUNK), value=(WIDTH, CHUNK))


def last_feed(layers):
    outs = Names((k, sds((LAYERS,) + v, F32)) for k, v in FEED_SHAPES.items())

    def kernel(r):
        for layer, (a, b) in enumerate(zip(r.own, r.got)):
            total = a[...].astype(F32) + b[...].astype(F32)
            r.inner[layer] = total[:, :FB]
            r.out[layer] = total[:, FB:IO]
            r.outer[layer, :WIDTH] = total[:, IO_PAD : IO_PAD + ACTIVE]
            r.outer[layer, WIDTH:] = total[:, IO_PAD + ACTIVE :]

    return mega(kernel, "last_feed", Names(own=[a for a, _ in layers], got=[b for _, b in layers]), outs, {}, 1000, vmem=24)


def last_qkv(keep, got):
    outs = Names((k, sds((LAYERS,) + v, F32)) for k, v in QKV_SHAPES.items())

    def kernel(r):
        total = r.own[...].astype(F32) + r.got[...].astype(F32)
        for layer in range(LAYERS):
            for i, name in enumerate(QKV_SHAPES):
                at = layer * padded(QKV) + i * CHUNK
                r[name][layer] = total[:, at : at + CHUNK]

    return mega(kernel, "last_qkv", Names(own=keep, got=got), outs, {}, 1000, vmem=24)


def linear(z, x, y, c):
    return (z * 2 + x) * 4 + y * 2 + c


PLACES = [(z, x, y, c) for z in range(4) for x in range(2) for y in range(2) for c in range(2)]


def move(array, where):
    pairs = [(linear(*place), linear(*where(*place))) for place in PLACES]
    return lax.ppermute(array, BOTH, pairs)


def to_plane(z, x, y, c):
    return (2 * y + c, x, z >> 1, z & 1)


def other_core(z, x, y, c):
    return (z, x, y, 1 - c)


def other_x(z, x, y, c):
    return (z, 1 - x, y, c)


def other_y(z, x, y, c):
    return (z, x, 1 - y, c)


def other_xy(z, x, y, c):
    return (z, 1 - x, 1 - y, c)


def near_z(z, x, y, c):
    return (z ^ 1, x, y, c)


def far_z(z, x, y, c):
    return (z ^ 2, x, y, c)


def gate(arrays, *others):
    return lax.optimization_barrier((arrays, others))[0]


def pick(array, index, axis):
    return lax.dynamic_index_in_dim(array, index, axis, keepdims=False)


class Small:
    def __init__(self):
        seq, rows = lax.axis_index("seq"), lax.axis_index("rows")
        self.z, self.x, self.y, self.c = seq // 2, seq % 2, rows // 2, rows % 2
        self.spot = jnp.stack([self.x, self.y, self.c, self.z]).astype(jnp.int32)

    def share_few(self, mine):
        far = jnp.concatenate(mine[1:], axis=0)
        return [mine[0], far, move(mine[0], other_core), move(far, other_core)]

    def starts(self, count):
        out = []
        for dc in (0, 1):
            for dx, dy in ((0, 0), (1, 0), (0, 1), (1, 1)):
                x, y, c = self.x ^ dx, self.y ^ dy, self.c ^ dc
                out.append(((2 * y + c) * 2 + x) * count)
        return jnp.stack(out)

    def reach(self, array):
        return [array, move(array, other_x), move(array, other_y), move(array, other_xy)]

    def share(self, mine):
        return mine + [move(a, other_core) for a in mine]


class Large:
    def __init__(self):
        self.shards = lax.axis_size("seq")
        self.spot = jnp.zeros((4,), jnp.int32)

    def starts(self, count):
        me = lax.axis_index("seq")
        return (me + jnp.arange(self.shards, dtype=jnp.int32)) % self.shards * count

    def gather(self, array):
        whole_row = lax.all_gather(array, "seq", axis=0, tiled=True)
        return [jnp.roll(whole_row, -lax.axis_index("seq") * array.shape[0], axis=0)]

    def spread(self, left, right):
        grad = lax.dot_general(left, right, (((0,), (0,)), ((), ())), preferred_element_type=F32).astype(BF)
        grad = lax.psum_scatter(grad, "seq", scatter_dimension=0, tiled=True)
        return lax.psum_scatter(grad, "rows", scatter_dimension=1, tiled=True).astype(F32)

    def grads(self, kept, back, tail, dq):
        near, send, to_x, to_y = back.near, back.send, back.to_x, back.to_y
        inner = cat(near[:, :FB], send[:, :FB], to_y[:, : 2 * FB])
        out = cat(near[:, NEAR_OUT:NEAR], send[:, NEAR_OUT:NEAR], to_y[:, SIDE_OUT:SIDE])
        outer = cat(*[to_x[:, i * CHUNK : (i + 1) * CHUNK] for i in (0, 2, 1, 3)])
        if "active" in kept:
            hidden, attn = kept.side[:, :D], kept.side[:, D:]
            mine, other = kept.keep_pack[:, 2 * D :], kept.active
        else:
            hidden, attn = to_y[:, SIDE : SIDE + D], to_y[:, SIDE + D :]
            mine, other = near[:, NEAR_PACK + 2 * D :], to_x[:, D:]
        active = jnp.stack([v.reshape(-1, 4, ACTIVE) for v in (mine, other)], axis=2).reshape(-1, FF)
        own = kept.blocks[0][: dq.shape[0]]
        return Names(
            inner=self.spread(hidden, inner), out=self.spread(attn, out), outer=self.spread(active, outer),
            query=self.spread(own, dq), key=self.spread(own, tail.dk), value=self.spread(own, tail.dv),
        )


def doc_layout(lengths_row, index):
    ends = jnp.cumsum(lengths_row, dtype=jnp.int32)
    passed = (index[:, None] >= ends[None, :]).astype(jnp.int32)
    segment = jnp.sum(passed, axis=1, dtype=jnp.int32)
    begin = jnp.sum(passed * lengths_row[None, :], axis=1, dtype=jnp.int32)
    return (segment, (index - begin).astype(jnp.int32))


def rotary_tables(position):
    lane = jnp.arange(LANES, dtype=jnp.int32)
    pairs = (lane % HEAD_DIM // 2).astype(F32)
    inverse = jnp.power(jnp.float32(10000.0), -2.0 * pairs / HEAD_DIM)
    angle = position.astype(F32)[:, None] * inverse[None, :]
    return jnp.cos(angle), jnp.sin(angle) * jnp.where(lane % 2 == 0, -1.0, 1.0)[None, :]


def both_cores(array):
    return array, move(array, other_core)


def all_sums(two, tail_two, one, tail_one):
    return jnp.concatenate([one.sums[:10], tail_one.qkv_sums[:3], two.sums[:10], tail_two.qkv_sums[:3]], axis=0)


VECTOR_ROWS = Names(g2=0, c2=1, bu=2, g1=3, c1=4, bo=5, bq=10, bk=11, bv=12)
LAYER_ROWS = 13


def last_vectors(place, own, got, whole):
    outs = Names((name, sds((LAYERS, WIDTH), F32)) for name in VECTOR_ROWS)
    outs.bi = sds((LAYERS, ACTIVE), F32)
    outs.passed = [sds(a.shape, a.dtype) for a in whole]

    def kernel(r):
        for a, b in zip(r.whole, r.passed):
            b[...] = a[...]
        x, z = r.place[0], r.place[3]
        total = r.own[...] + r.got[...]
        r.s_total[...] = total
        shard = 2 * z + x
        turn = pltpu.roll(total, (D - shard * WIDTH) % D, 1)[:, :WIDTH]
        for layer in range(LAYERS):
            for name, row in VECTOR_ROWS.items():
                at = LAYER_ROWS * layer + row
                r[name][layer : layer + 1, :] = turn[at : at + 1]
            row = r.s_total[pl.ds(LAYER_ROWS * layer + 6 + z, 1), :]
            r.bi[layer : layer + 1, :] = jnp.where(x == 0, row[:, :ACTIVE], row[:, ACTIVE:])

    scratch = Names(s_total=pltpu.VMEM(own.shape, F32))
    return mega(kernel, "last_vectors", Names(place=place, own=own, got=got, whole=list(whole)), outs, scratch, 1000, vmem=24)


class Program:
    def __init__(self, place, spot, lengths_row, n, starts, params):
        wq, bq, wk, bk, wv, bv, wo, bo, g1, c1, wi, bi, wu, bu, g2, c2 = params
        self.weights = Names(wq=wq, wk=wk, wv=wv, wo=wo, wi=wi, wu=wu)
        self.spot, self.n = spot, n
        self.vec = jnp.stack([bq, bk, bv, bo, g1, c1, bu, g2, c2], axis=1).astype(F32)
        self.bi = bi.astype(F32)[:, None, :]
        index = (starts[:, None] + jnp.arange(n, dtype=jnp.int32)).reshape(-1)
        segment, position = doc_layout(lengths_row, index)
        self.segments = segment[:n, None], segment[None, :]
        self.cos, self.sin = rotary_tables(position)
        self.own_cos, self.own_sin = rotary_tables(position[:n])

    def project(self, layer, rows):
        w = self.weights
        return project(rows, layer, w["wq"], w["wk"], w["wv"], self.vec, self.cos, self.sin)

    def forward(self, layer, x, blocks, qkv=None, cotangent=None, after=()):
        kept = layer_forward(
            layer, self.spot, x, blocks, self.weights, self.bi, self.vec, self.cos, self.sin, *self.segments, qkv, cotangent, after
        )
        kept.blocks = blocks
        if qkv:
            kept.update(zip("qkv", qkv), own_k=qkv[1][: self.n], own_v=qkv[2][: self.n])
        return kept

    def queries(self, kept, back, after=()):
        return query_back(
            kept.q, kept.k, kept.v, back.pack, kept.lse, back.delta, *self.segments, self.own_cos, self.own_sin, after
        )[0]

    def back(self, layer, kept, back, dq, packs, below=None, far=(), after=()):
        return layer_back(
            layer, self.spot, kept, back, dq, packs, self.weights, self.vec, self.own_cos, self.own_sin, *self.segments, below, far, after
        )


def large_body(tokens, lengths, cotangent, *params):
    place = Large()
    n = tokens.shape[1]
    run = Program(place, place.spot, lengths[0], n, place.starts(n), params)

    def step(layer, x, x_b, cotangent=None):
        blocks = place.gather(x_b)
        return run.forward(layer, x, blocks, run.project(layer, blocks[0]), cotangent)

    first = step(0, tokens[0], tokens[0])
    second = step(1, first.result, first.result_b, cotangent[0])
    dq_two = run.queries(second, second)
    back_one = run.back(1, second, second, dq_two, place.gather(second.pack), first)
    dq_one = run.queries(first, back_one)
    back_none = run.back(0, first, back_one, dq_one, place.gather(back_one.pack))
    grads_one = place.grads(first, back_one, back_none, dq_one)
    grads_two = place.grads(second, second, back_one, dq_two)
    m = Names((name, jnp.stack([grads_one[name], grads_two[name]])) for name in grads_one)
    total = lax.psum(all_sums(second, back_one, back_one, back_none), BOTH).reshape(LAYERS, LAYER_ROWS, D)
    me, shards = lax.axis_index("seq"), lax.axis_size("seq")
    v = Names(
        (name, lax.dynamic_slice_in_dim(total[:, row], me * (D // shards), D // shards, 1))
        for name, row in VECTOR_ROWS.items()
    )
    v.bi = lax.dynamic_slice_in_dim(total[:, 6:10].reshape(LAYERS, FF), me * (FF // shards), FF // shards, 1)
    return result(second.result_b, back_none.grad, m, v)


def small_body(tokens, lengths, cotangent, *params):
    place = Small()
    spot, n = place.spot, tokens.shape[1]
    current = move(tokens[0], to_plane)
    run = Program(place, spot, move(lengths, to_plane)[0], n, place.starts(n), params)
    blocks = place.share(gate(place.reach(current), run.cos, run.sin, run.own_cos, run.own_sin, run.vec, run.bi))
    grad = move(gate(cotangent[0], current), to_plane)
    first = run.forward(0, current, blocks, after=(grad,))
    a_near = both_cores(first.keep_pack)
    blocks = place.share(place.reach(first.result_b))
    side, active = gate((first.side, first.active), blocks)
    a_side, a_cross = move(side, other_y), move(active, other_x)
    second = run.forward(1, first.result, blocks, cotangent=grad, after=(a_near[1],))

    reached = place.reach(second.pack)
    dq_two = run.queries(second, second, after=(a_side, a_cross))
    packs = place.share(gate(reached, dq_two))
    to_y, to_x, send, result_b = gate((second.to_y, second.to_x, second.send, second.result_b), packs)
    from_y, from_x, near = move(to_y, other_y), move(to_x, other_x), (second.near, move(send, other_core))
    output = move(result_b, to_plane)
    back_one = run.back(1, second, second, dq_two, packs, first, (a_side, a_cross))

    pack, from_y, from_x, near_got = gate((back_one.pack, from_y, from_x, near[1]), output)
    near = near[0], near_got
    reached = place.reach(pack)
    side, cross = [both_cores(a) for a in gate((from_y, from_x), pack)]
    dq_one = run.queries(first, back_one)
    packs = place.share_few(gate(reached, dq_one))
    to_y, to_x = gate((back_one.to_y, back_one.to_x), reached, dq_one)
    one_y, one_x = move(to_y, other_y), move(to_x, other_x)
    there = [(a, SIDE, b, D) for a, b in zip(side, cross)]
    two = feed_pieces(spot, ([(a, NEAR_PACK) for a in near], there), near, side, cross, after=(dq_one, *reached), vmem=60)
    two_io, two_u = move(two.io_send, other_x), move(two.u_send, other_y)
    near = back_one.near, move(gate(back_one.send, reached, dq_one), other_core)
    back_none = run.back(0, first, back_one, dq_one, packs, after=(two.io_send, near[1], one_x))

    two_sum = first_sum(spot, ((two.io_keep, two_io), (two.u_keep, two_u)), vmem=60, after=(back_none.grad, one_y, near[1]))
    side, cross = [both_cores(a) for a in gate((one_y, one_x), back_none.grad)]
    q_side = move(back_none.qkv_side, other_y)
    tokens_grad = move(back_none.grad, to_plane)
    sums = all_sums(second, back_one, back_one, back_none)
    from_sums = move(sums, other_core)
    two_near = move(two_sum.send, near_z)
    there = [(a_side, 0, a_cross, 0), (near[1], NEAR_PACK, near[1], NEAR_PACK + 2 * D)]
    one = feed_pieces(spot, ([(a, 0) for a in a_near], there), near, side, cross, after=(two_sum.send, tokens_grad))
    one_io, one_u = move(one.io_send, other_x), move(one.u_send, other_y)
    sums = gate(sums + from_sums, two_sum.send)
    from_sums = move(sums, near_z)
    qkv_send, q_side = gate((back_none.qkv_send, q_side), one.io_send)
    q_near, q_side = (back_none.qkv_near, move(qkv_send, other_core)), both_cores(q_side)
    qkv = qkv_pieces(spot, (first.blocks, second.blocks), q_near, q_side, after=(one.io_send, from_sums))
    q_x = move(qkv.send, other_x)
    two_z = second_sum(spot, two_sum.keep, two_near, after=(qkv.send, one_io))
    two_far = move(two_z.send, far_z)
    sums = gate(sums + from_sums, qkv.send)
    from_sums = move(sums, far_z)
    one_sum = first_sum(spot, ((one.io_keep, one_io), (one.u_keep, one_u)), after=(two_z.send, from_sums))
    one_near = move(one_sum.send, near_z)
    sums = gate(sums + from_sums, one_sum.send)
    from_sums = move(sums, other_x)
    q_sum = first_sum(spot, ((qkv.keep, q_x),), after=(one_sum.send, two_far))
    q_near = move(q_sum.send, near_z)
    sums = gate(sums + from_sums, q_sum.send)
    from_sums = move(sums, other_y)
    one_z = second_sum(spot, one_sum.keep, one_near, after=(q_sum.send,))
    one_far = move(one_z.send, far_z)
    q_z = second_sum(spot, q_sum.keep, q_near, after=(one_z.send,))
    q_far = move(q_z.send, far_z)
    v = last_vectors(spot, sums, from_sums, (output, tokens_grad))
    m = last_feed(((one_z.keep, one_far), (two_z.keep, two_far)))
    m.outer = m.outer.swapaxes(1, 2)
    m.update(last_qkv(q_z.keep, q_far))
    return result(*v.passed, m, v)


def result(output, tokens_grad, m, v):
    return (
        output[None], tokens_grad[None],
        m.query, v.bq, m.key, v.bk, m.value, v.bv, m.out, v.bo, v.g1, v.c1,
        m.inner, v.bi, m.outer, v.bu, v.g2, v.c2,
    )


def solution(mesh):
    token = P("rows", "seq", None)
    mat, vec = P(None, "seq", "rows"), P(None, "seq")
    small = (mesh.shape["seq"], mesh.shape["rows"]) == (8, 4)
    return jax.shard_map(
        small_body if small else large_body,
        mesh=mesh,
        in_specs=(token, P("rows", None), token) + (P(),) * 16,
        out_specs=(token, token, mat, vec, mat, vec, mat, vec, mat, vec, vec, vec, mat, vec, mat, vec, vec, vec),
        check_vma=False,
    )
```
